32 devices in a mesh: unit: 8 (over z, y), dp: 4 (over x, core).
Axes of the slice: x: 2, y: 2, z: 4, core: 2. Of those that a mesh axis runs over, the one named last changes fastest.
Arguments:
- token_ids: int32 [4, 8, 512], P('dp'), may hold values from 0 to 30719
- segments: int32 [4, 8, 512], P('dp', 'unit'), may hold values from 0 to 7, never falling along the last dimension, each value on 1 to 256 neighbouring positions
- positions: int32 [4, 8, 64], P('dp', 'unit'), may hold values from 0 to 511
- teacher: bfloat16 [4, 8, 64, 30720], P('dp', None, None, 'unit'), may hold values from -18 to 18, as said below
- gate_noise: float32 [782], replicated, may hold values from 0.01 to 0.99
- unit_noise: float32 [3072], replicated, may hold values from 0.01 to 0.99
- multipliers: float32 [2], replicated, may hold values from 2 to 40
- step_count: int32 [1], replicated, may hold values from 1 to 20
- layer_mats: float32 [768, 4352], P(('unit', 'dp')), as said below
- mats_first: float32 [768, 4352], P(('unit', 'dp')), may hold values from -9.536743e-07 to 9.536743e-07
- mats_second: float32 [768, 4352], P(('unit', 'dp')), may hold values from 3.1512686e-13 to 1.2605074e-12
- layer_vecs: float32 [14, 768], P(None, ('unit', 'dp')), as said below
- vecs_first: float32 [14, 768], P(None, ('unit', 'dp')), may hold values from -9.536743e-07 to 9.536743e-07
- vecs_second: float32 [14, 768], P(None, ('unit', 'dp')), may hold values from 3.1512686e-13 to 1.2605074e-12
- ffn_mats: float32 [2, 768, 3072], P(None, 'dp', 'unit'), as said below
- ffn_first: float32 [2, 768, 3072], P(None, 'dp', 'unit'), may hold values from -9.536743e-07 to 9.536743e-07
- ffn_second: float32 [2, 768, 3072], P(None, 'dp', 'unit'), may hold values from 3.1512686e-13 to 1.2605074e-12
- unit_vecs: float32 [2, 3072], P(None, ('unit', 'dp')), as said below
- unit_first: float32 [2, 3072], P(None, ('unit', 'dp')), may hold values from -9.536743e-07 to 9.536743e-07
- unit_second: float32 [2, 3072], P(None, ('unit', 'dp')), may hold values from 3.1512686e-13 to 1.2605074e-12
- word_table: float32 [30720, 768], P('unit', 'dp'), may hold values from -0.6 to 0.6, as said below
- table_first: float32 [30720, 768], P('unit', 'dp'), may hold values from -9.536743e-07 to 9.536743e-07
- table_second: float32 [30720, 768], P('unit', 'dp'), may hold values from 3.1512686e-13 to 1.2605074e-12
- word_bias: float32 [30720], P(('unit', 'dp')), may hold values from -3 to 3
- bias_first: float32 [30720], P(('unit', 'dp')), may hold values from -9.536743e-07 to 9.536743e-07
- bias_second: float32 [30720], P(('unit', 'dp')), may hold values from 3.1512686e-13 to 1.2605074e-12
- mask_logits: float32 [14], replicated, may hold values from 3 to 6
- mask_first: float32 [14], replicated, may hold values from -9.536743e-07 to 9.536743e-07
- mask_second: float32 [14], replicated, may hold values from 3.1512686e-13 to 1.2605074e-12
Outputs:
- loss: float32 [], replicated
- kept: float32 [], replicated
- grad_norm: float32 [], replicated
- mats_new: float32 [768, 4352], P(('unit', 'dp'))
- mats_grad: float32 [768, 4352], P(('unit', 'dp'))
- vecs_new: float32 [14, 768], P(None, ('unit', 'dp'))
- vecs_grad: float32 [14, 768], P(None, ('unit', 'dp'))
- ffn_new: float32 [2, 768, 3072], P(None, 'dp', 'unit')
- ffn_grad: float32 [2, 768, 3072], P(None, 'dp', 'unit')
- unit_new: float32 [2, 3072], P(None, ('unit', 'dp'))
- unit_grad: float32 [2, 3072], P(None, ('unit', 'dp'))
- table_new: float32 [30720, 768], P('unit', 'dp')
- table_grad: float32 [30720, 768], P('unit', 'dp')
- bias_new: float32 [30720], P(('unit', 'dp'))
- bias_grad: float32 [30720], P(('unit', 'dp'))
- mask_new: float32 [14], replicated
- mask_grad: float32 [14], replicated
The draws below stay inside these ranges and needn't reach their ends.
Inputs may be any that keep to these rules, and one draw needn't show every extreme that they name: `token_ids`: token ids index the vocabulary. `segments`: segment numbers never fall along a row. Masked positions index tokens of their row; they may repeat. layer_mats entries are independent normal draws. layer_vecs: gains near one, biases of either sign, hidden logits. ffn_mats entries are independent normal draws. unit_vecs: biases of either sign and unit logits. teacher logits are independent draws. word_table entries are independent draws.
All inputs are finite; a program needn't handle non-finite values.
Results may differ from the reference program's by a relative error of at most 0.012.
The reference program's roundings to bfloat16 on the way count: a program that leaves them out, or rounds other values in their place, can miss the bound.
Values may be sent and summed in bfloat16 or wider, within the bound.
A program may use at most 320 MiB of HBM per device.

```python
import math
import jax
import jax.numpy as jnp
import numpy as np
from jax import lax

D = 768
H = 12
DH = 64
FF = 3072
SEQ = 512
VOCAB = 30720
NMASK = 64
ROWS_G = 8
NPOS = 2048
NPARAM = 31701518
N_DP = 4


def draw_layer_mats(key, part):
    columns = jnp.arange(5 * D + SEQ)
    scale = jnp.where(columns < 3 * D, 1.2, jnp.where(columns < 4 * D, 4.0, 1.0)) * D ** (-0.5)
    scale = jnp.where(columns >= 5 * D, 0.1, scale)
    return jax.random.normal(key, (D, 5 * D + SEQ), jnp.float32) * scale[None, :]


def draw_layer_vecs(key, part):
    key_gain, key_shift, key_logit = jax.random.split(key, 3)
    gains = jax.random.uniform(key_gain, (14, D), jnp.float32, 0.7, 1.3)
    shifts = 0.3 * jax.random.normal(key_shift, (14, D), jnp.float32)
    logits = jax.random.uniform(key_logit, (14, D), jnp.float32, 0.5, 4.0)
    which = jnp.arange(14)[:, None]
    is_gain = (which == 0) | (which == 5) | (which == 8) | (which == 11)
    return jnp.where(which == 13, logits, jnp.where(is_gain, gains, shifts))


def draw_ffn_mats(key, part):
    draws = jax.random.normal(key, (2, D, FF), jnp.float32)
    scale = jnp.array([D ** (-0.5), 3.0 * FF ** (-0.5)], jnp.float32)
    return draws * scale[:, None, None]


def draw_unit_vecs(key, part):
    key_shift, key_logit = jax.random.split(key)
    shifts = 0.3 * jax.random.normal(key_shift, (FF,), jnp.float32)
    logits = jax.random.uniform(key_logit, (FF,), jnp.float32, 0.5, 4.0)
    return jnp.stack([shifts, logits])


def draw_word_table(key, part):
    draws = jax.random.normal(key, (VOCAB, D), jnp.float32)
    return jnp.clip(0.1 * draws, -0.6, 0.6)


def draw_teacher(key, part):
    draws = jax.random.normal(key, (N_DP, ROWS_G, NMASK, VOCAB), jnp.float32)
    return jnp.clip(3.0 * draws, -18.0, 18.0).astype(jnp.bfloat16)


def touch_ends(values, own_key, low, high):
    shape = values.shape
    index_at = [jax.random.randint(jax.random.fold_in(own_key, axis), (), 0, shape[axis]) for axis in range(len(shape))]
    values = values.at[tuple(index_at)].set(low)
    longest = shape.index(max(shape))
    index_at[longest] = (index_at[longest] + 1) % shape[longest]
    return values.at[tuple(index_at)].set(high)


def shard_levels(own_key, extent, pieces, low, largest):
    loudness, own = 1.0, jax.random.fold_in(own_key, 6)
    for dim, blocks in pieces:
        steps = jnp.exp(jax.random.uniform(jax.random.fold_in(own, dim), (blocks,), jnp.float32, low / len(pieces), largest / len(pieces)))
        loudness = loudness * jnp.repeat(steps, extent[dim] // blocks).reshape([-1 if axis == dim else 1 for axis in range(len(extent))])
    return loudness


def cumulative_ranks(amount, lean):
    weights = [(1 << 20) // math.isqrt(standing ** lean) + 1 for standing in range(1, amount + 1)]
    width = 1 + sum(weights) // (1 << 30)
    return np.cumsum(np.array([max(1, weight // width) for weight in weights]))


def ranked(key, shape, number_of, skew):
    listing = cumulative_ranks(number_of, skew)
    lot = jax.random.randint(jax.random.fold_in(key, 1), shape, 0, int(listing[number_of - 1]))
    rank = jnp.searchsorted(jnp.asarray(listing, jnp.int32), lot, side="right")
    return jax.random.permutation(jax.random.fold_in(key, 2), number_of)[rank].astype(jnp.int32)


def split_up(number_of, total, bound, lean):
    loads = [(1 << 20) // math.isqrt(standing ** lean) + 1 for standing in range(2, number_of + 1)]
    rest, holding = total - bound - (number_of - 1), [1] * (number_of - 1)
    while rest > 0:
        free = [i for i in range(number_of - 1) if holding[i] < bound]
        whole, budget = sum([loads[i] for i in free]), rest
        for i in free:
            extra = min(bound - holding[i], max(1, budget * loads[i] // whole), rest)
            holding[i] = holding[i] + extra
            rest = rest - extra
    return np.array([bound] + holding)


def uneven(key, number_of, total, bound, skew):
    if number_of == 2:
        one = jax.random.randint(key, (), max(1, total - bound), min(bound, total - 1) + 1)
        return jnp.stack([one, total - one])
    tallies = jnp.asarray(split_up(number_of, total, bound, skew), jnp.int32)
    couples = (number_of - 1) // 2
    donor, receiver = tallies[1:1 + 2 * couples:2], tallies[2:2 + 2 * couples:2]
    slack = jnp.minimum(donor - 1, bound - receiver)
    shifted = jax.random.randint(jax.random.fold_in(key, 1), (couples,), 0, 1 << 20) % (slack + 1)
    tallies = tallies.at[1:1 + 2 * couples:2].set(donor - shifted).at[2:2 + 2 * couples:2].set(receiver + shifted)
    return tallies[jax.random.permutation(jax.random.fold_in(key, 2), number_of)]


def gaussian(key, extent, deviation, most, cuts=(), held_as=jnp.bfloat16):
    entries = jax.random.normal(key, extent, jnp.float32) * deviation
    if len(cuts) > 0:
        entries = shard_levels(key, extent, cuts, -0.22, 0.18) * entries
    return jnp.clip(entries, min=-most, max=most).astype(held_as)


def setup_inputs(seed: int = 0) -> dict:
    keys = jax.random.split(jax.random.key(seed), 30)
    token_ids = touch_ends(ranked(keys[0], (N_DP, ROWS_G, SEQ), VOCAB, 2), jax.random.fold_in(keys[0], 3), 0, VOCAB - 1).astype(jnp.int32)
    segments = jax.vmap(lambda own: jnp.searchsorted(jnp.cumsum(uneven(own, 8, SEQ, SEQ // 2, 2)), jnp.arange(SEQ), side="right"))(jax.random.split(keys[1], N_DP * ROWS_G)).reshape((N_DP, ROWS_G, SEQ)).astype(jnp.int32)
    positions = touch_ends(jax.random.randint(keys[2], (N_DP, ROWS_G, NMASK), 0, SEQ), jax.random.fold_in(keys[2], 1), 0, SEQ - 1).astype(jnp.int32)
    teacher = draw_teacher(jax.random.fold_in(keys[29], 71), 0)
    gate_noise = jnp.clip(jax.random.uniform(keys[4], (D + H + 2,), jnp.float32, 0.01, 0.99), 0.01, 0.99)
    unit_noise = jnp.clip(jax.random.uniform(keys[5], (FF,), jnp.float32, 0.01, 0.99), 0.01, 0.99)
    multipliers = jnp.clip(jax.random.uniform(keys[6], (2,), jnp.float32, 2.0, 40.0), 2.0, 40.0)
    step_count = jax.random.randint(keys[7], (1,), 1, 21).astype(jnp.int32)
    layer_mats = draw_layer_mats(jax.random.fold_in(keys[29], 71), 0)
    mats_first = gaussian(keys[9], (D, 5 * D + SEQ), (0.0009 * NPARAM ** -0.5), 9.5367431640625e-07, ((0, 32),), jnp.float32)
    mats_second = jnp.clip(jnp.exp(math.log(1.2605074319396725e-12) - 1.3862944 * jax.random.uniform(keys[10], (D, 5 * D + SEQ), jnp.float32) ** shard_levels(keys[10], (D, 5 * D + SEQ), ((0, 32),), -0.2, 0.2)), 3.1512685798491813e-13, 1.2605074319396725e-12)
    layer_vecs = draw_layer_vecs(jax.random.fold_in(keys[29], 71), 0)
    vecs_first = gaussian(keys[12], (14, D), (0.0009 * NPARAM ** -0.5), 9.5367431640625e-07, ((1, 32),), jnp.float32)
    vecs_second = jnp.clip(jnp.exp(math.log(1.2605074319396725e-12) - 1.3862944 * jax.random.uniform(keys[13], (14, D), jnp.float32) ** shard_levels(keys[13], (14, D), ((1, 32),), -0.2, 0.2)), 3.1512685798491813e-13, 1.2605074319396725e-12)
    ffn_mats = draw_ffn_mats(jax.random.fold_in(keys[29], 71), 0)
    ffn_first = gaussian(keys[15], (2, D, FF), (0.0009 * NPARAM ** -0.5), 9.5367431640625e-07, ((1, 4), (2, 8)), jnp.float32)
    ffn_second = jnp.clip(jnp.exp(math.log(1.2605074319396725e-12) - 1.3862944 * jax.random.uniform(keys[16], (2, D, FF), jnp.float32) ** shard_levels(keys[16], (2, D, FF), ((1, 4), (2, 8)), -0.2, 0.2)), 3.1512685798491813e-13, 1.2605074319396725e-12)
    unit_vecs = draw_unit_vecs(jax.random.fold_in(keys[29], 71), 0)
    unit_first = gaussian(keys[18], (2, FF), (0.0009 * NPARAM ** -0.5), 9.5367431640625e-07, ((1, 32),), jnp.float32)
    unit_second = jnp.clip(jnp.exp(math.log(1.2605074319396725e-12) - 1.3862944 * jax.random.uniform(keys[19], (2, FF), jnp.float32) ** shard_levels(keys[19], (2, FF), ((1, 32),), -0.2, 0.2)), 3.1512685798491813e-13, 1.2605074319396725e-12)
    word_table = draw_word_table(jax.random.fold_in(keys[29], 71), 0)
    table_first = gaussian(keys[21], (VOCAB, D), (0.0009 * NPARAM ** -0.5), 9.5367431640625e-07, ((0, 8), (1, 4)), jnp.float32)
    table_second = jnp.clip(jnp.exp(math.log(1.2605074319396725e-12) - 1.3862944 * jax.random.uniform(keys[22], (VOCAB, D), jnp.float32) ** shard_levels(keys[22], (VOCAB, D), ((0, 8), (1, 4)), -0.2, 0.2)), 3.1512685798491813e-13, 1.2605074319396725e-12)
    word_bias = gaussian(keys[23], (VOCAB,), 0.5, 3.0, ((0, 32),), jnp.float32)
    bias_first = gaussian(keys[24], (VOCAB,), (0.0009 * NPARAM ** -0.5), 9.5367431640625e-07, ((0, 32),), jnp.float32)
    bias_second = jnp.clip(jnp.exp(math.log(1.2605074319396725e-12) - 1.3862944 * jax.random.uniform(keys[25], (VOCAB,), jnp.float32) ** shard_levels(keys[25], (VOCAB,), ((0, 32),), -0.2, 0.2)), 3.1512685798491813e-13, 1.2605074319396725e-12)
    mask_logits = jnp.clip(jax.random.uniform(keys[26], (H + 2,), jnp.float32, 3.0, 6.0), 3.0, 6.0)
    mask_first = gaussian(keys[27], (H + 2,), (0.0009 * NPARAM ** -0.5), 9.5367431640625e-07, (), jnp.float32)
    mask_second = jnp.clip(jnp.exp(jax.random.uniform(keys[28], (H + 2,), jnp.float32, math.log(3.1512685798491813e-13), math.log(1.2605074319396725e-12))), 3.1512685798491813e-13, 1.2605074319396725e-12)
    return dict(token_ids=token_ids, segments=segments, positions=positions, teacher=teacher, gate_noise=gate_noise, unit_noise=unit_noise, multipliers=multipliers, step_count=step_count, layer_mats=layer_mats, mats_first=mats_first, mats_second=mats_second, layer_vecs=layer_vecs, vecs_first=vecs_first, vecs_second=vecs_second, ffn_mats=ffn_mats, ffn_first=ffn_first, ffn_second=ffn_second, unit_vecs=unit_vecs, unit_first=unit_first, unit_second=unit_second, word_table=word_table, table_first=table_first, table_second=table_second, word_bias=word_bias, bias_first=bias_first, bias_second=bias_second, mask_logits=mask_logits, mask_first=mask_first, mask_second=mask_second)


EPS_NORM = 1e-12
GAMMA = -0.1
ZETA = 1.1
BETA = 2.0 / 3.0
TARGET = 0.95
TEMPER = 2.0
MAX_NORM = 0.0001
BETA_ONE = 0.9
BETA_TWO = 0.999
ADAM_EPS = 1e-08
DECAY = 0.01
RATE_MATS = 0.5
RATE_VECS = 5.0
RATE_TABLE = 1.0
HIGHEST = lax.Precision.HIGHEST

@jax.custom_vjp
def low(v):
    return lax.optimization_barrier(v.astype(jnp.bfloat16)).astype(jnp.float32)

@jax.custom_vjp
def low_back(v):
    return v

def low_keep(v):
    return (low(v), None)

def low_pass(kept, grad):
    return (grad,)

def back_keep(v):
    return (v, None)

def back_low(kept, grad):
    return (low(grad),)
low.defvjp(low_keep, low_pass)
low_back.defvjp(back_keep, back_low)

def matmul(left, right):
    return jnp.dot(left, right, precision=HIGHEST, preferred_element_type=jnp.float32)

def layer_norm(values, gain, shift):
    center = values - lax.optimization_barrier(jnp.mean(values, -1, keepdims=True))
    spread = lax.optimization_barrier(jnp.mean(center * center, -1, keepdims=True))
    return center * lax.rsqrt(spread + EPS_NORM) * gain + shift

def gate(logit, noise):
    soft = jax.nn.sigmoid((jnp.log(noise) - jnp.log(1.0 - noise) + logit) / BETA)
    return jnp.clip(soft * (ZETA - GAMMA) + GAMMA, 0.0, 1.0)

def keep_score(logit):
    return jax.nn.sigmoid(logit - BETA * math.log(-GAMMA / ZETA))

def row_divergence(weights, row_ids, segment, picks, teach):
    mats, vecs, ffn_w, unit_w, table, bias, zhid, zhead, zmha, zmlp, zunit = weights
    word = low_back(table[row_ids])
    embed = word + mats[:, 5 * D:5 * D + SEQ].T
    start = layer_norm(embed, vecs[0], vecs[1]) * zhid
    start_low = low(start)
    queries = low_back(low(matmul(start_low, mats[:, :D]) + vecs[2]))
    keys_f = low_back(low(matmul(start_low, mats[:, D:2 * D])))
    values_f = low_back(low(matmul(start_low, mats[:, 2 * D:3 * D]) + vecs[3]))
    shape3 = (SEQ, H, DH)
    scores = low_back(jnp.einsum('qhd,khd->hqk', queries.reshape(shape3), keys_f.reshape(shape3), precision=HIGHEST) * DH ** (-0.5))
    same = segment[:, None] == segment[None, :]
    probs = jax.nn.softmax(jnp.where(same[None], scores, -1000000000.0), axis=-1)
    context = low_back(jnp.einsum('hqk,khd->qhd', low(probs), values_f.reshape(shape3), precision=HIGHEST))
    scaled = low((context * zhead[None, :, None]).reshape(SEQ, D))
    attn_res = low_back(matmul(scaled, mats[:, 3 * D:4 * D])) + vecs[4]
    middle = layer_norm(start + attn_res * zmha * zhid, vecs[5], vecs[6])
    hidden_pre = low_back(matmul(low(middle), ffn_w[0])) + unit_w[0]
    hidden = low(jax.nn.gelu(hidden_pre) * zunit)
    ffn_res = low_back(matmul(hidden, ffn_w[1].T)) + vecs[7]
    final = layer_norm(middle + ffn_res * zmlp * zhid, vecs[8], vecs[9])
    picked = low(final[picks])
    trans = low_back(matmul(picked, mats[:, 4 * D:5 * D])) + vecs[10]
    trans_low = low(layer_norm(jax.nn.gelu(trans), vecs[11], vecs[12]))
    student = (low_back(matmul(trans_low, table.T)) + bias) / TEMPER
    teach_log = jax.nn.log_softmax(teach.astype(jnp.float32) / TEMPER, axis=-1)
    return jnp.sum(jnp.exp(teach_log) * (teach_log - jax.nn.log_softmax(student, axis=-1)))

def forward(mats, vecs, ffn_w, unit_w, table, bias, masks, token_ids, segments, positions, teacher, gate_noise, unit_noise, multipliers):
    mats, vecs, ffn_w, unit_w, table, bias, masks = [low(item) for item in (mats, vecs, ffn_w, unit_w, table, bias, masks)]
    zhid = gate(vecs[13], gate_noise[:D])
    zhead = gate(masks[:H], gate_noise[D:D + H])
    zmha = gate(masks[H], gate_noise[D + H])
    zmlp = gate(masks[H + 1], gate_noise[D + H + 1])
    zunit = gate(unit_w[1], unit_noise)
    hid_sum = jnp.sum(keep_score(vecs[13]))
    head_sum = jnp.sum(keep_score(masks[:H])) * keep_score(masks[H])
    unit_sum = jnp.sum(keep_score(unit_w[1])) * keep_score(masks[H + 1])
    kept = (4.0 * DH * hid_sum * head_sum + 2.0 * hid_sum * unit_sum) / (4.0 * D * D + 2.0 * D * FF)
    weights = (mats, vecs, ffn_w, unit_w, table, bias, zhid, zhead, zmha, zmlp, zunit)
    row_fn = jax.checkpoint(row_divergence)

    def scan_step(total, row):
        return (total + row_fn(weights, row[0], row[1], row[2], row[3]), None)
    rows = (token_ids.reshape(-1, SEQ), segments.reshape(-1, SEQ), positions.reshape(-1, NMASK), teacher.reshape(-1, NMASK, VOCAB))
    total, _ = lax.scan(scan_step, jnp.zeros((), jnp.float32), rows)
    sparsity = 1.0 - kept
    lagrange = multipliers[0] * (sparsity - TARGET) + multipliers[1] * (sparsity - TARGET) ** 2
    return (TEMPER * TEMPER * total / NPOS + lagrange, kept)

def adamw(weight, first, second, grad, rate, count):
    first = BETA_ONE * first + (1.0 - BETA_ONE) * grad
    second = BETA_TWO * second + (1.0 - BETA_TWO) * grad * grad
    first_hat = first / (1.0 - BETA_ONE ** count)
    second_hat = second / (1.0 - BETA_TWO ** count)
    return weight - rate * (first_hat / (jnp.sqrt(second_hat) + ADAM_EPS) + DECAY * weight)

def reference(token_ids, segments, positions, teacher, gate_noise, unit_noise, multipliers, step_count, layer_mats, mats_first, mats_second, layer_vecs, vecs_first, vecs_second, ffn_mats, ffn_first, ffn_second, unit_vecs, unit_first, unit_second, word_table, table_first, table_second, word_bias, bias_first, bias_second, mask_logits, mask_first, mask_second):

    def objective(mats, vecs, ffn_w, unit_w, table, bias, masks):
        return forward(mats, vecs, ffn_w, unit_w, table, bias, masks, token_ids, segments, positions, teacher, gate_noise, unit_noise, multipliers)
    params = (layer_mats, layer_vecs, ffn_mats, unit_vecs, word_table, word_bias, mask_logits)
    loss, pull, kept = jax.vjp(objective, *params, has_aux=True)
    grads = pull(jnp.ones((), loss.dtype))
    grad_norm = jnp.sqrt(sum((jnp.sum(item * item) for item in grads)))
    coef = jnp.minimum(1.0, MAX_NORM / (grad_norm + 1e-06))
    count = step_count[0].astype(jnp.float32)
    mats_grad = grads[0] * coef
    vecs_grad = grads[1] * coef
    ffn_grad = grads[2] * coef
    unit_grad = grads[3] * coef
    table_grad = grads[4] * coef
    bias_grad = grads[5] * coef
    mask_grad = grads[6] * coef
    mats_new = adamw(layer_mats, mats_first, mats_second, mats_grad, RATE_MATS, count)
    vecs_new = adamw(layer_vecs, vecs_first, vecs_second, vecs_grad, RATE_VECS, count)
    ffn_new = adamw(ffn_mats, ffn_first, ffn_second, ffn_grad, RATE_MATS, count)
    unit_new = adamw(unit_vecs, unit_first, unit_second, unit_grad, RATE_VECS, count)
    table_new = adamw(word_table, table_first, table_second, table_grad, RATE_TABLE, count)
    bias_new = adamw(word_bias, bias_first, bias_second, bias_grad, RATE_VECS, count)
    mask_new = adamw(mask_logits, mask_first, mask_second, mask_grad, RATE_VECS, count)
    return (loss, kept, grad_norm, mats_new, mats_grad, vecs_new, vecs_grad, ffn_new, ffn_grad, unit_new, unit_grad, table_new, table_grad, bias_new, bias_grad, mask_new, mask_grad)
```

```python
import functools
import math

import jax
import jax.numpy as jnp
from jax import lax
from jax.experimental import pallas as pl
from jax.experimental.pallas import tpu as pltpu
from jax.sharding import PartitionSpec as P

EPS_NORM = 1e-12
GAMMA = -0.1
ZETA = 1.1
BETA = 2.0 / 3.0
TARGET = 0.95
TEMPER = 2.0
MAX_NORM = 0.0001
BETA_ONE = 0.9
BETA_TWO = 0.999
ADAM_EPS = 1e-08
DECAY = 0.01
RATE_MATS = 0.5
RATE_VECS = 5.0
RATE_TABLE = 1.0


MESH = pl.DeviceIdType.MESH
VMEM_LIMIT = 56 * 1024 * 1024


def on_chip():
    return pl.BlockSpec(memory_space=pltpu.VMEM)


def call_params(collective):
    return pltpu.CompilerParams(
        collective_id=collective, has_side_effects=True, vmem_limit_bytes=VMEM_LIMIT
    )


def greet_unit(n, me):
    barrier = pltpu.get_barrier_semaphore()

    def step(j, carry):
        pl.semaphore_signal(
            barrier, inc=1, device_id={"unit": lax.rem(me + j, n)}, device_id_type=MESH
        )
        return carry

    lax.fori_loop(1, n, step, 0)
    pl.semaphore_wait(barrier, n - 1)


def greet_all(nu, nd, me):
    barrier = pltpu.get_barrier_semaphore()

    def step(j, carry):
        peer = lax.rem(me + j, nu * nd)
        pl.semaphore_signal(
            barrier,
            inc=1,
            device_id={"unit": peer // nd, "dp": lax.rem(peer, nd)},
            device_id_type=MESH,
        )
        return carry

    lax.fori_loop(1, nu * nd, step, 0)
    pl.semaphore_wait(barrier, nu * nd - 1)


def gather_kernel(n, x_ref, out_ref, send_sem, recv_sem):
    me = lax.axis_index("unit")
    greet_unit(n, me)

    def copy(peer, slot):
        return pltpu.make_async_remote_copy(
            src_ref=x_ref,
            dst_ref=out_ref.at[slot],
            send_sem=send_sem.at[peer],
            recv_sem=recv_sem.at[slot],
            device_id={"unit": peer},
            device_id_type=MESH,
        )

    def start(j, carry):
        copy(lax.rem(me + j, n), me).start()
        return carry

    def wait(j, carry):
        peer = lax.rem(me + j, n)
        copy(peer, me).wait_send()
        copy(peer, peer).wait_recv()
        return carry

    lax.fori_loop(1, n, start, 0)
    out_ref[me] = x_ref[...]
    lax.fori_loop(1, n, wait, 0)


def gather_unit(x, n, collective):
    return pl.pallas_call(
        functools.partial(gather_kernel, n),
        out_shape=jax.ShapeDtypeStruct((n,) + x.shape, x.dtype),
        in_specs=[on_chip()],
        out_specs=on_chip(),
        scratch_shapes=[pltpu.SemaphoreType.DMA((n,)), pltpu.SemaphoreType.DMA((n,))],
        compiler_params=call_params(collective),
    )(x)


def scatter_kernel(n, x_ref, out_ref, held, send_sem, recv_sem):
    me = lax.axis_index("unit")
    greet_unit(n, me)

    def copy(peer, slot):
        return pltpu.make_async_remote_copy(
            src_ref=x_ref.at[peer],
            dst_ref=held.at[slot],
            send_sem=send_sem.at[peer],
            recv_sem=recv_sem.at[slot],
            device_id={"unit": peer},
            device_id_type=MESH,
        )

    def start(j, carry):
        copy(lax.rem(me + j, n), me).start()
        return carry

    def wait(j, carry):
        peer = lax.rem(me + j, n)
        copy(peer, me).wait_send()
        copy(peer, peer).wait_recv()
        return carry

    lax.fori_loop(1, n, start, 0)
    held[me] = x_ref[me]
    lax.fori_loop(1, n, wait, 0)
    out_ref[...] = jnp.zeros_like(out_ref)

    def add(j, carry):
        out_ref[...] += held[j].astype(jnp.float32)
        return carry

    lax.fori_loop(0, n, add, 0)


def scatter_unit(x, n, collective):
    return pl.pallas_call(
        functools.partial(scatter_kernel, n),
        out_shape=jax.ShapeDtypeStruct(x.shape[1:], jnp.float32),
        in_specs=[on_chip()],
        out_specs=on_chip(),
        scratch_shapes=[
            pltpu.VMEM(x.shape, x.dtype),
            pltpu.SemaphoreType.DMA((n,)),
            pltpu.SemaphoreType.DMA((n,)),
        ],
        compiler_params=call_params(collective),
    )(x)


def total_kernel(nu, nd, x_ref, out_ref, held, send_sem, recv_sem):
    n = nu * nd
    me = lax.axis_index("unit") * nd + lax.axis_index("dp")
    greet_all(nu, nd, me)

    def copy(peer, slot):
        return pltpu.make_async_remote_copy(
            src_ref=x_ref,
            dst_ref=held.at[slot],
            send_sem=send_sem.at[peer],
            recv_sem=recv_sem.at[slot],
            device_id={"unit": peer // nd, "dp": lax.rem(peer, nd)},
            device_id_type=MESH,
        )

    def start(j, carry):
        copy(lax.rem(me + j, n), me).start()
        return carry

    def wait(j, carry):
        peer = lax.rem(me + j, n)
        copy(peer, me).wait_send()
        copy(peer, peer).wait_recv()
        return carry

    lax.fori_loop(1, n, start, 0)
    held[me] = x_ref[...]
    lax.fori_loop(1, n, wait, 0)
    out_ref[...] = jnp.zeros_like(out_ref)

    def add(j, carry):
        out_ref[...] += held[j]
        return carry

    lax.fori_loop(0, n, add, 0)


def total_all(x, nu, nd, collective):
    n = nu * nd
    return pl.pallas_call(
        functools.partial(total_kernel, nu, nd),
        out_shape=jax.ShapeDtypeStruct(x.shape, x.dtype),
        in_specs=[on_chip()],
        out_specs=on_chip(),
        scratch_shapes=[
            pltpu.VMEM((n,) + x.shape, x.dtype),
            pltpu.SemaphoreType.DMA((n,)),
            pltpu.SemaphoreType.DMA((n,)),
        ],
        compiler_params=call_params(collective),
    )(x)


def fetch_kernel(
    nu, nd, cap, wanted, table, out, asked, match, rows, send_a, recv_a, send_b, recv_b, own_sem
):
    n = nu * nd
    my_unit = lax.axis_index("unit")
    my_dp = lax.axis_index("dp")
    me = my_unit * nd + my_dp
    vocab = table.shape[0]
    block = 1280 if vocab % 1280 == 0 else vocab
    greet_all(nu, nd, me)

    def ask(peer, slot):
        return pltpu.make_async_remote_copy(
            src_ref=wanted.at[peer // nd],
            dst_ref=asked.at[slot],
            send_sem=send_a.at[peer],
            recv_sem=recv_a.at[slot],
            device_id={"unit": peer // nd, "dp": lax.rem(peer, nd)},
            device_id_type=MESH,
        )

    def answer(unit, dp, from_unit, from_dp):
        peer = unit * nd + dp
        return pltpu.make_async_remote_copy(
            src_ref=rows.at[peer],
            dst_ref=out.at[from_dp, from_unit],
            send_sem=send_b.at[peer],
            recv_sem=recv_b.at[from_unit * nd + from_dp],
            device_id={"unit": unit, "dp": dp},
            device_id_type=MESH,
        )

    def ask_start(j, carry):
        ask(lax.rem(me + j, n), me).start()
        return carry

    def ask_wait(j, carry):
        peer = lax.rem(me + j, n)
        ask(peer, me).wait_send()
        ask(peer, peer).wait_recv()
        return carry

    lax.fori_loop(1, n, ask_start, 0)
    asked[me] = wanted[my_unit]
    lax.fori_loop(1, n, ask_wait, 0)

    def one_group(g, carry):
        dp = lax.rem(my_dp + g, nd)
        total = jnp.zeros((nu * cap, table.shape[1]), jnp.float32)
        for start in range(0, vocab, block):
            lanes = lax.broadcasted_iota(jnp.int32, (cap, block), 1) + start
            for unit in range(nu):
                ids = jnp.swapaxes(
                    jnp.broadcast_to(asked[unit * nd + dp], (8, 128)), 0, 1
                )[:cap, :1]
                match[unit * cap : (unit + 1) * cap, :] = jnp.where(
                    ids == lanes, 1.0, 0.0
                ).astype(jnp.bfloat16)
            total = total + jnp.dot(
                match[...], table[start : start + block, :], preferred_element_type=jnp.float32
            )
        for unit in range(nu):
            rows[unit * nd + dp] = total[unit * cap : (unit + 1) * cap].astype(jnp.bfloat16)

        def send(unit, carry):
            @pl.when(jnp.logical_or(unit != my_unit, dp != my_dp))
            def _():
                answer(unit, dp, my_unit, my_dp).start()

            return carry

        lax.fori_loop(0, nu, send, 0)
        return carry

    lax.fori_loop(0, nd, one_group, 0)
    own = pltpu.make_async_copy(rows.at[me], out.at[my_dp, my_unit], own_sem)
    own.start()
    own.wait()

    def answer_wait(j, carry):
        peer = lax.rem(me + j, n)
        unit, dp = peer // nd, lax.rem(peer, nd)
        answer(unit, dp, my_unit, my_dp).wait_send()
        answer(unit, dp, unit, dp).wait_recv()
        return carry

    lax.fori_loop(1, n, answer_wait, 0)


def fetch_rows(wanted, table, nu, nd, cap, collective):
    n = nu * nd
    vocab, part = table.shape
    block = 1280 if vocab % 1280 == 0 else vocab
    return pl.pallas_call(
        functools.partial(fetch_kernel, nu, nd, cap),
        out_shape=(
            jax.ShapeDtypeStruct((nd, nu, cap, part), jnp.bfloat16),
            jax.ShapeDtypeStruct((n, 1, 128), jnp.int32),
        ),
        in_specs=[on_chip(), on_chip()],
        out_specs=(on_chip(), on_chip()),
        scratch_shapes=[
            pltpu.VMEM((nu * cap, block), jnp.bfloat16),
            pltpu.VMEM((n, cap, part), jnp.bfloat16),
            pltpu.SemaphoreType.DMA((n,)),
            pltpu.SemaphoreType.DMA((n,)),
            pltpu.SemaphoreType.DMA((n,)),
            pltpu.SemaphoreType.DMA((n,)),
            pltpu.SemaphoreType.DMA,
        ],
        compiler_params=call_params(collective),
    )(wanted, table)


def return_kernel(nu, nd, x_ref, out_ref, send_sem, recv_sem, own_sem):
    n = nu * nd
    my_unit = lax.axis_index("unit")
    my_dp = lax.axis_index("dp")
    me = my_unit * nd + my_dp
    greet_all(nu, nd, me)

    def copy(peer, slot):
        unit, dp = peer // nd, lax.rem(peer, nd)
        return pltpu.make_async_remote_copy(
            src_ref=x_ref.at[dp, unit],
            dst_ref=out_ref.at[slot],
            send_sem=send_sem.at[peer],
            recv_sem=recv_sem.at[slot],
            device_id={"unit": unit, "dp": dp},
            device_id_type=MESH,
        )

    def start(j, carry):
        copy(lax.rem(me + j, n), me).start()
        return carry

    def wait(j, carry):
        peer = lax.rem(me + j, n)
        copy(peer, me).wait_send()
        copy(peer, peer).wait_recv()
        return carry

    lax.fori_loop(1, n, start, 0)
    own = pltpu.make_async_copy(x_ref.at[my_dp, my_unit], out_ref.at[me], own_sem)
    own.start()
    own.wait()
    lax.fori_loop(1, n, wait, 0)


def return_rows(x, nu, nd, collective):
    n = nu * nd
    return pl.pallas_call(
        functools.partial(return_kernel, nu, nd),
        out_shape=jax.ShapeDtypeStruct((n,) + x.shape[2:], x.dtype),
        in_specs=[on_chip()],
        out_specs=on_chip(),
        scratch_shapes=[
            pltpu.SemaphoreType.DMA((n,)),
            pltpu.SemaphoreType.DMA((n,)),
            pltpu.SemaphoreType.DMA,
        ],
        compiler_params=call_params(collective),
    )(x)


def rounded(values):
    return lax.optimization_barrier(values.astype(jnp.bfloat16)).astype(jnp.float32)


def layer_norm(values, gain, shift):
    center = values - jnp.mean(values, -1, keepdims=True)
    spread = jnp.mean(center * center, -1, keepdims=True)
    return center * lax.rsqrt(spread + EPS_NORM) * gain + shift


def norm_back(values, gain, shift, grad):
    _, pull = jax.vjp(layer_norm, values, gain, shift)
    return pull(grad)


def gelu_back(values, grad):
    _, pull = jax.vjp(jax.nn.gelu, values)
    return pull(grad)[0]


def gate(logit, noise):
    soft = jax.nn.sigmoid((jnp.log(noise) - jnp.log(1.0 - noise) + logit) / BETA)
    return jnp.clip(soft * (ZETA - GAMMA) + GAMMA, 0.0, 1.0)


def gate_back(logit, noise, grad):
    _, pull = jax.vjp(gate, logit, noise)
    return pull(grad)[0]


def keep_score(logit):
    return jax.nn.sigmoid(logit - BETA * math.log(-GAMMA / ZETA))


def score_slope(logit):
    score = keep_score(logit)
    return score * (1.0 - score)


def contract_rows(left, right):
    return lax.dot_general(
        left, right, (((0,), (0,)), ((), ())), preferred_element_type=jnp.float32
    )


def adamw(weight, first, second, grad, rate, count):
    first = BETA_ONE * first + (1.0 - BETA_ONE) * grad
    second = BETA_TWO * second + (1.0 - BETA_TWO) * grad * grad
    first_hat = first / (1.0 - BETA_ONE**count)
    second_hat = second / (1.0 - BETA_TWO**count)
    return weight - rate * (first_hat / (jnp.sqrt(second_hat) + ADAM_EPS) + DECAY * weight)


def on_device(
    token_ids,
    segments,
    positions,
    teacher,
    gate_noise,
    unit_noise,
    multipliers,
    step_count,
    layer_mats,
    mats_first,
    mats_second,
    layer_vecs,
    vecs_first,
    vecs_second,
    ffn_mats,
    ffn_first,
    ffn_second,
    unit_vecs,
    unit_first,
    unit_second,
    word_table,
    table_first,
    table_second,
    word_bias,
    bias_first,
    bias_second,
    mask_logits,
    mask_first,
    mask_second,
):
    low_type = jnp.bfloat16
    full_type = jnp.float32
    exact = lax.Precision.HIGHEST
    units_n = lax.axis_size("unit")
    groups_n = lax.axis_size("dp")
    everyone = ("unit", "dp")
    heads = mask_logits.shape[0] - 2
    share_rows = layer_mats.shape[0]
    width = share_rows * units_n * groups_n
    head_size = width // heads
    seq_len = segments.shape[2]
    nmask = positions.shape[2]
    unit_idx = lax.axis_index("unit")
    n_vecs = layer_vecs.shape[0]
    vec_pad = -n_vecs % 128
    vocab_slice = word_table.shape[0]
    table_part = word_table.shape[1]
    cap = 16 * -(-5 * seq_len // (4 * 16 * units_n))

    mats_low = layer_mats.astype(low_type)
    qkv_cols = 3 * width
    trans_end = 5 * width
    table_low = word_table.astype(low_type)
    first_send = jnp.concatenate(
        [
            mats_low[:, :qkv_cols],
            mats_low[:, trans_end:],
            jnp.pad(layer_vecs.T, ((0, 0), (0, vec_pad))).astype(low_type),
        ],
        1,
    )
    first_all = lax.all_gather(first_send, everyone, axis=0, tiled=True)
    second_all = lax.all_gather(mats_low[:, qkv_cols:trans_end], everyone, axis=0, tiled=True)
    small_len = unit_vecs.size + word_bias.size
    ffn_cols = ffn_mats.shape[2]
    small_rows = -(-small_len // (16 * ffn_cols)) * 16
    ffn_rows = ffn_mats.shape[1]
    slice_pack = jnp.concatenate(
        [
            ffn_mats.reshape(2 * ffn_rows, ffn_cols),
            jnp.pad(
                jnp.concatenate([unit_vecs.reshape(-1), word_bias]),
                (0, small_rows * ffn_cols - small_len),
            ).reshape(small_rows, ffn_cols),
        ],
        0,
    ).astype(low_type)
    slice_all = lax.all_gather(slice_pack, "dp", axis=0)
    table_cols = lax.all_gather(table_low.T, "dp", axis=0, tiled=True)

    ids = lax.dynamic_index_in_dim(token_ids[0], unit_idx, 0, keepdims=False)
    place = jnp.arange(seq_len, dtype=jnp.int32)
    same_id = ids[:, None] == ids[None, :]
    first_place = jnp.min(jnp.where(same_id, place[None, :], seq_len), 1)
    is_first = first_place == place
    owner = ids // vocab_slice
    slot = jnp.sum(
        (
            is_first[None, :]
            & (owner[None, :] == owner[:, None])
            & (place[None, :] < first_place[:, None])
        ).astype(jnp.int32),
        1,
    )
    slots_used = jnp.max(slot) + 1
    local_id = ids - owner * vocab_slice
    entry = jnp.arange(units_n * cap, dtype=jnp.int32)

    def round_match(k):
        here = slot - k * cap
        code = jnp.where((here >= 0) & (here < cap), owner * cap + here, -1)
        return entry[:, None] == code[None, :]

    def round_wanted(match):
        return jnp.max(
            jnp.where(match & is_first[None, :], local_id[None, :], -1), 1
        ).reshape(units_n, cap)

    match_0 = round_match(0)
    wanted_0 = jnp.concatenate(
        [
            round_wanted(match_0),
            jnp.broadcast_to(slots_used, (units_n, 128 - cap)),
        ],
        1,
    )[:, None, :]
    fetched, asked = fetch_rows(wanted_0, table_low, units_n, groups_n, cap, 1)
    asked = asked[:, 0, :]
    rounds = (jnp.max(asked[:, cap:]) + cap - 1) // cap
    match_0 = match_0.astype(low_type)

    def spread(match, parts):
        return jnp.concatenate(
            [
                contract_rows(match, parts[d].reshape(units_n * cap, table_part))
                for d in range(groups_n)
            ],
            1,
        )

    def round_asked(match):
        wanted_all = lax.all_gather(round_wanted(match), everyone, axis=0)
        return lax.dynamic_index_in_dim(wanted_all, unit_idx, 1, keepdims=False)

    def more_words(k, words):
        match = round_match(k)
        mine = round_asked(match)
        found = jnp.where(
            (mine >= 0)[:, :, None], jnp.take(table_low, jnp.maximum(mine, 0), axis=0), 0
        )
        found = lax.all_to_all(found, everyone, 0, 0, tiled=True)
        found = jnp.swapaxes(
            found.reshape(units_n, groups_n, cap, table_part), 0, 1
        )
        return words + spread(match.astype(low_type), found)

    word = lax.fori_loop(1, rounds, more_words, spread(match_0, fetched))

    vecs_f = first_all[:, qkv_cols + seq_len : qkv_cols + seq_len + n_vecs].T.astype(full_type)
    masks_r = rounded(mask_logits)
    hid_logit = vecs_f[13]
    noise_hid = gate_noise[:width]
    noise_head = gate_noise[width : width + heads]
    zhid = gate(hid_logit, noise_hid)
    zhead = gate(masks_r[:heads], noise_head)
    zmha = gate(masks_r[heads], gate_noise[width + heads])
    zmlp = gate(masks_r[heads + 1], gate_noise[width + heads + 1])
    w_q = first_all[:, :width]
    w_kv = first_all[:, width:qkv_cols]
    w_out = second_all[:, :width]
    w_trans = second_all[:, width:]
    pos_table = first_all[:, qkv_cols : qkv_cols + seq_len].T.astype(full_type)
    embed = word + pos_table
    start_norm = layer_norm(embed, vecs_f[0], vecs_f[1])
    start = start_norm * zhid
    start_low = start.astype(low_type)

    picks = positions.reshape(-1)
    pick_low = (picks[:, None] == place[None, :]).astype(low_type)
    pick_full = pick_low.astype(full_type)
    start_p = jnp.dot(pick_full, start, precision=exact, preferred_element_type=full_type)
    start_p_low = start_p.astype(low_type)
    seg = segments.reshape(-1)
    seg_p = jnp.sum(jnp.where(picks[:, None] == place[None, :], seg[None, :], 0), 1)
    same = seg_p[:, None] == seg[None, :]
    queries = (
        jnp.dot(start_p_low, w_q, preferred_element_type=full_type) + vecs_f[2]
    ).astype(low_type)
    kv = jnp.dot(start_low, w_kv, preferred_element_type=full_type)
    keys_b = kv[:, :width].astype(low_type)
    values_b = (kv[:, width:] + vecs_f[3]).astype(low_type)
    scale = head_size ** (-0.5)
    q3 = queries.reshape(nmask, heads, head_size)
    k3 = keys_b.reshape(seq_len, heads, head_size)
    v3 = values_b.reshape(seq_len, heads, head_size)
    scores = jnp.einsum("qhd,khd->hqk", q3, k3, preferred_element_type=full_type) * scale
    probs = jax.nn.softmax(jnp.where(same[None], scores, -1000000000.0), axis=-1)
    probs_low = probs.astype(low_type)
    context = jnp.einsum(
        "hqk,khd->qhd", probs_low, v3, preferred_element_type=full_type
    ).reshape(nmask, width)
    context_r = context
    zcols = jnp.repeat(zhead, head_size)
    scaled = (context_r * zcols).astype(low_type)
    attn_res = jnp.dot(scaled, w_out, preferred_element_type=full_type) + vecs_f[4]
    middle_in = start_p + attn_res * zmha * zhid
    middle = layer_norm(middle_in, vecs_f[5], vecs_f[6])
    rows_all = gather_unit(middle.astype(low_type), units_n, 2).reshape(-1, width)

    up_w = slice_all[:, :ffn_rows].reshape(width, ffn_cols)
    down_w = slice_all[:, ffn_rows : 2 * ffn_rows].reshape(width, ffn_cols)
    small = slice_all[:, 2 * ffn_rows :].reshape(groups_n, -1)
    unit_group = jnp.swapaxes(
        small[:, : unit_vecs.size].reshape(groups_n, 2, unit_vecs.shape[1]), 0, 1
    ).reshape(2, -1)
    bias_group = small[:, unit_vecs.size : small_len].reshape(-1).astype(full_type)
    unit_bias = unit_group[0].astype(full_type)
    unit_logit = unit_group[1].astype(full_type)
    slice_units = unit_bias.shape[0]
    ffn_width = slice_units * units_n
    noise_units = lax.dynamic_slice_in_dim(unit_noise, unit_idx * slice_units, slice_units, 0)
    zunit = gate(unit_logit, noise_units)
    hidden_pre = jnp.dot(rows_all, up_w, preferred_element_type=full_type) + unit_bias
    hidden_gelu = jax.nn.gelu(hidden_pre)
    hidden = (hidden_gelu * zunit).astype(low_type)
    rows3 = (units_n, nmask, width)
    ffn_out = scatter_unit(
        jnp.dot(hidden, down_w.T, preferred_element_type=full_type)
        .astype(low_type)
        .reshape(rows3),
        units_n,
        3,
    )
    ffn_res = ffn_out + vecs_f[7]
    final_in = middle + ffn_res * zmlp * zhid
    final = layer_norm(final_in, vecs_f[8], vecs_f[9])
    picked = final.astype(low_type)
    trans_pre = jnp.dot(picked, w_trans, preferred_element_type=full_type) + vecs_f[10]
    trans_gelu = jax.nn.gelu(trans_pre)
    trans_low = layer_norm(trans_gelu, vecs_f[11], vecs_f[12]).astype(low_type)
    trans_all = gather_unit(trans_low, units_n, 4).reshape(-1, width)

    student = (
        jnp.dot(trans_all, table_cols, preferred_element_type=full_type) + bias_group
    ) / TEMPER
    teach = teacher.reshape(-1, vocab_slice).astype(full_type) / TEMPER
    s_max = jnp.max(student, -1)
    s_sum = jnp.sum(jnp.exp(student - s_max[:, None]), -1)
    t_max = jnp.max(teach, -1)
    t_exp = jnp.exp(teach - t_max[:, None])
    t_sum = jnp.sum(t_exp, -1)
    cross = jnp.sum(t_exp * (teach - student), -1)
    unit_part = jnp.sum(keep_score(unit_logit))
    stats = gather_unit(
        jnp.concatenate(
            [
                jnp.stack([s_max, s_sum, t_max, t_sum, cross]),
                jnp.broadcast_to(unit_part, (3, s_max.shape[0])),
            ],
            0,
        ),
        units_n,
        5,
    )
    s_top = jnp.max(stats[:, 0], 0)
    t_top = jnp.max(stats[:, 2], 0)
    s_all = jnp.sum(stats[:, 1] * jnp.exp(stats[:, 0] - s_top), 0)
    t_scale = jnp.exp(stats[:, 2] - t_top)
    t_all = jnp.sum(stats[:, 3] * t_scale, 0)
    cross_all = jnp.sum(stats[:, 4] * t_scale, 0)
    unit_score = jnp.sum(stats[:, 5, 0])
    lse_student = s_top + jnp.log(s_all)
    lse_teach = t_top + jnp.log(t_all)
    kl_rows = cross_all / t_all - lse_teach + lse_student
    kl_own = jnp.sum(lax.dynamic_slice_in_dim(kl_rows, unit_idx * nmask, nmask, 0))
    npos = groups_n * kl_rows.shape[0]
    grad_logit = (
        TEMPER
        / npos
        * (jnp.exp(student - lse_student[:, None]) - jnp.exp(teach - lse_teach[:, None]))
    )
    grad_bias = jnp.sum(grad_logit, 0)
    grad_logit_low = grad_logit.astype(low_type)
    grad_trans = scatter_unit(
        lax.dot_general(
            grad_logit_low,
            table_cols,
            (((1,), (1,)), ((), ())),
            preferred_element_type=full_type,
        )
        .astype(low_type)
        .reshape(rows3),
        units_n,
        6,
    )
    grad_table = contract_rows(trans_all, grad_logit_low).astype(low_type)
    share_head = lax.psum_scatter(grad_table, "dp", scatter_dimension=0, tiled=True)

    hid_sum = jnp.sum(keep_score(hid_logit))
    head_scores = keep_score(masks_r[:heads])
    mha_score = keep_score(masks_r[heads])
    mlp_score = keep_score(masks_r[heads + 1])
    head_sum = jnp.sum(head_scores) * mha_score
    unit_sum = unit_score * mlp_score
    full_size = 4.0 * width * width + 2.0 * width * ffn_width
    kept = (4.0 * head_size * hid_sum * head_sum + 2.0 * hid_sum * unit_sum) / full_size
    sparsity = 1.0 - kept
    lagrange = multipliers[0] * (sparsity - TARGET) + multipliers[1] * (sparsity - TARGET) ** 2
    lag_slope = -(multipliers[0] + 2.0 * multipliers[1] * (sparsity - TARGET))
    grad_tgelu, grad_hgain, grad_hshift = norm_back(trans_gelu, vecs_f[11], vecs_f[12], grad_trans)
    grad_tpre = gelu_back(trans_pre, grad_tgelu)
    grad_tbias = jnp.sum(grad_tpre, 0)
    grad_tpre_low = grad_tpre.astype(low_type)
    grad_wtrans = contract_rows(picked, grad_tpre_low)
    grad_final = jnp.dot(grad_tpre_low, w_trans.T, preferred_element_type=full_type)
    grad_final_in, grad_gain2, grad_shift2 = norm_back(final_in, vecs_f[8], vecs_f[9], grad_final)
    grad_fres = grad_final_in * zmlp * zhid
    grad_dbias = jnp.sum(grad_fres, 0)
    grad_zmlp = jnp.sum(grad_final_in * ffn_res * zhid)
    grad_zhid = jnp.sum(grad_final_in * ffn_res * zmlp, 0)
    back_all = gather_unit(grad_fres.astype(low_type), units_n, 7).reshape(-1, width)
    grad_hidden = jnp.dot(back_all, down_w, preferred_element_type=full_type)
    grad_hpre = gelu_back(hidden_pre, grad_hidden * zunit)
    grad_hpre_low = grad_hpre.astype(low_type)
    grad_middle_ffn = scatter_unit(
        jnp.dot(grad_hpre_low, up_w.T, preferred_element_type=full_type)
        .astype(low_type)
        .reshape(rows3),
        units_n,
        8,
    )
    grad_down = contract_rows(back_all, hidden)
    grad_up = contract_rows(rows_all, grad_hpre_low)
    grad_zunit = jnp.sum(grad_hidden * hidden_gelu, 0)
    grad_ubias = jnp.sum(grad_hpre, 0)
    grad_ulogit = gate_back(unit_logit, noise_units, grad_zunit)
    small_grads = jnp.concatenate(
        [
            jnp.swapaxes(
                jnp.stack([grad_ubias, grad_ulogit]).reshape(2, groups_n, -1), 0, 1
            ).reshape(groups_n, -1),
            grad_bias.reshape(groups_n, -1),
        ],
        1,
    )
    slice_grads = jnp.concatenate(
        [
            grad_up.astype(low_type).reshape(groups_n, ffn_rows, ffn_cols),
            grad_down.astype(low_type).reshape(groups_n, ffn_rows, ffn_cols),
            jnp.pad(small_grads, ((0, 0), (0, small_rows * ffn_cols - small_len)))
            .astype(low_type)
            .reshape(groups_n, small_rows, ffn_cols),
        ],
        1,
    )
    share_slice = lax.psum_scatter(slice_grads, "dp", scatter_dimension=0, tiled=False).astype(
        full_type
    )

    grad_middle_in, grad_gain1, grad_shift1 = norm_back(
        middle_in, vecs_f[5], vecs_f[6], grad_final_in + grad_middle_ffn
    )
    grad_ares = grad_middle_in * zmha * zhid
    grad_obias = jnp.sum(grad_ares, 0)
    grad_zmha = jnp.sum(grad_middle_in * attn_res * zhid)
    grad_zhid = grad_zhid + jnp.sum(grad_middle_in * attn_res * zmha, 0)
    grad_ares_low = grad_ares.astype(low_type)
    grad_wout = contract_rows(scaled, grad_ares_low)
    share_second = lax.psum_scatter(
        jnp.concatenate([grad_wout, grad_wtrans], 1).astype(low_type),
        everyone,
        scatter_dimension=0,
        tiled=True,
    ).astype(full_type)
    grad_scaled = jnp.dot(grad_ares_low, w_out.T, preferred_element_type=full_type)
    grad_zhead = jnp.sum((grad_scaled * context_r).reshape(nmask, heads, head_size), axis=(0, 2))
    g3 = (grad_scaled * zcols).astype(low_type).reshape(nmask, heads, head_size)
    grad_probs = jnp.einsum("qhd,khd->hqk", g3, v3, preferred_element_type=full_type)
    grad_scores = (probs * (grad_probs - jnp.sum(grad_probs * probs, -1, keepdims=True))).astype(
        low_type
    )
    grad_q = (
        jnp.einsum("hqk,khd->qhd", grad_scores, k3, preferred_element_type=full_type) * scale
    ).reshape(nmask, width)
    grad_k = (
        jnp.einsum("hqk,qhd->khd", grad_scores, q3, preferred_element_type=full_type) * scale
    ).reshape(seq_len, width)
    grad_v = jnp.einsum("hqk,qhd->khd", probs_low, g3, preferred_element_type=full_type).reshape(
        seq_len, width
    )
    grad_q_low = grad_q.astype(low_type)
    grad_kv = jnp.concatenate([grad_k, grad_v], 1).astype(low_type)
    grad_qbias = jnp.sum(grad_q_low.astype(full_type), 0)
    grad_vbias = jnp.sum(grad_kv[:, width:].astype(full_type), 0)
    grad_wq = contract_rows(start_p_low, grad_q_low)
    grad_wkv = contract_rows(start_low, grad_kv)
    grad_start_p = grad_middle_in + jnp.dot(grad_q_low, w_q.T, preferred_element_type=full_type)
    grad_start = lax.dot_general(
        pick_full,
        grad_start_p,
        (((0,), (0,)), ((), ())),
        precision=exact,
        preferred_element_type=full_type,
    ) + jnp.dot(grad_kv, w_kv.T, preferred_element_type=full_type)
    grad_zhid = grad_zhid + jnp.sum(grad_start * start_norm, 0)
    grad_embed, grad_gain0, grad_shift0 = norm_back(embed, vecs_f[0], vecs_f[1], grad_start * zhid)
    grad_hid = gate_back(hid_logit, noise_hid, grad_zhid)
    grad_vecs = jnp.stack(
        [
            grad_gain0,
            grad_shift0,
            grad_qbias,
            grad_vbias,
            grad_obias,
            grad_gain1,
            grad_shift1,
            grad_dbias,
            grad_gain2,
            grad_shift2,
            grad_tbias,
            grad_hgain,
            grad_hshift,
            grad_hid,
        ]
    )
    share_first = lax.psum_scatter(
        jnp.concatenate(
            [
                grad_wq.astype(low_type),
                grad_wkv.astype(low_type),
                grad_embed.T.astype(low_type),
                jnp.pad(grad_vecs.T, ((0, 0), (0, vec_pad))).astype(low_type),
            ],
            1,
        ),
        everyone,
        scatter_dimension=0,
        tiled=True,
    ).astype(full_type)

    embed_low = grad_embed.astype(low_type)

    def word_parts(match):
        return jnp.stack(
            [
                jnp.dot(
                    match,
                    embed_low[:, d * table_part : (d + 1) * table_part],
                    preferred_element_type=full_type,
                )
                .astype(low_type)
                .reshape(units_n, cap, table_part)
                for d in range(groups_n)
            ]
        )

    returned = return_rows(word_parts(match_0), units_n, groups_n, 9).reshape(-1, table_part)
    asked_ids = asked[:, :cap].reshape(-1)
    hit = (jnp.arange(vocab_slice, dtype=jnp.int32)[:, None] == asked_ids[None, :]).astype(low_type)
    share_table = share_head.astype(full_type).T + jnp.dot(
        hit, returned, preferred_element_type=full_type
    )

    def more_grads(k, total):
        match = round_match(k)
        mine = round_asked(match).reshape(-1)
        back = jnp.swapaxes(word_parts(match.astype(low_type)), 0, 1).reshape(
            units_n * groups_n, cap, table_part
        )
        back = lax.all_to_all(back, everyone, 0, 0, tiled=True).reshape(-1, table_part)
        target = jnp.where(mine >= 0, mine, vocab_slice)
        return total.at[target].add(back.astype(full_type), mode="drop")

    share_table = lax.fori_loop(1, rounds, more_grads, share_table)

    grad_head = gate_back(masks_r[:heads], noise_head, grad_zhead)
    grad_mha = gate_back(masks_r[heads], gate_noise[width + heads], grad_zmha)
    grad_mlp = gate_back(masks_r[heads + 1], gate_noise[width + heads + 1], grad_zmlp)
    share_mats = jnp.concatenate(
        [share_first[:, :qkv_cols], share_second, share_first[:, qkv_cols : qkv_cols + seq_len]], 1
    )
    share_vecs = share_first[:, qkv_cols + seq_len : qkv_cols + seq_len + n_vecs].T
    share_ffn = share_slice[: 2 * ffn_rows].reshape(2, ffn_rows, ffn_cols)
    share_small = share_slice[2 * ffn_rows :].reshape(-1)
    share_unit = share_small[: unit_vecs.size].reshape(unit_vecs.shape)
    share_bias = share_small[unit_vecs.size : small_len]
    own_hid = rounded(layer_vecs[13])
    own_unit = rounded(unit_vecs[1])
    lag_hid = (
        lag_slope * (4.0 * head_size * head_sum + 2.0 * unit_sum) / full_size * score_slope(own_hid)
    )
    share_vecs = share_vecs.at[13].add(lag_hid)
    lag_unit = lag_slope * 2.0 * hid_sum * mlp_score / full_size * score_slope(own_unit)
    share_unit = share_unit.at[1].add(lag_unit)
    lag_head = (
        lag_slope * 4.0 * head_size * hid_sum * mha_score / full_size * score_slope(masks_r[:heads])
    )
    lag_mha = (
        lag_slope
        * 4.0
        * head_size
        * hid_sum
        * jnp.sum(head_scores)
        / full_size
        * score_slope(masks_r[heads])
    )
    lag_mlp = lag_slope * 2.0 * hid_sum * unit_score / full_size * score_slope(masks_r[heads + 1])
    lag_masks = jnp.concatenate([lag_head, lag_mha[None], lag_mlp[None]])
    square_part = sum(
        (
            jnp.sum(item * item)
            for item in (share_mats, share_vecs, share_ffn, share_unit, share_table, share_bias)
        )
    )
    mine = jnp.concatenate(
        [grad_head, grad_mha[None], grad_mlp[None], kl_own[None], square_part[None]]
    )
    n_masks = heads + 2
    totals = total_all(
        jnp.pad(mine, (0, 1024 - mine.shape[0])).reshape(8, 128), units_n, groups_n, 10
    )[0]
    share_masks = totals[:n_masks] + lag_masks
    grad_norm = jnp.sqrt(totals[n_masks + 1] + jnp.sum(share_masks * share_masks))
    loss = TEMPER * TEMPER * totals[n_masks] / npos + lagrange
    coef = jnp.minimum(1.0, MAX_NORM / (grad_norm + 1e-06))
    count = step_count[0].astype(full_type)
    mats_grad = share_mats * coef
    vecs_grad = share_vecs * coef
    ffn_grad = share_ffn * coef
    unit_grad = share_unit * coef
    table_grad = share_table * coef
    bias_grad = share_bias * coef
    mask_grad = share_masks * coef
    mats_new = adamw(layer_mats, mats_first, mats_second, mats_grad, RATE_MATS, count)
    vecs_new = adamw(layer_vecs, vecs_first, vecs_second, vecs_grad, RATE_VECS, count)
    ffn_new = adamw(ffn_mats, ffn_first, ffn_second, ffn_grad, RATE_MATS, count)
    unit_new = adamw(unit_vecs, unit_first, unit_second, unit_grad, RATE_VECS, count)
    table_new = adamw(word_table, table_first, table_second, table_grad, RATE_TABLE, count)
    bias_new = adamw(word_bias, bias_first, bias_second, bias_grad, RATE_VECS, count)
    mask_new = adamw(mask_logits, mask_first, mask_second, mask_grad, RATE_VECS, count)
    return (
        loss,
        kept,
        grad_norm,
        mats_new,
        mats_grad,
        vecs_new,
        vecs_grad,
        ffn_new,
        ffn_grad,
        unit_new,
        unit_grad,
        table_new,
        table_grad,
        bias_new,
        bias_grad,
        mask_new,
        mask_grad,
    )


def solution(mesh):
    return jax.shard_map(
        on_device,
        mesh=mesh,
        in_specs=(
            P("dp", None, None),
            P("dp", "unit", None),
            P("dp", "unit", None),
            P("dp", None, None, "unit"),
            P(),
            P(),
            P(),
            P(),
            P(("unit", "dp"), None),
            P(("unit", "dp"), None),
            P(("unit", "dp"), None),
            P(None, ("unit", "dp")),
            P(None, ("unit", "dp")),
            P(None, ("unit", "dp")),
            P(None, "dp", "unit"),
            P(None, "dp", "unit"),
            P(None, "dp", "unit"),
            P(None, ("unit", "dp")),
            P(None, ("unit", "dp")),
            P(None, ("unit", "dp")),
            P("unit", "dp"),
            P("unit", "dp"),
            P("unit", "dp"),
            P(("unit", "dp")),
            P(("unit", "dp")),
            P(("unit", "dp")),
            P(),
            P(),
            P(),
        ),
        out_specs=(
            P(),
            P(),
            P(),
            P(("unit", "dp"), None),
            P(("unit", "dp"), None),
            P(None, ("unit", "dp")),
            P(None, ("unit", "dp")),
            P(None, "dp", "unit"),
            P(None, "dp", "unit"),
            P(None, ("unit", "dp")),
            P(None, ("unit", "dp")),
            P("unit", "dp"),
            P("unit", "dp"),
            P(("unit", "dp")),
            P(("unit", "dp")),
            P(),
            P(),
        ),
        check_vma=False,
    )
```

```python
import functools
import math

import jax
import jax.numpy as jnp
from jax import lax
from jax.experimental import pallas as pl
from jax.experimental.pallas import tpu as pltpu
from jax.sharding import PartitionSpec as P

EPS_NORM = 1e-12
GAMMA = -0.1
ZETA = 1.1
BETA = 2.0 / 3.0
TARGET = 0.95
TEMPER = 2.0
MAX_NORM = 0.0001
BETA_ONE = 0.9
BETA_TWO = 0.999
ADAM_EPS = 1e-08
DECAY = 0.01
RATE_MATS = 0.5
RATE_VECS = 5.0
RATE_TABLE = 1.0


def rounded(values):
    return lax.optimization_barrier(values.astype(jnp.bfloat16)).astype(jnp.float32)


def layer_norm(values, gain, shift):
    center = values - jnp.mean(values, -1, keepdims=True)
    spread = jnp.mean(center * center, -1, keepdims=True)
    return center * lax.rsqrt(spread + EPS_NORM) * gain + shift


def norm_back(values, gain, shift, grad):
    _, pull = jax.vjp(layer_norm, values, gain, shift)
    return pull(grad)


def gelu_back(values, grad):
    _, pull = jax.vjp(jax.nn.gelu, values)
    return pull(grad)[0]


def gate(logit, noise):
    soft = jax.nn.sigmoid((jnp.log(noise) - jnp.log(1.0 - noise) + logit) / BETA)
    return jnp.clip(soft * (ZETA - GAMMA) + GAMMA, 0.0, 1.0)


def gate_back(logit, noise, grad):
    _, pull = jax.vjp(gate, logit, noise)
    return pull(grad)[0]


def keep_score(logit):
    return jax.nn.sigmoid(logit - BETA * math.log(-GAMMA / ZETA))


def score_slope(logit):
    score = keep_score(logit)
    return score * (1.0 - score)


def contract_rows(left, right):
    return lax.dot_general(
        left, right, (((0,), (0,)), ((), ())), preferred_element_type=jnp.float32
    )


MESH = pl.DeviceIdType.MESH
VMEM_LIMIT = 56 * 1024 * 1024


def on_chip():
    return pl.BlockSpec(memory_space=pltpu.VMEM)


def call_params(collective):
    return pltpu.CompilerParams(
        collective_id=collective, has_side_effects=True, vmem_limit_bytes=VMEM_LIMIT
    )


def greet_unit(n, me):
    barrier = pltpu.get_barrier_semaphore()

    def step(j, carry):
        pl.semaphore_signal(
            barrier, inc=1, device_id={"unit": lax.rem(me + j, n)}, device_id_type=MESH
        )
        return carry

    lax.fori_loop(1, n, step, 0)
    pl.semaphore_wait(barrier, n - 1)


def greet_all(nu, nd, me):
    barrier = pltpu.get_barrier_semaphore()

    def step(j, carry):
        peer = lax.rem(me + j, nu * nd)
        pl.semaphore_signal(
            barrier,
            inc=1,
            device_id={"unit": peer // nd, "dp": lax.rem(peer, nd)},
            device_id_type=MESH,
        )
        return carry

    lax.fori_loop(1, nu * nd, step, 0)
    pl.semaphore_wait(barrier, nu * nd - 1)


def gather_kernel(n, x_ref, out_ref, send_sem, recv_sem):
    me = lax.axis_index("unit")
    greet_unit(n, me)

    def copy(peer, slot):
        return pltpu.make_async_remote_copy(
            src_ref=x_ref,
            dst_ref=out_ref.at[slot],
            send_sem=send_sem.at[peer],
            recv_sem=recv_sem.at[slot],
            device_id={"unit": peer},
            device_id_type=MESH,
        )

    def start(j, carry):
        copy(lax.rem(me + j, n), me).start()
        return carry

    def wait(j, carry):
        peer = lax.rem(me + j, n)
        copy(peer, me).wait_send()
        copy(peer, peer).wait_recv()
        return carry

    lax.fori_loop(1, n, start, 0)
    out_ref[me] = x_ref[...]
    lax.fori_loop(1, n, wait, 0)


def gather_unit(x, n, collective):
    return pl.pallas_call(
        functools.partial(gather_kernel, n),
        out_shape=jax.ShapeDtypeStruct((n,) + x.shape, x.dtype),
        in_specs=[on_chip()],
        out_specs=on_chip(),
        scratch_shapes=[pltpu.SemaphoreType.DMA((n,)), pltpu.SemaphoreType.DMA((n,))],
        compiler_params=call_params(collective),
    )(x)


def scatter_kernel(n, x_ref, out_ref, held, send_sem, recv_sem):
    me = lax.axis_index("unit")
    greet_unit(n, me)

    def copy(peer, slot):
        return pltpu.make_async_remote_copy(
            src_ref=x_ref.at[peer],
            dst_ref=held.at[slot],
            send_sem=send_sem.at[peer],
            recv_sem=recv_sem.at[slot],
            device_id={"unit": peer},
            device_id_type=MESH,
        )

    def start(j, carry):
        copy(lax.rem(me + j, n), me).start()
        return carry

    def wait(j, carry):
        peer = lax.rem(me + j, n)
        copy(peer, me).wait_send()
        copy(peer, peer).wait_recv()
        return carry

    lax.fori_loop(1, n, start, 0)
    held[me] = x_ref[me]
    lax.fori_loop(1, n, wait, 0)
    out_ref[...] = jnp.zeros_like(out_ref)

    def add(j, carry):
        out_ref[...] += held[j].astype(jnp.float32)
        return carry

    lax.fori_loop(0, n, add, 0)


def scatter_unit(x, n, collective):
    return pl.pallas_call(
        functools.partial(scatter_kernel, n),
        out_shape=jax.ShapeDtypeStruct(x.shape[1:], jnp.float32),
        in_specs=[on_chip()],
        out_specs=on_chip(),
        scratch_shapes=[
            pltpu.VMEM(x.shape, x.dtype),
            pltpu.SemaphoreType.DMA((n,)),
            pltpu.SemaphoreType.DMA((n,)),
        ],
        compiler_params=call_params(collective),
    )(x)


def total_kernel(nu, nd, x_ref, out_ref, held, send_sem, recv_sem):
    n = nu * nd
    me = lax.axis_index("unit") * nd + lax.axis_index("dp")
    greet_all(nu, nd, me)

    def copy(peer, slot):
        return pltpu.make_async_remote_copy(
            src_ref=x_ref,
            dst_ref=held.at[slot],
            send_sem=send_sem.at[peer],
            recv_sem=recv_sem.at[slot],
            device_id={"unit": peer // nd, "dp": lax.rem(peer, nd)},
            device_id_type=MESH,
        )

    def start(j, carry):
        copy(lax.rem(me + j, n), me).start()
        return carry

    def wait(j, carry):
        peer = lax.rem(me + j, n)
        copy(peer, me).wait_send()
        copy(peer, peer).wait_recv()
        return carry

    lax.fori_loop(1, n, start, 0)
    held[me] = x_ref[...]
    lax.fori_loop(1, n, wait, 0)
    out_ref[...] = jnp.zeros_like(out_ref)

    def add(j, carry):
        out_ref[...] += held[j]
        return carry

    lax.fori_loop(0, n, add, 0)


def total_all(x, nu, nd, collective):
    n = nu * nd
    return pl.pallas_call(
        functools.partial(total_kernel, nu, nd),
        out_shape=jax.ShapeDtypeStruct(x.shape, x.dtype),
        in_specs=[on_chip()],
        out_specs=on_chip(),
        scratch_shapes=[
            pltpu.VMEM((n,) + x.shape, x.dtype),
            pltpu.SemaphoreType.DMA((n,)),
            pltpu.SemaphoreType.DMA((n,)),
        ],
        compiler_params=call_params(collective),
    )(x)


def grid_of(nu, nd):
    ny = 2 if nu % 2 == 0 else 1
    nc = 2 if nd % 2 == 0 else 1
    return (nu // ny, ny, nd // nc, nc)


def grid_place(grid):
    unit, dp = lax.axis_index("unit"), lax.axis_index("dp")
    return (unit // grid[1], lax.rem(unit, grid[1]), dp // grid[3], lax.rem(dp, grid[3]))


def grid_device(grid, place):
    return {"unit": place[0] * grid[1] + place[1], "dp": place[2] * grid[3] + place[3]}


def moved(place, axis, index):
    return tuple(index if k == axis else place[k] for k in range(4))


GATHER_ORDERS = ((0, 1, 2, 3), (0, 2, 1, 3))
REDUCE_ORDERS = ((3, 2, 1, 0), (3, 1, 2, 0))


class Gather:
    def __init__(self, grid, place, order, x, out, send_sem, recv_sem):
        self.grid, self.place, self.order = grid, place, order
        self.x, self.out, self.send_sem, self.recv_sem = x, out, send_sem, recv_sem

    def window(self, stage, index):
        axis = self.order[stage]
        where = []
        for k in range(4):
            if k == axis:
                where.append(pl.ds(index, 1))
            elif k in self.order[:stage]:
                where.append(pl.ds(0, self.grid[k]))
            else:
                where.append(pl.ds(self.place[k], 1))
        return self.out.at[tuple(where)]

    def copy(self, stage, hop, arriving):
        axis = self.order[stage]
        n = self.grid[axis]
        mine = self.place[axis]
        to = lax.rem(mine + hop, n)
        held = self.window(stage, lax.rem(mine + n - hop, n) if arriving else mine)
        return pltpu.make_async_remote_copy(
            src_ref=held,
            dst_ref=held,
            send_sem=self.send_sem.at[stage, hop],
            recv_sem=self.recv_sem.at[stage, hop],
            device_id=grid_device(self.grid, moved(self.place, axis, to)),
            device_id_type=MESH,
        )

    def start(self, stage):
        if stage == 0:
            self.out[self.place] = self.x[...]
        for hop in range(1, self.grid[self.order[stage]]):
            self.copy(stage, hop, False).start()

    def finish(self, stage):
        for hop in range(1, self.grid[self.order[stage]]):
            self.copy(stage, hop, False).wait_send()
            self.copy(stage, hop, True).wait_recv()


class Reduce:
    def __init__(self, grid, place, order, x, helds, sums, out, send_sem, recv_sem):
        self.grid, self.place, self.order = grid, place, order
        self.refs = (x,) + tuple(sums)
        self.helds, self.out = helds, out
        self.send_sem, self.recv_sem = send_sem, recv_sem

    def window(self, stage, index):
        axis = self.order[stage]
        where = []
        for k in range(4):
            if k == axis:
                where.append(pl.ds(index, 1))
            elif k in self.order[:stage]:
                where.append(pl.ds(0, 1))
            else:
                where.append(pl.ds(0, self.grid[k]))
        return self.refs[stage].at[tuple(where)]

    def copy(self, stage, hop):
        axis = self.order[stage]
        to = lax.rem(self.place[axis] + hop, self.grid[axis])
        return pltpu.make_async_remote_copy(
            src_ref=self.window(stage, to),
            dst_ref=self.helds[stage].at[hop - 1],
            send_sem=self.send_sem.at[stage, hop],
            recv_sem=self.recv_sem.at[stage, hop],
            device_id=grid_device(self.grid, moved(self.place, axis, to)),
            device_id_type=MESH,
        )

    def start(self, stage):
        for hop in range(1, self.grid[self.order[stage]]):
            self.copy(stage, hop).start()

    def finish(self, stage):
        axis = self.order[stage]
        n = self.grid[axis]
        for hop in range(1, n):
            self.copy(stage, hop).wait()
        left = [
            1 if k in self.order[: stage + 1] else self.grid[k] for k in range(4)
        ]
        last = stage == 3

        def add(i, carry):
            where = []
            for k in (3, 2, 1, 0):
                where.insert(0, lax.rem(i, left[k]))
                i = i // left[k]
            own = moved(tuple(where), axis, self.place[axis])
            total = self.refs[stage][own].astype(jnp.float32)
            for hop in range(1, n):
                total = total + self.helds[stage][(hop - 1, *where)].astype(jnp.float32)
            if last:
                self.out[...] = total
            else:
                self.refs[stage + 1][tuple(where)] = total.astype(jnp.bfloat16)
            return carry

        lax.fori_loop(0, math.prod(left), add, 0)


def reduce_scratch(grid, orders, shapes):
    helds, sums = [], []
    for order, shape in zip(orders, shapes, strict=True):
        left = list(grid)
        for stage, axis in enumerate(order):
            n = left[axis]
            left[axis] = 1
            helds.append(pltpu.VMEM((max(n - 1, 1), *left, *shape), jnp.bfloat16))
            if stage < 3:
                sums.append(pltpu.VMEM((*left, *shape), jnp.bfloat16))
    return helds, sums


def fetch_kernel(nu, nd, cap, count, *refs):
    wanted, table = refs[:2]
    parts = refs[2 : 2 + count]
    out, asked = refs[2 + count : 4 + count]
    wholes = refs[4 + count : 4 + 2 * count]
    match, rows, send_a, recv_a, send_b, recv_b, own_sem, send_g, recv_g = refs[4 + 2 * count :]
    n = nu * nd
    grid = grid_of(nu, nd)
    place = grid_place(grid)
    gathers = [
        Gather(
            grid,
            place,
            GATHER_ORDERS[i % 2],
            parts[i],
            wholes[i],
            send_g.at[i],
            recv_g.at[i],
        )
        for i in range(count)
    ]
    my_unit = lax.axis_index("unit")
    my_dp = lax.axis_index("dp")
    me = my_unit * nd + my_dp
    vocab = table.shape[0]
    block = 1280 if vocab % 1280 == 0 else vocab
    greet_all(nu, nd, me)

    def ask(peer, slot):
        return pltpu.make_async_remote_copy(
            src_ref=wanted.at[peer // nd],
            dst_ref=asked.at[slot],
            send_sem=send_a.at[peer],
            recv_sem=recv_a.at[slot],
            device_id={"unit": peer // nd, "dp": lax.rem(peer, nd)},
            device_id_type=MESH,
        )

    def answer(unit, dp, from_unit, from_dp):
        peer = unit * nd + dp
        return pltpu.make_async_remote_copy(
            src_ref=rows.at[peer],
            dst_ref=out.at[from_dp, from_unit],
            send_sem=send_b.at[peer],
            recv_sem=recv_b.at[from_unit * nd + from_dp],
            device_id={"unit": unit, "dp": dp},
            device_id_type=MESH,
        )

    def ask_start(j, carry):
        ask(lax.rem(me + j, n), me).start()
        return carry

    def ask_wait(j, carry):
        peer = lax.rem(me + j, n)
        ask(peer, me).wait_send()
        ask(peer, peer).wait_recv()
        return carry

    lax.fori_loop(1, n, ask_start, 0)
    for gather in gathers:
        gather.start(0)
    asked[me] = wanted[my_unit]
    lax.fori_loop(1, n, ask_wait, 0)

    def one_group(g, carry):
        dp = lax.rem(my_dp + g, nd)
        total = jnp.zeros((nu * cap, table.shape[1]), jnp.float32)
        for start in range(0, vocab, block):
            lanes = lax.broadcasted_iota(jnp.int32, (cap, block), 1) + start
            for unit in range(nu):
                ids = jnp.swapaxes(
                    jnp.broadcast_to(asked[unit * nd + dp], (8, 128)), 0, 1
                )[:cap, :1]
                match[unit * cap : (unit + 1) * cap, :] = jnp.where(
                    ids == lanes, 1.0, 0.0
                ).astype(jnp.bfloat16)
            total = total + jnp.dot(
                match[...], table[start : start + block, :], preferred_element_type=jnp.float32
            )
        for unit in range(nu):
            rows[unit * nd + dp] = total[unit * cap : (unit + 1) * cap].astype(jnp.bfloat16)

        def send(unit, carry):
            @pl.when(jnp.logical_or(unit != my_unit, dp != my_dp))
            def _():
                answer(unit, dp, my_unit, my_dp).start()

            return carry

        lax.fori_loop(0, nu, send, 0)
        return carry

    def advance(t):
        for i, gather in enumerate(gathers):
            stage = t - i // 2
            if 0 <= stage < 4:
                gather.finish(stage)
                if stage < 3:
                    gather.start(stage + 1)

    lax.fori_loop(0, nd, one_group, 0)
    for t in range(4 + (count - 1) // 2):
        advance(t)
    own = pltpu.make_async_copy(rows.at[me], out.at[my_dp, my_unit], own_sem)
    own.start()
    own.wait()

    def answer_wait(j, carry):
        peer = lax.rem(me + j, n)
        unit, dp = peer // nd, lax.rem(peer, nd)
        answer(unit, dp, my_unit, my_dp).wait_send()
        answer(unit, dp, unit, dp).wait_recv()
        return carry

    lax.fori_loop(1, n, answer_wait, 0)


def fetch_rows(wanted, table, parts, nu, nd, cap, collective):
    n = nu * nd
    vocab, part = table.shape
    block = 1280 if vocab % 1280 == 0 else vocab
    count = len(parts)
    grid = grid_of(nu, nd)
    reach = max(grid)
    return pl.pallas_call(
        functools.partial(fetch_kernel, nu, nd, cap, count),
        out_shape=(
            jax.ShapeDtypeStruct((nd, nu, cap, part), jnp.bfloat16),
            jax.ShapeDtypeStruct((n, 1, 128), jnp.int32),
            *(jax.ShapeDtypeStruct((*grid, *x.shape), x.dtype) for x in parts),
        ),
        in_specs=[on_chip()] * (2 + count),
        out_specs=(on_chip(),) * (2 + count),
        scratch_shapes=[
            pltpu.VMEM((nu * cap, block), jnp.bfloat16),
            pltpu.VMEM((n, cap, part), jnp.bfloat16),
            pltpu.SemaphoreType.DMA((n,)),
            pltpu.SemaphoreType.DMA((n,)),
            pltpu.SemaphoreType.DMA((n,)),
            pltpu.SemaphoreType.DMA((n,)),
            pltpu.SemaphoreType.DMA,
            pltpu.SemaphoreType.DMA((count, 4, reach)),
            pltpu.SemaphoreType.DMA((count, 4, reach)),
        ],
        compiler_params=call_params(collective),
    )(wanted, table, *parts)


def return_kernel(nu, nd, count, *refs):
    x_ref, ids_ref, base_ref = refs[:3]
    grads = refs[3 : 3 + count]
    table_ref = refs[3 + count]
    shares = refs[4 + count : 4 + 2 * count]
    out_ref = refs[4 + 2 * count]
    rest = refs[5 + 2 * count :]
    helds, sums = rest[: 4 * count], rest[4 * count : 7 * count]
    send_sem, recv_sem, own_sem, send_r, recv_r = rest[7 * count :]
    n = nu * nd
    my_unit = lax.axis_index("unit")
    my_dp = lax.axis_index("dp")
    me = my_unit * nd + my_dp
    grid = grid_of(nu, nd)
    place = grid_place(grid)
    reduces = [
        Reduce(
            grid,
            place,
            REDUCE_ORDERS[i % 2],
            grads[i],
            helds[4 * i : 4 * i + 4],
            sums[3 * i : 3 * i + 3],
            shares[i],
            send_r.at[i],
            recv_r.at[i],
        )
        for i in range(count)
    ]
    greet_all(nu, nd, me)

    def copy(peer, slot):
        unit, dp = peer // nd, lax.rem(peer, nd)
        return pltpu.make_async_remote_copy(
            src_ref=x_ref.at[dp, unit],
            dst_ref=out_ref.at[slot],
            send_sem=send_sem.at[peer],
            recv_sem=recv_sem.at[slot],
            device_id={"unit": unit, "dp": dp},
            device_id_type=MESH,
        )

    def start(j, carry):
        copy(lax.rem(me + j, n), me).start()
        return carry

    def wait(j, carry):
        peer = lax.rem(me + j, n)
        copy(peer, me).wait_send()
        copy(peer, peer).wait_recv()
        return carry

    for reduce in reduces:
        reduce.start(0)
    lax.fori_loop(1, n, start, 0)
    own = pltpu.make_async_copy(x_ref.at[my_dp, my_unit], out_ref.at[me], own_sem)
    own.start()
    own.wait()

    vocab, part = base_ref.shape
    block = 384 if vocab % 384 == 0 else vocab // 5

    def add_rows(b, carry):
        first = pl.multiple_of(b * block, 64)
        lines = lax.broadcasted_iota(jnp.int32, (block, ids_ref.shape[1]), 0) + first
        hit = jnp.where(lines == ids_ref[...], 1.0, 0.0).astype(jnp.bfloat16)
        table_ref[pl.ds(first, block), :] = base_ref[pl.ds(first, block), :].astype(
            jnp.float32
        ) + jnp.dot(
            hit,
            out_ref[...].reshape(ids_ref.shape[1], part),
            preferred_element_type=jnp.float32,
        )
        return carry

    steps = 4 + (count - 1) // 2
    blocks = vocab // block
    for t in range(steps):
        for i, reduce in enumerate(reduces):
            stage = t - i // 2
            if 0 <= stage < 4:
                reduce.finish(stage)
                if stage < 3:
                    reduce.start(stage + 1)
        if t == 1:
            lax.fori_loop(1, n, wait, 0)
        if t >= 1:
            done, left = t - 1, steps - 1
            lax.fori_loop(blocks * done // left, blocks * (done + 1) // left, add_rows, 0)


def return_rows(x, ids, base, grads, nu, nd, collective):
    n = nu * nd
    grid = grid_of(nu, nd)
    count = len(grads)
    reach = max(grid)
    shapes = [(g.shape[0] // n, g.shape[1]) for g in grads]
    helds, sums = reduce_scratch(
        grid, [REDUCE_ORDERS[i % 2] for i in range(count)], shapes
    )
    return pl.pallas_call(
        functools.partial(return_kernel, nu, nd, count),
        out_shape=(
            jax.ShapeDtypeStruct(base.shape, jnp.float32),
            *(jax.ShapeDtypeStruct(shape, jnp.float32) for shape in shapes),
        ),
        in_specs=[on_chip()] * (3 + count),
        out_specs=(on_chip(),) * (1 + count),
        scratch_shapes=[
            pltpu.VMEM((n,) + x.shape[2:], x.dtype),
            *helds,
            *sums,
            pltpu.SemaphoreType.DMA((n,)),
            pltpu.SemaphoreType.DMA((n,)),
            pltpu.SemaphoreType.DMA,
            pltpu.SemaphoreType.DMA((count, 4, reach)),
            pltpu.SemaphoreType.DMA((count, 4, reach)),
        ],
        compiler_params=call_params(collective),
    )(x, ids, base, *(g.reshape(*grid, *shape) for g, shape in zip(grads, shapes, strict=True)))


class UnitGather:
    def __init__(self, n, me, buf, send_sem, recv_sem):
        self.n, self.me, self.buf = n, me, buf
        self.send_sem, self.recv_sem = send_sem, recv_sem
        self.inner = n // 2
        self.half, self.idx = me // self.inner, lax.rem(me, self.inner)
        self.mirror = (1 - self.half) * self.inner + self.idx

    def near(self, hop):
        return self.half * self.inner + lax.rem(self.idx + hop, self.inner)

    def copy(self, block, to, kind, hop):
        return pltpu.make_async_remote_copy(
            src_ref=self.buf.at[block],
            dst_ref=self.buf.at[block],
            send_sem=self.send_sem.at[kind, hop],
            recv_sem=self.recv_sem.at[block],
            device_id={"unit": to},
            device_id_type=MESH,
        )

    def hops(self, step):
        lax.fori_loop(1, self.inner, lambda hop, carry: (step(hop), carry)[1], 0)

    def start(self):
        self.copy(self.me, self.mirror, 0, 0).start()
        self.hops(lambda hop: self.copy(self.me, self.near(hop), 0, hop).start())

    def forward(self):
        self.copy(self.mirror, self.mirror, 0, 0).wait_recv()
        self.hops(lambda hop: self.copy(self.mirror, self.near(hop), 1, hop).start())

    def wait_half(self):
        self.hops(lambda hop: self.copy(self.near(hop), self.mirror, 0, 0).wait_recv())

    def wait_rest(self):
        far = (1 - self.half) * self.inner

        def step(hop):
            block = far + lax.rem(self.idx + hop, self.inner)
            self.copy(block, self.mirror, 0, 0).wait_recv()

        self.hops(step)

    def finish(self):
        self.copy(self.me, self.mirror, 0, 0).wait_send()

        def step(hop):
            self.copy(self.me, self.near(hop), 0, hop).wait_send()
            self.copy(self.mirror, self.near(hop), 1, hop).wait_send()

        self.hops(step)


class UnitReduce:
    def __init__(self, n, me, part, held, mine, other, send_sem, recv_sem):
        self.n, self.me, self.part = n, me, part
        self.held, self.mine, self.other = held, mine, other
        self.send_sem, self.recv_sem = send_sem, recv_sem
        self.inner = n // 2
        self.half, self.idx = me // self.inner, lax.rem(me, self.inner)
        self.mirror = (1 - self.half) * self.inner + self.idx

    def copy(self, kind, hop):
        index = lax.rem(self.idx + hop, self.inner)
        half = self.half if kind else 1 - self.half
        return pltpu.make_async_remote_copy(
            src_ref=self.part.at[half * self.inner + index],
            dst_ref=self.held.at[kind, hop - 1],
            send_sem=self.send_sem.at[kind, hop],
            recv_sem=self.recv_sem.at[kind, hop],
            device_id={"unit": self.half * self.inner + index},
            device_id_type=MESH,
        )

    def across(self):
        return pltpu.make_async_remote_copy(
            src_ref=self.mine,
            dst_ref=self.other,
            send_sem=self.send_sem.at[0, 0],
            recv_sem=self.recv_sem.at[0, 0],
            device_id={"unit": self.mirror},
            device_id_type=MESH,
        )

    def start(self, kind):
        def step(hop, carry):
            self.copy(kind, hop).start()
            return carry

        lax.fori_loop(1, self.inner, step, 0)

    def wait(self, kind):
        def step(hop, carry):
            self.copy(kind, hop).wait()
            return carry

        lax.fori_loop(1, self.inner, step, 0)

    def total(self, kind, block):
        result = self.part[block].astype(jnp.float32)
        for hop in range(1, self.inner):
            result = result + self.held[kind, hop - 1].astype(jnp.float32)
        return result

    def middle(self):
        self.wait(0)
        self.mine[...] = self.total(0, self.mirror).astype(jnp.bfloat16)
        self.across().start()

    def finish(self):
        self.wait(1)
        result = self.total(1, self.me)
        self.across().wait()
        return result + self.other[...].astype(jnp.float32)


def row_sum(values):
    return jnp.sum(values, 0, keepdims=True)


def mid_kernel(n, npos, *refs):
    middle_ref, up_ref, down_ref, unit_ref, table_ref, vbias_ref, teach_ref, wt_ref, vecs_ref = refs[
        :9
    ]
    gtable, gvbias, gup, gdown, gunit, gwt, gmid, gvecs, stat_out = refs[9:18]
    rows, backs, trans, hpre, hid, ghp, student, glow, acc, tmax, statc, stats = refs[18:30]
    part, mine, helds, others = refs[30], refs[31], refs[32:35], refs[35:38]
    gather_send, gather_recv, reduce_send, reduce_recv, stat_send, stat_recv = refs[38:44]
    me = lax.axis_index("unit")
    low, full = jnp.bfloat16, jnp.float32
    count, width = middle_ref.shape
    vocab = table_ref.shape[1]
    tile = 768 if vocab % 768 == 0 else vocab
    tiles = vocab // tile
    group = max(1, 256 // count)
    block = group * count
    per_half = n // 2 // group
    half = me // (n // 2)
    own_blocks = (half * per_half, (half + 1) * per_half)
    far_blocks = ((1 - half) * per_half, (2 - half) * per_half)
    greet_unit(n, me)
    gathers = [
        UnitGather(n, me, buf, gather_send.at[i], gather_recv.at[i])
        for i, buf in enumerate((rows, trans, backs))
    ]
    reduces = [
        UnitReduce(
            n, me, part, helds[i], mine, others[i], reduce_send.at[i], reduce_recv.at[i]
        )
        for i in range(3)
    ]

    def vec(k):
        return vecs_ref[k : k + 1, :]

    def loop(span, step):
        lax.fori_loop(span[0], span[1], lambda b, carry: (step(b), carry)[1], 0)

    def lines(b):
        return pl.ds(pl.multiple_of(b * block, block), block)

    def columns(v):
        return pl.ds(pl.multiple_of(v * tile, 128), tile)

    def gathered(buf, b):
        return buf[pl.ds(b * group, group)].reshape(block, width)

    def put_part(b, values):
        part[pl.ds(b * group, group)] = values.astype(low).reshape(group, count, width)

    middle = middle_ref[...]
    rows[me] = middle.astype(low)
    gathers[0].start()

    def teacher_top(b):
        top = jnp.max(teach_ref[lines(b), :].astype(full), 1, keepdims=True) / TEMPER
        tmax[lines(b), :] = jnp.broadcast_to(top, (block, 128))

    loop((0, n // group), teacher_top)
    gathers[0].forward()
    gathers[0].wait_half()

    def up_down(b):
        pre = (
            jnp.dot(gathered(rows, b), up_ref[...], preferred_element_type=full)
            + unit_ref[0:1, :]
        )
        hpre[lines(b), :] = pre
        hidden = (jax.nn.gelu(pre) * unit_ref[1:2, :]).astype(low)
        hid[lines(b), :] = hidden
        put_part(
            b,
            lax.dot_general(
                hidden, down_ref[...], (((1,), (1,)), ((), ())), preferred_element_type=full
            ),
        )

    loop(own_blocks, up_down)
    reduces[0].start(1)
    gathers[0].wait_rest()
    loop(far_blocks, up_down)
    reduces[0].start(0)
    reduces[0].middle()
    ffn_res = reduces[0].finish() + vec(7)
    final_in = middle + ffn_res * vec(14)
    final = layer_norm(final_in, vec(8), vec(9))
    picked = final.astype(low)
    trans_pre = jnp.dot(picked, wt_ref[...], preferred_element_type=full) + vec(10)
    trans_gelu = jax.nn.gelu(trans_pre)
    trans[me] = layer_norm(trans_gelu, vec(11), vec(12)).astype(low)
    gathers[1].start()
    gathers[0].finish()
    gathers[1].forward()
    gathers[1].wait_half()

    def head(b):
        these = gathered(trans, b)
        t_top = tmax[lines(b), :1]

        def one(v, carry):
            s_max, s_sum, t_sum, cross = carry
            logits = (
                jnp.dot(these, table_ref[:, columns(v)], preferred_element_type=full)
                + vbias_ref[:, columns(v)]
            ) / TEMPER
            student[lines(b), columns(v)] = logits
            teach = teach_ref[lines(b), columns(v)].astype(full) / TEMPER
            top = jnp.maximum(s_max, jnp.max(logits, 1, keepdims=True))
            s_sum = s_sum * jnp.exp(s_max - top) + jnp.sum(
                jnp.exp(logits - top), 1, keepdims=True
            )
            t_exp = jnp.exp(teach - t_top)
            t_sum = t_sum + jnp.sum(t_exp, 1, keepdims=True)
            cross = cross + jnp.sum(t_exp * (teach - logits), 1, keepdims=True)
            return top, s_sum, t_sum, cross

        zero = jnp.zeros((block, 1), full)
        s_max, s_sum, t_sum, cross = lax.fori_loop(
            0, tiles, one, (jnp.full((block, 1), -1e30, full), zero, zero, zero)
        )
        lane = lax.broadcasted_iota(jnp.int32, (block, 128), 1)
        packed = jnp.where(lane == 0, s_max, unit_ref[2:3, 0:1])
        for k, item in ((1, s_sum), (2, t_top), (3, t_sum), (4, cross)):
            packed = jnp.where(lane == k, item, packed)
        statc[lines(b), :] = packed

    loop(own_blocks, head)
    gathers[1].wait_rest()
    loop(far_blocks, head)
    stats[me] = jnp.swapaxes(statc[...], 0, 1)[:8]

    def stat_copy(peer, slot):
        return pltpu.make_async_remote_copy(
            src_ref=stats.at[me],
            dst_ref=stats.at[slot],
            send_sem=stat_send.at[peer],
            recv_sem=stat_recv.at[slot],
            device_id={"unit": peer},
            device_id_type=MESH,
        )

    def stat_wait(j):
        peer = lax.rem(me + j, n)
        stat_copy(peer, me).wait_send()
        stat_copy(peer, peer).wait_recv()

    loop((1, n), lambda j: stat_copy(lax.rem(me + j, n), me).start())
    gathers[1].finish()
    loop((1, n), stat_wait)
    s_top, t_top = stats[0, 0:1], stats[0, 2:3]
    for k in range(1, n):
        s_top = jnp.maximum(s_top, stats[k, 0:1])
        t_top = jnp.maximum(t_top, stats[k, 2:3])
    s_all = t_all = cross_all = jnp.zeros_like(s_top)
    unit_all = jnp.zeros((1, 1), full)
    for k in range(n):
        s_all = s_all + stats[k, 1:2] * jnp.exp(stats[k, 0:1] - s_top)
        scale = jnp.exp(stats[k, 2:3] - t_top)
        t_all = t_all + stats[k, 3:4] * scale
        cross_all = cross_all + stats[k, 4:5] * scale
        unit_all = unit_all + stats[k, 5:6, 0:1]
    lse_student = s_top + jnp.log(s_all)
    lse_teach = t_top + jnp.log(t_all)
    kl_rows = cross_all / t_all - lse_teach + lse_student
    place = lax.broadcasted_iota(jnp.int32, kl_rows.shape, 1)
    is_own = jnp.logical_and(place >= me * count, place < (me + 1) * count)
    kl_own = jnp.sum(jnp.where(is_own, kl_rows, 0.0), 1, keepdims=True)
    line = lax.broadcasted_iota(jnp.int32, (8, 128), 0)
    stat_out[...] = jnp.where(line == 0, kl_own, unit_all)
    both = jnp.where(
        lax.broadcasted_iota(jnp.int32, (8, n * count), 0) == 0, lse_student, lse_teach
    )
    statc[:, :8] = jnp.swapaxes(both, 0, 1)

    gvbias[...] = jnp.zeros_like(gvbias)

    def head_back(b):
        acc[...] = jnp.zeros_like(acc)
        from_student, from_teach = statc[lines(b), 0:1], statc[lines(b), 1:2]

        def one(v):
            teach = teach_ref[lines(b), columns(v)].astype(full) / TEMPER
            grad = (
                TEMPER
                / npos
                * (
                    jnp.exp(student[lines(b), columns(v)] - from_student)
                    - jnp.exp(teach - from_teach)
                )
            )
            gvbias[:, columns(v)] += row_sum(grad)
            grad_low = grad.astype(low)
            glow[lines(b), columns(v)] = grad_low
            acc[...] += lax.dot_general(
                grad_low,
                table_ref[:, columns(v)],
                (((1,), (1,)), ((), ())),
                preferred_element_type=full,
            )

        loop((0, tiles), one)
        put_part(b, acc[...])

    loop(far_blocks, head_back)
    reduces[1].start(0)
    loop(own_blocks, head_back)
    reduces[1].start(1)
    reduces[1].middle()

    def table_back(v):
        gtable[:, columns(v)] = lax.dot_general(
            trans[...].reshape(n * count, width),
            glow[:, columns(v)],
            (((0,), (0,)), ((), ())),
            preferred_element_type=full,
        ).astype(low)

    loop((0, tiles // 2), table_back)
    grad_trans = reduces[1].finish()
    grad_tgelu, grad_hgain, grad_hshift = norm_back(trans_gelu, vec(11), vec(12), grad_trans)
    grad_tpre = gelu_back(trans_pre, grad_tgelu)
    grad_tpre_low = grad_tpre.astype(low)
    grad_final = lax.dot_general(
        grad_tpre_low, wt_ref[...], (((1,), (1,)), ((), ())), preferred_element_type=full
    )
    grad_final_in, grad_gain2, grad_shift2 = norm_back(final_in, vec(8), vec(9), grad_final)
    grad_fres = grad_final_in * vec(14)
    backs[me] = grad_fres.astype(low)
    gathers[2].start()
    gvecs[0:7, :] = jnp.zeros((7, width), full)
    gvecs[7:8, :] = row_sum(grad_fres)
    gvecs[8:9, :] = grad_gain2
    gvecs[9:10, :] = grad_shift2
    gvecs[10:11, :] = row_sum(grad_tpre)
    gvecs[11:12, :] = grad_hgain
    gvecs[12:13, :] = grad_hshift
    gvecs[13:14, :] = row_sum(grad_final_in * ffn_res)
    gvecs[14:16, :] = jnp.zeros((2, width), full)
    gwt[...] = contract_rows(picked, grad_tpre_low).astype(low)
    gathers[2].forward()
    gathers[2].wait_half()
    gunit[...] = jnp.zeros_like(gunit)

    def up_down_back(b):
        grad_hidden = jnp.dot(gathered(backs, b), down_ref[...], preferred_element_type=full)
        pre = hpre[lines(b), :]
        gunit[1:2, :] += row_sum(grad_hidden * jax.nn.gelu(pre))
        grad_pre = gelu_back(pre, grad_hidden * unit_ref[1:2, :])
        gunit[0:1, :] += row_sum(grad_pre)
        grad_pre_low = grad_pre.astype(low)
        ghp[lines(b), :] = grad_pre_low
        put_part(
            b,
            lax.dot_general(
                grad_pre_low, up_ref[...], (((1,), (1,)), ((), ())), preferred_element_type=full
            ),
        )

    loop(own_blocks, up_down_back)
    reduces[2].start(1)
    loop((tiles // 2, tiles), table_back)
    gathers[2].wait_rest()
    loop(far_blocks, up_down_back)
    reduces[2].start(0)
    gup[...] = contract_rows(rows[...].reshape(n * count, width), ghp[...]).astype(low)
    reduces[2].middle()
    gdown[...] = contract_rows(backs[...].reshape(n * count, width), hid[...]).astype(low)
    gmid[...] = grad_final_in + reduces[2].finish()
    gathers[2].finish()


def mid_step(
    middle, up_w, down_w, unit_rows, table, vbias, teach, w_trans, vec_rows, n, npos, collective
):
    count, width = middle.shape
    vocab, units = table.shape[1], up_w.shape[1]
    low, full = jnp.bfloat16, jnp.float32
    rows = n * count
    inner = n // 2
    blocks = pltpu.VMEM((n, count, width), low)
    one = pltpu.VMEM((count, width), low)
    return pl.pallas_call(
        functools.partial(mid_kernel, n, npos),
        out_shape=(
            jax.ShapeDtypeStruct((width, vocab), low),
            jax.ShapeDtypeStruct((1, vocab), full),
            jax.ShapeDtypeStruct((width, units), low),
            jax.ShapeDtypeStruct((width, units), low),
            jax.ShapeDtypeStruct((8, units), full),
            jax.ShapeDtypeStruct((width, width), low),
            jax.ShapeDtypeStruct((count, width), full),
            jax.ShapeDtypeStruct((16, width), full),
            jax.ShapeDtypeStruct((8, 128), full),
        ),
        in_specs=[on_chip()] * 9,
        out_specs=(on_chip(),) * 9,
        scratch_shapes=[
            blocks,
            blocks,
            blocks,
            pltpu.VMEM((rows, units), full),
            pltpu.VMEM((rows, units), low),
            pltpu.VMEM((rows, units), low),
            pltpu.VMEM((rows, vocab), full),
            pltpu.VMEM((rows, vocab), low),
            pltpu.VMEM((max(256, count), width), full),
            pltpu.VMEM((rows, 128), full),
            pltpu.VMEM((rows, 128), full),
            pltpu.VMEM((n, 8, rows), full),
            blocks,
            one,
            *[pltpu.VMEM((2, inner - 1, count, width), low)] * 3,
            *[one] * 3,
            pltpu.SemaphoreType.DMA((3, 2, inner)),
            pltpu.SemaphoreType.DMA((3, n)),
            pltpu.SemaphoreType.DMA((3, 2, inner)),
            pltpu.SemaphoreType.DMA((3, 2, inner)),
            pltpu.SemaphoreType.DMA((n,)),
            pltpu.SemaphoreType.DMA((n,)),
        ],
        compiler_params=call_params(collective),
    )(middle, up_w, down_w, unit_rows, table, vbias, teach, w_trans, vec_rows)


def adamw(weight, first, second, grad, rate, count):
    first = BETA_ONE * first + (1.0 - BETA_ONE) * grad
    second = BETA_TWO * second + (1.0 - BETA_TWO) * grad * grad
    first_hat = first / (1.0 - BETA_ONE**count)
    second_hat = second / (1.0 - BETA_TWO**count)
    return weight - rate * (first_hat / (jnp.sqrt(second_hat) + ADAM_EPS) + DECAY * weight)


def on_device(
    token_ids,
    segments,
    positions,
    teacher,
    gate_noise,
    unit_noise,
    multipliers,
    step_count,
    layer_mats,
    mats_first,
    mats_second,
    layer_vecs,
    vecs_first,
    vecs_second,
    ffn_mats,
    ffn_first,
    ffn_second,
    unit_vecs,
    unit_first,
    unit_second,
    word_table,
    table_first,
    table_second,
    word_bias,
    bias_first,
    bias_second,
    mask_logits,
    mask_first,
    mask_second,
):
    low_type = jnp.bfloat16
    full_type = jnp.float32
    exact = lax.Precision.HIGHEST
    units_n = lax.axis_size("unit")
    groups_n = lax.axis_size("dp")
    everyone = ("unit", "dp")
    heads = mask_logits.shape[0] - 2
    share_rows = layer_mats.shape[0]
    width = share_rows * units_n * groups_n
    head_size = width // heads
    seq_len = segments.shape[2]
    nmask = positions.shape[2]
    unit_idx = lax.axis_index("unit")
    n_vecs = layer_vecs.shape[0]
    vec_pad = -n_vecs % 128
    vocab_slice = word_table.shape[0]
    table_part = word_table.shape[1]
    cap = 16 * -(-5 * seq_len // (4 * 16 * units_n))

    mats_low = layer_mats.astype(low_type)
    trans_end = 5 * width
    table_low = word_table.astype(low_type)
    map_parts = [mats_low[:, k * width : (k + 1) * width] for k in range(5)] + [
        jnp.concatenate(
            [
                mats_low[:, trans_end:],
                jnp.pad(layer_vecs.T, ((0, 0), (0, vec_pad))).astype(low_type),
            ],
            1,
        )
    ]
    small_len = unit_vecs.size + word_bias.size
    ffn_cols = ffn_mats.shape[2]
    small_rows = -(-small_len // (16 * ffn_cols)) * 16
    ffn_rows = ffn_mats.shape[1]
    slice_pack = jnp.concatenate(
        [
            ffn_mats.reshape(2 * ffn_rows, ffn_cols),
            jnp.pad(
                jnp.concatenate([unit_vecs.reshape(-1), word_bias]),
                (0, small_rows * ffn_cols - small_len),
            ).reshape(small_rows, ffn_cols),
        ],
        0,
    ).astype(low_type)
    ids = lax.dynamic_index_in_dim(token_ids[0], unit_idx, 0, keepdims=False)
    place = jnp.arange(seq_len, dtype=jnp.int32)
    same_id = ids[:, None] == ids[None, :]
    first_place = jnp.min(jnp.where(same_id, place[None, :], seq_len), 1)
    is_first = first_place == place
    owner = ids // vocab_slice
    slot = jnp.sum(
        (
            is_first[None, :]
            & (owner[None, :] == owner[:, None])
            & (place[None, :] < first_place[:, None])
        ).astype(jnp.int32),
        1,
    )
    slots_used = jnp.max(slot) + 1
    local_id = ids - owner * vocab_slice
    entry = jnp.arange(units_n * cap, dtype=jnp.int32)

    def round_match(k):
        here = slot - k * cap
        code = jnp.where((here >= 0) & (here < cap), owner * cap + here, -1)
        return entry[:, None] == code[None, :]

    def round_wanted(match):
        return jnp.max(
            jnp.where(match & is_first[None, :], local_id[None, :], -1), 1
        ).reshape(units_n, cap)

    match_0 = round_match(0)
    wanted_0 = jnp.concatenate(
        [
            round_wanted(match_0),
            jnp.broadcast_to(slots_used, (units_n, 128 - cap)),
        ],
        1,
    )[:, None, :]
    fetched, asked, *maps = fetch_rows(
        wanted_0, table_low, map_parts, units_n, groups_n, cap, 1
    )
    w_q, w_k, w_v, w_out, w_trans, pos_vecs = [part.reshape(width, -1) for part in maps]
    asked = asked[:, 0, :]
    slice_all = lax.all_gather(slice_pack, "dp", axis=0)
    asked, table_send = lax.optimization_barrier((asked, table_low.T))
    table_cols = lax.all_gather(table_send, "dp", axis=0, tiled=True)
    rounds = (jnp.max(asked[:, cap:]) + cap - 1) // cap
    match_0 = match_0.astype(low_type)

    def spread(match, parts):
        return jnp.concatenate(
            [
                contract_rows(match, parts[d].reshape(units_n * cap, table_part))
                for d in range(groups_n)
            ],
            1,
        )

    def round_asked(match):
        wanted_all = lax.all_gather(round_wanted(match), everyone, axis=0)
        return lax.dynamic_index_in_dim(wanted_all, unit_idx, 1, keepdims=False)

    def more_words(k, words):
        match = round_match(k)
        mine = round_asked(match)
        found = jnp.where(
            (mine >= 0)[:, :, None], jnp.take(table_low, jnp.maximum(mine, 0), axis=0), 0
        )
        found = lax.all_to_all(found, everyone, 0, 0, tiled=True)
        found = jnp.swapaxes(
            found.reshape(units_n, groups_n, cap, table_part), 0, 1
        )
        return words + spread(match.astype(low_type), found)

    word = lax.fori_loop(1, rounds, more_words, spread(match_0, fetched))

    vecs_f = pos_vecs[:, seq_len : seq_len + n_vecs].T.astype(full_type)
    masks_r = rounded(mask_logits)
    hid_logit = vecs_f[13]
    noise_hid = gate_noise[:width]
    noise_head = gate_noise[width : width + heads]
    zhid = gate(hid_logit, noise_hid)
    zhead = gate(masks_r[:heads], noise_head)
    zmha = gate(masks_r[heads], gate_noise[width + heads])
    zmlp = gate(masks_r[heads + 1], gate_noise[width + heads + 1])
    pos_table = pos_vecs[:, :seq_len].T.astype(full_type)
    embed = word + pos_table
    start_norm = layer_norm(embed, vecs_f[0], vecs_f[1])
    start = start_norm * zhid
    start_low = start.astype(low_type)

    picks = positions.reshape(-1)
    pick_low = (picks[:, None] == place[None, :]).astype(low_type)
    pick_full = pick_low.astype(full_type)
    start_p = jnp.dot(pick_full, start, precision=exact, preferred_element_type=full_type)
    start_p_low = start_p.astype(low_type)
    seg = segments.reshape(-1)
    seg_p = jnp.sum(jnp.where(picks[:, None] == place[None, :], seg[None, :], 0), 1)
    same = seg_p[:, None] == seg[None, :]
    queries = (
        jnp.dot(start_p_low, w_q, preferred_element_type=full_type) + vecs_f[2]
    ).astype(low_type)
    keys_b = jnp.dot(start_low, w_k, preferred_element_type=full_type).astype(low_type)
    values_b = (
        jnp.dot(start_low, w_v, preferred_element_type=full_type) + vecs_f[3]
    ).astype(low_type)
    scale = head_size ** (-0.5)
    q3 = queries.reshape(nmask, heads, head_size)
    k3 = keys_b.reshape(seq_len, heads, head_size)
    v3 = values_b.reshape(seq_len, heads, head_size)
    scores = jnp.einsum("qhd,khd->hqk", q3, k3, preferred_element_type=full_type) * scale
    probs = jax.nn.softmax(jnp.where(same[None], scores, -1000000000.0), axis=-1)
    probs_low = probs.astype(low_type)
    context = jnp.einsum(
        "hqk,khd->qhd", probs_low, v3, preferred_element_type=full_type
    ).reshape(nmask, width)
    context_r = context
    zcols = jnp.repeat(zhead, head_size)
    scaled = (context_r * zcols).astype(low_type)
    attn_res = jnp.dot(scaled, w_out, preferred_element_type=full_type) + vecs_f[4]
    middle_in = start_p + attn_res * zmha * zhid
    middle = layer_norm(middle_in, vecs_f[5], vecs_f[6])
    up_w = slice_all[:, :ffn_rows].reshape(width, ffn_cols)
    down_w = slice_all[:, ffn_rows : 2 * ffn_rows].reshape(width, ffn_cols)
    small = slice_all[:, 2 * ffn_rows :].reshape(groups_n, -1)
    unit_group = jnp.swapaxes(
        small[:, : unit_vecs.size].reshape(groups_n, 2, unit_vecs.shape[1]), 0, 1
    ).reshape(2, -1)
    bias_group = small[:, unit_vecs.size : small_len].reshape(-1).astype(full_type)
    unit_bias = unit_group[0].astype(full_type)
    unit_logit = unit_group[1].astype(full_type)
    slice_units = unit_bias.shape[0]
    ffn_width = slice_units * units_n
    noise_units = lax.dynamic_slice_in_dim(unit_noise, unit_idx * slice_units, slice_units, 0)
    zunit = gate(unit_logit, noise_units)
    npos = groups_n * units_n * nmask
    (
        grad_table,
        grad_bias,
        grad_up,
        grad_down,
        grad_units,
        grad_wtrans,
        grad_middle,
        mid_vecs,
        mid_stats,
    ) = mid_step(
        middle,
        up_w,
        down_w,
        jnp.concatenate(
            [
                unit_bias[None],
                zunit[None],
                jnp.full((6, slice_units), jnp.sum(keep_score(unit_logit))),
            ],
            0,
        ),
        table_cols,
        bias_group[None],
        teacher.reshape(-1, vocab_slice),
        w_trans,
        jnp.concatenate([vecs_f, (zmlp * zhid)[None], zhid[None]], 0),
        units_n,
        npos,
        2,
    )
    share_head = lax.psum_scatter(grad_table, "dp", scatter_dimension=0, tiled=True)
    kl_own = mid_stats[0, 0]
    unit_score = mid_stats[1, 0]
    grad_bias = grad_bias[0]

    hid_sum = jnp.sum(keep_score(hid_logit))
    head_scores = keep_score(masks_r[:heads])
    mha_score = keep_score(masks_r[heads])
    mlp_score = keep_score(masks_r[heads + 1])
    head_sum = jnp.sum(head_scores) * mha_score
    unit_sum = unit_score * mlp_score
    full_size = 4.0 * width * width + 2.0 * width * ffn_width
    kept = (4.0 * head_size * hid_sum * head_sum + 2.0 * hid_sum * unit_sum) / full_size
    sparsity = 1.0 - kept
    lagrange = multipliers[0] * (sparsity - TARGET) + multipliers[1] * (sparsity - TARGET) ** 2
    lag_slope = -(multipliers[0] + 2.0 * multipliers[1] * (sparsity - TARGET))
    grad_dbias, grad_gain2, grad_shift2, grad_tbias, grad_hgain, grad_hshift, mid_gate = [
        mid_vecs[k] for k in range(7, 14)
    ]
    grad_zmlp = jnp.sum(mid_gate * zhid)
    grad_zhid = mid_gate * zmlp
    grad_ubias = grad_units[0]
    grad_ulogit = gate_back(unit_logit, noise_units, grad_units[1])
    small_grads = jnp.concatenate(
        [
            jnp.swapaxes(
                jnp.stack([grad_ubias, grad_ulogit]).reshape(2, groups_n, -1), 0, 1
            ).reshape(groups_n, -1),
            grad_bias.reshape(groups_n, -1),
        ],
        1,
    )
    slice_grads = jnp.concatenate(
        [
            grad_up.astype(low_type).reshape(groups_n, ffn_rows, ffn_cols),
            grad_down.astype(low_type).reshape(groups_n, ffn_rows, ffn_cols),
            jnp.pad(small_grads, ((0, 0), (0, small_rows * ffn_cols - small_len)))
            .astype(low_type)
            .reshape(groups_n, small_rows, ffn_cols),
        ],
        1,
    )
    share_head, slice_grads = lax.optimization_barrier((share_head, slice_grads))
    share_slice = lax.psum_scatter(slice_grads, "dp", scatter_dimension=0, tiled=False).astype(
        full_type
    )

    grad_middle_in, grad_gain1, grad_shift1 = norm_back(
        middle_in, vecs_f[5], vecs_f[6], grad_middle
    )
    grad_ares = grad_middle_in * zmha * zhid
    grad_obias = jnp.sum(grad_ares, 0)
    grad_zmha = jnp.sum(grad_middle_in * attn_res * zhid)
    grad_zhid = grad_zhid + jnp.sum(grad_middle_in * attn_res * zmha, 0)
    grad_ares_low = grad_ares.astype(low_type)
    grad_wout = contract_rows(scaled, grad_ares_low)
    grad_scaled = jnp.dot(grad_ares_low, w_out.T, preferred_element_type=full_type)
    grad_zhead = jnp.sum((grad_scaled * context_r).reshape(nmask, heads, head_size), axis=(0, 2))
    g3 = (grad_scaled * zcols).astype(low_type).reshape(nmask, heads, head_size)
    grad_probs = jnp.einsum("qhd,khd->hqk", g3, v3, preferred_element_type=full_type)
    grad_scores = (probs * (grad_probs - jnp.sum(grad_probs * probs, -1, keepdims=True))).astype(
        low_type
    )
    grad_q = (
        jnp.einsum("hqk,khd->qhd", grad_scores, k3, preferred_element_type=full_type) * scale
    ).reshape(nmask, width)
    grad_k = (
        jnp.einsum("hqk,qhd->khd", grad_scores, q3, preferred_element_type=full_type) * scale
    ).reshape(seq_len, width)
    grad_v = jnp.einsum("hqk,qhd->khd", probs_low, g3, preferred_element_type=full_type).reshape(
        seq_len, width
    )
    grad_q_low = grad_q.astype(low_type)
    grad_k_low = grad_k.astype(low_type)
    grad_v_low = grad_v.astype(low_type)
    grad_qbias = jnp.sum(grad_q_low.astype(full_type), 0)
    grad_vbias = jnp.sum(grad_v_low.astype(full_type), 0)
    grad_wq = contract_rows(start_p_low, grad_q_low)
    grad_wk = contract_rows(start_low, grad_k_low)
    grad_wv = contract_rows(start_low, grad_v_low)
    grad_start_p = grad_middle_in + jnp.dot(grad_q_low, w_q.T, preferred_element_type=full_type)
    grad_start = (
        lax.dot_general(
            pick_full,
            grad_start_p,
            (((0,), (0,)), ((), ())),
            precision=exact,
            preferred_element_type=full_type,
        )
        + jnp.dot(grad_k_low, w_k.T, preferred_element_type=full_type)
        + jnp.dot(grad_v_low, w_v.T, preferred_element_type=full_type)
    )
    grad_zhid = grad_zhid + jnp.sum(grad_start * start_norm, 0)
    grad_embed, grad_gain0, grad_shift0 = norm_back(embed, vecs_f[0], vecs_f[1], grad_start * zhid)
    grad_hid = gate_back(hid_logit, noise_hid, grad_zhid)
    grad_vecs = jnp.stack(
        [
            grad_gain0,
            grad_shift0,
            grad_qbias,
            grad_vbias,
            grad_obias,
            grad_gain1,
            grad_shift1,
            grad_dbias,
            grad_gain2,
            grad_shift2,
            grad_tbias,
            grad_hgain,
            grad_hshift,
            grad_hid,
        ]
    )
    embed_low = grad_embed.astype(low_type)

    def word_parts(match):
        return jnp.stack(
            [
                jnp.dot(
                    match,
                    embed_low[:, d * table_part : (d + 1) * table_part],
                    preferred_element_type=full_type,
                )
                .astype(low_type)
                .reshape(units_n, cap, table_part)
                for d in range(groups_n)
            ]
        )

    map_grads = [
        item.astype(low_type)
        for item in (
            grad_wq,
            grad_wk,
            grad_wv,
            grad_wout,
            grad_wtrans,
            jnp.concatenate(
                [grad_embed.T, jnp.pad(grad_vecs.T, ((0, 0), (0, vec_pad)))],
                1,
            ),
        )
    ]
    share_table, *shares = return_rows(
        word_parts(match_0),
        asked[:, :cap].reshape(1, -1),
        share_head.T,
        map_grads,
        units_n,
        groups_n,
        9,
    )

    def more_grads(k, total):
        match = round_match(k)
        mine = round_asked(match).reshape(-1)
        back = jnp.swapaxes(word_parts(match.astype(low_type)), 0, 1).reshape(
            units_n * groups_n, cap, table_part
        )
        back = lax.all_to_all(back, everyone, 0, 0, tiled=True).reshape(-1, table_part)
        target = jnp.where(mine >= 0, mine, vocab_slice)
        return total.at[target].add(back.astype(full_type), mode="drop")

    share_table = lax.fori_loop(1, rounds, more_grads, share_table)

    grad_head = gate_back(masks_r[:heads], noise_head, grad_zhead)
    grad_mha = gate_back(masks_r[heads], gate_noise[width + heads], grad_zmha)
    grad_mlp = gate_back(masks_r[heads + 1], gate_noise[width + heads + 1], grad_zmlp)
    share_mats = jnp.concatenate([*shares[:5], shares[5][:, :seq_len]], 1)
    share_vecs = shares[5][:, seq_len : seq_len + n_vecs].T
    share_ffn = share_slice[: 2 * ffn_rows].reshape(2, ffn_rows, ffn_cols)
    share_small = share_slice[2 * ffn_rows :].reshape(-1)
    share_unit = share_small[: unit_vecs.size].reshape(unit_vecs.shape)
    share_bias = share_small[unit_vecs.size : small_len]
    own_hid = rounded(layer_vecs[13])
    own_unit = rounded(unit_vecs[1])
    lag_hid = (
        lag_slope * (4.0 * head_size * head_sum + 2.0 * unit_sum) / full_size * score_slope(own_hid)
    )
    share_vecs = share_vecs.at[13].add(lag_hid)
    lag_unit = lag_slope * 2.0 * hid_sum * mlp_score / full_size * score_slope(own_unit)
    share_unit = share_unit.at[1].add(lag_unit)
    lag_head = (
        lag_slope * 4.0 * head_size * hid_sum * mha_score / full_size * score_slope(masks_r[:heads])
    )
    lag_mha = (
        lag_slope
        * 4.0
        * head_size
        * hid_sum
        * jnp.sum(head_scores)
        / full_size
        * score_slope(masks_r[heads])
    )
    lag_mlp = lag_slope * 2.0 * hid_sum * unit_score / full_size * score_slope(masks_r[heads + 1])
    lag_masks = jnp.concatenate([lag_head, lag_mha[None], lag_mlp[None]])
    square_part = sum(
        (
            jnp.sum(item * item)
            for item in (share_mats, share_vecs, share_ffn, share_unit, share_table, share_bias)
        )
    )
    mine = jnp.concatenate(
        [grad_head, grad_mha[None], grad_mlp[None], kl_own[None], square_part[None]]
    )
    n_masks = heads + 2
    totals = total_all(
        jnp.pad(mine, (0, 1024 - mine.shape[0])).reshape(8, 128), units_n, groups_n, 10
    )[0]
    share_masks = totals[:n_masks] + lag_masks
    grad_norm = jnp.sqrt(totals[n_masks + 1] + jnp.sum(share_masks * share_masks))
    loss = TEMPER * TEMPER * totals[n_masks] / npos + lagrange
    coef = jnp.minimum(1.0, MAX_NORM / (grad_norm + 1e-06))
    count = step_count[0].astype(full_type)
    mats_grad = share_mats * coef
    vecs_grad = share_vecs * coef
    ffn_grad = share_ffn * coef
    unit_grad = share_unit * coef
    table_grad = share_table * coef
    bias_grad = share_bias * coef
    mask_grad = share_masks * coef
    mats_new = adamw(layer_mats, mats_first, mats_second, mats_grad, RATE_MATS, count)
    vecs_new = adamw(layer_vecs, vecs_first, vecs_second, vecs_grad, RATE_VECS, count)
    ffn_new = adamw(ffn_mats, ffn_first, ffn_second, ffn_grad, RATE_MATS, count)
    unit_new = adamw(unit_vecs, unit_first, unit_second, unit_grad, RATE_VECS, count)
    table_new = adamw(word_table, table_first, table_second, table_grad, RATE_TABLE, count)
    bias_new = adamw(word_bias, bias_first, bias_second, bias_grad, RATE_VECS, count)
    mask_new = adamw(mask_logits, mask_first, mask_second, mask_grad, RATE_VECS, count)
    return (
        loss,
        kept,
        grad_norm,
        mats_new,
        mats_grad,
        vecs_new,
        vecs_grad,
        ffn_new,
        ffn_grad,
        unit_new,
        unit_grad,
        table_new,
        table_grad,
        bias_new,
        bias_grad,
        mask_new,
        mask_grad,
    )


def solution(mesh):
    return jax.shard_map(
        on_device,
        mesh=mesh,
        in_specs=(
            P("dp", None, None),
            P("dp", "unit", None),
            P("dp", "unit", None),
            P("dp", None, None, "unit"),
            P(),
            P(),
            P(),
            P(),
            P(("unit", "dp"), None),
            P(("unit", "dp"), None),
            P(("unit", "dp"), None),
            P(None, ("unit", "dp")),
            P(None, ("unit", "dp")),
            P(None, ("unit", "dp")),
            P(None, "dp", "unit"),
            P(None, "dp", "unit"),
            P(None, "dp", "unit"),
            P(None, ("unit", "dp")),
            P(None, ("unit", "dp")),
            P(None, ("unit", "dp")),
            P("unit", "dp"),
            P("unit", "dp"),
            P("unit", "dp"),
            P(("unit", "dp")),
            P(("unit", "dp")),
            P(("unit", "dp")),
            P(),
            P(),
            P(),
        ),
        out_specs=(
            P(),
            P(),
            P(),
            P(("unit", "dp"), None),
            P(("unit", "dp"), None),
            P(None, ("unit", "dp")),
            P(None, ("unit", "dp")),
            P(None, "dp", "unit"),
            P(None, "dp", "unit"),
            P(None, ("unit", "dp")),
            P(None, ("unit", "dp")),
            P("unit", "dp"),
            P("unit", "dp"),
            P(("unit", "dp")),
            P(("unit", "dp")),
            P(),
            P(),
        ),
        check_vma=False,
    )
```

```python
import functools
import math

import jax
import jax.numpy as jnp
from jax import lax
from jax.experimental import pallas as pl
from jax.experimental.pallas import tpu as pltpu
from jax.sharding import PartitionSpec as P

EPS_NORM = 1e-12
GAMMA = -0.1
ZETA = 1.1
BETA = 2.0 / 3.0
TARGET = 0.95
TEMPER = 2.0
MAX_NORM = 0.0001
BETA_ONE = 0.9
BETA_TWO = 0.999
ADAM_EPS = 1e-08
DECAY = 0.01
RATE_MATS = 0.5
RATE_VECS = 5.0
RATE_TABLE = 1.0


def rounded(values):
    return lax.optimization_barrier(values.astype(jnp.bfloat16)).astype(jnp.float32)


def layer_norm(values, gain, shift):
    center = values - jnp.mean(values, -1, keepdims=True)
    spread = jnp.mean(center * center, -1, keepdims=True)
    return center * lax.rsqrt(spread + EPS_NORM) * gain + shift


def norm_back(values, gain, shift, grad):
    _, pull = jax.vjp(layer_norm, values, gain, shift)
    return pull(grad)


def gelu_back(values, grad):
    _, pull = jax.vjp(jax.nn.gelu, values)
    return pull(grad)[0]


def gate(logit, noise):
    soft = jax.nn.sigmoid((jnp.log(noise) - jnp.log(1.0 - noise) + logit) / BETA)
    return jnp.clip(soft * (ZETA - GAMMA) + GAMMA, 0.0, 1.0)


def gate_back(logit, noise, grad):
    _, pull = jax.vjp(gate, logit, noise)
    return pull(grad)[0]


def keep_score(logit):
    return jax.nn.sigmoid(logit - BETA * math.log(-GAMMA / ZETA))


def score_slope(logit):
    score = keep_score(logit)
    return score * (1.0 - score)


def contract_rows(left, right):
    return lax.dot_general(
        left, right, (((0,), (0,)), ((), ())), preferred_element_type=jnp.float32
    )


MESH = pl.DeviceIdType.MESH
VMEM_LIMIT = 60 * 1024 * 1024


def on_chip():
    return pl.BlockSpec(memory_space=pltpu.VMEM)


def call_params(collective):
    return pltpu.CompilerParams(
        collective_id=collective, has_side_effects=True, vmem_limit_bytes=VMEM_LIMIT
    )


def greet_unit(n, me):
    barrier = pltpu.get_barrier_semaphore()

    def step(j, carry):
        pl.semaphore_signal(
            barrier, inc=1, device_id={"unit": lax.rem(me + j, n)}, device_id_type=MESH
        )
        return carry

    lax.fori_loop(1, n, step, 0)
    pl.semaphore_wait(barrier, n - 1)


def greet_all(nu, nd, me):
    barrier = pltpu.get_barrier_semaphore()

    def step(j, carry):
        peer = lax.rem(me + j, nu * nd)
        pl.semaphore_signal(
            barrier,
            inc=1,
            device_id={"unit": peer // nd, "dp": lax.rem(peer, nd)},
            device_id_type=MESH,
        )
        return carry

    lax.fori_loop(1, nu * nd, step, 0)
    pl.semaphore_wait(barrier, nu * nd - 1)


def gather_kernel(n, x_ref, out_ref, send_sem, recv_sem):
    me = lax.axis_index("unit")
    greet_unit(n, me)

    def copy(peer, slot):
        return pltpu.make_async_remote_copy(
            src_ref=x_ref,
            dst_ref=out_ref.at[slot],
            send_sem=send_sem.at[peer],
            recv_sem=recv_sem.at[slot],
            device_id={"unit": peer},
            device_id_type=MESH,
        )

    def start(j, carry):
        copy(lax.rem(me + j, n), me).start()
        return carry

    def wait(j, carry):
        peer = lax.rem(me + j, n)
        copy(peer, me).wait_send()
        copy(peer, peer).wait_recv()
        return carry

    lax.fori_loop(1, n, start, 0)
    out_ref[me] = x_ref[...]
    lax.fori_loop(1, n, wait, 0)


def gather_unit(x, n, collective):
    return pl.pallas_call(
        functools.partial(gather_kernel, n),
        out_shape=jax.ShapeDtypeStruct((n,) + x.shape, x.dtype),
        in_specs=[on_chip()],
        out_specs=on_chip(),
        scratch_shapes=[pltpu.SemaphoreType.DMA((n,)), pltpu.SemaphoreType.DMA((n,))],
        compiler_params=call_params(collective),
    )(x)


def scatter_kernel(n, x_ref, out_ref, held, send_sem, recv_sem):
    me = lax.axis_index("unit")
    greet_unit(n, me)

    def copy(peer, slot):
        return pltpu.make_async_remote_copy(
            src_ref=x_ref.at[peer],
            dst_ref=held.at[slot],
            send_sem=send_sem.at[peer],
            recv_sem=recv_sem.at[slot],
            device_id={"unit": peer},
            device_id_type=MESH,
        )

    def start(j, carry):
        copy(lax.rem(me + j, n), me).start()
        return carry

    def wait(j, carry):
        peer = lax.rem(me + j, n)
        copy(peer, me).wait_send()
        copy(peer, peer).wait_recv()
        return carry

    lax.fori_loop(1, n, start, 0)
    held[me] = x_ref[me]
    lax.fori_loop(1, n, wait, 0)
    out_ref[...] = jnp.zeros_like(out_ref)

    def add(j, carry):
        out_ref[...] += held[j].astype(jnp.float32)
        return carry

    lax.fori_loop(0, n, add, 0)


def scatter_unit(x, n, collective):
    return pl.pallas_call(
        functools.partial(scatter_kernel, n),
        out_shape=jax.ShapeDtypeStruct(x.shape[1:], jnp.float32),
        in_specs=[on_chip()],
        out_specs=on_chip(),
        scratch_shapes=[
            pltpu.VMEM(x.shape, x.dtype),
            pltpu.SemaphoreType.DMA((n,)),
            pltpu.SemaphoreType.DMA((n,)),
        ],
        compiler_params=call_params(collective),
    )(x)


def total_kernel(nu, nd, x_ref, out_ref, held, send_sem, recv_sem):
    n = nu * nd
    me = lax.axis_index("unit") * nd + lax.axis_index("dp")
    greet_all(nu, nd, me)

    def copy(peer, slot):
        return pltpu.make_async_remote_copy(
            src_ref=x_ref,
            dst_ref=held.at[slot],
            send_sem=send_sem.at[peer],
            recv_sem=recv_sem.at[slot],
            device_id={"unit": peer // nd, "dp": lax.rem(peer, nd)},
            device_id_type=MESH,
        )

    def start(j, carry):
        copy(lax.rem(me + j, n), me).start()
        return carry

    def wait(j, carry):
        peer = lax.rem(me + j, n)
        copy(peer, me).wait_send()
        copy(peer, peer).wait_recv()
        return carry

    lax.fori_loop(1, n, start, 0)
    held[me] = x_ref[...]
    lax.fori_loop(1, n, wait, 0)
    out_ref[...] = jnp.zeros_like(out_ref)

    def add(j, carry):
        out_ref[...] += held[j]
        return carry

    lax.fori_loop(0, n, add, 0)


def total_all(x, nu, nd, collective):
    n = nu * nd
    return pl.pallas_call(
        functools.partial(total_kernel, nu, nd),
        out_shape=jax.ShapeDtypeStruct(x.shape, x.dtype),
        in_specs=[on_chip()],
        out_specs=on_chip(),
        scratch_shapes=[
            pltpu.VMEM((n,) + x.shape, x.dtype),
            pltpu.SemaphoreType.DMA((n,)),
            pltpu.SemaphoreType.DMA((n,)),
        ],
        compiler_params=call_params(collective),
    )(x)


def packed_shape(cap, part):
    return (cap + cap // 2, 128) if part == 192 and cap % 32 == 0 else (cap, part)


def lane_place(part, width, first):
    lines = lax.broadcasted_iota(jnp.int32, (part, width), 0) + first
    return jnp.where(
        lines == lax.broadcasted_iota(jnp.int32, (part, width), 1), 1.0, 0.0
    ).astype(jnp.bfloat16)


def half_place(width, first, upper):
    lines = lax.broadcasted_iota(jnp.int32, (128, width), 0)
    lanes = lax.broadcasted_iota(jnp.int32, (128, width), 1)
    low_end, shift = (64, first - 64) if upper else (0, first)
    inside = jnp.logical_and(lines >= low_end, lines < low_end + 64)
    return jnp.where(jnp.logical_and(inside, lines + shift == lanes), 1.0, 0.0).astype(
        jnp.bfloat16
    )


def product(left, right, left_dim=1, right_dim=0):
    return lax.dot_general(
        left,
        right,
        (((left_dim,), (right_dim,)), ((), ())),
        preferred_element_type=jnp.float32,
    )


def pack_rows(values, count, cap, width, first, part):
    full = product(values, lane_place(min(part, 128), width, first), 1, 1)
    if packed_shape(cap, part)[0] == cap:
        rest = []
        if part > 128:
            full = product(values, lane_place(part, width, first), 1, 1)
        return full.astype(jnp.bfloat16).reshape(count, cap, part), rest
    left = product(values, half_place(width, first + 128, False), 1, 1)
    right = product(values, half_place(width, first + 128, True), 1, 1)
    shape = (count, cap, 128)
    tail = left.reshape(shape)[:, : cap // 2] + right.reshape(shape)[:, cap // 2 :]
    return full.astype(jnp.bfloat16).reshape(shape), [tail.astype(jnp.bfloat16)]


def unpack_rows(ref, cap, width, first, part):
    count = ref.shape[0]
    if packed_shape(cap, part)[0] == cap:
        return product(ref[...].reshape(count * cap, part), lane_place(part, width, first))
    full = product(ref[:, :cap, :].reshape(count * cap, 128), lane_place(128, width, first))
    tail = ref[:, cap:, :].reshape(count * cap // 2, 128)
    shape = (count, cap // 2, width)
    both = jnp.concatenate(
        [
            product(tail, half_place(width, first + 128, False)).reshape(shape),
            product(tail, half_place(width, first + 128, True)).reshape(shape),
        ],
        1,
    )
    return full + both.reshape(count * cap, width)


def grid_of(nu, nd):
    ny = 2 if nu % 2 == 0 else 1
    nc = 2 if nd % 2 == 0 else 1
    return (nu // ny, ny, nd // nc, nc)


def grid_place(grid):
    unit, dp = lax.axis_index("unit"), lax.axis_index("dp")
    return (unit // grid[1], lax.rem(unit, grid[1]), dp // grid[3], lax.rem(dp, grid[3]))


def grid_device(grid, place):
    return {"unit": place[0] * grid[1] + place[1], "dp": place[2] * grid[3] + place[3]}


def dp_grid(grid, place):
    return (
        (1, 1, grid[2], grid[3]),
        (0, 0, place[2], place[3]),
        lambda at: {"dp": at[2] * grid[3] + at[3]},
    )


def moved(place, axis, index):
    return tuple(index if k == axis else place[k] for k in range(4))


GATHER_ORDERS = ((0, 2, 1, 3), (0, 2, 1, 3))
REDUCE_ORDERS = ((3, 2, 1, 0), (3, 1, 2, 0))
DP_ORDER = (3, 2)


class Gather:
    def __init__(self, grid, place, order, x, out, send_sem, recv_sem):
        self.grid, self.place, self.order = grid, place, order
        self.x, self.out, self.send_sem, self.recv_sem = x, out, send_sem, recv_sem

    def window(self, stage, index):
        axis = self.order[stage]
        where = []
        for k in range(4):
            if k == axis:
                where.append(pl.ds(index, 1))
            elif k in self.order[:stage]:
                where.append(pl.ds(0, self.grid[k]))
            else:
                where.append(pl.ds(self.place[k], 1))
        return self.out.at[tuple(where)]

    def copy(self, stage, hop, arriving):
        axis = self.order[stage]
        n = self.grid[axis]
        mine = self.place[axis]
        to = lax.rem(mine + hop, n)
        held = self.window(stage, lax.rem(mine + n - hop, n) if arriving else mine)
        return pltpu.make_async_remote_copy(
            src_ref=held,
            dst_ref=held,
            send_sem=self.send_sem.at[stage, hop],
            recv_sem=self.recv_sem.at[stage, hop],
            device_id=grid_device(self.grid, moved(self.place, axis, to)),
            device_id_type=MESH,
        )

    def start(self, stage):
        if stage == 0:
            self.out[self.place] = self.x[...]
        for hop in range(1, self.grid[self.order[stage]]):
            self.copy(stage, hop, False).start()

    def finish(self, stage):
        for hop in range(1, self.grid[self.order[stage]]):
            self.copy(stage, hop, False).wait_send()
            self.copy(stage, hop, True).wait_recv()


class Reduce:
    def __init__(self, grid, place, order, x, helds, sums, out, send_sem, recv_sem, device=None):
        self.grid, self.place, self.order = grid, place, order
        self.device = device or (lambda at: grid_device(grid, at))
        self.refs = (x,) + tuple(sums)
        self.helds, self.out = helds, out
        self.send_sem, self.recv_sem = send_sem, recv_sem

    def window(self, stage, index):
        axis = self.order[stage]
        where = []
        for k in range(4):
            if k == axis:
                where.append(pl.ds(index, 1))
            elif k in self.order[:stage]:
                where.append(pl.ds(0, 1))
            else:
                where.append(pl.ds(0, self.grid[k]))
        return self.refs[stage].at[tuple(where)]

    def copy(self, stage, hop):
        axis = self.order[stage]
        to = lax.rem(self.place[axis] + hop, self.grid[axis])
        return pltpu.make_async_remote_copy(
            src_ref=self.window(stage, to),
            dst_ref=self.helds[stage].at[hop - 1],
            send_sem=self.send_sem.at[stage, hop],
            recv_sem=self.recv_sem.at[stage, hop],
            device_id=self.device(moved(self.place, axis, to)),
            device_id_type=MESH,
        )

    def start(self, stage):
        for hop in range(1, self.grid[self.order[stage]]):
            self.copy(stage, hop).start()

    def finish(self, stage):
        axis = self.order[stage]
        n = self.grid[axis]
        for hop in range(1, n):
            self.copy(stage, hop).wait()
        left = [
            1 if k in self.order[: stage + 1] else self.grid[k] for k in range(4)
        ]
        last = stage == len(self.order) - 1

        def add(i, carry):
            where = []
            for k in (3, 2, 1, 0):
                where.insert(0, lax.rem(i, left[k]))
                i = i // left[k]
            own = moved(tuple(where), axis, self.place[axis])
            total = self.refs[stage][own].astype(jnp.float32)
            for hop in range(1, n):
                total = total + self.helds[stage][(hop - 1, *where)].astype(jnp.float32)
            if last:
                self.out[...] = total
            else:
                self.refs[stage + 1][tuple(where)] = total.astype(jnp.bfloat16)
            return carry

        lax.fori_loop(0, math.prod(left), add, 0)


def reduce_scratch(grid, orders, shapes):
    helds, sums = [], []
    for order, shape in zip(orders, shapes, strict=True):
        left = list(grid)
        for stage, axis in enumerate(order):
            n = left[axis]
            left[axis] = 1
            helds.append(pltpu.VMEM((max(n - 1, 1), *left, *shape), jnp.bfloat16))
            if stage < len(order) - 1:
                sums.append(pltpu.VMEM((*left, *shape), jnp.bfloat16))
    return helds, sums


def fetch_kernel(nu, nd, cap, count, *refs):
    wanted, table = refs[:2]
    parts = refs[2 : 2 + count]
    out, asked = refs[2 + count : 4 + count]
    wholes = refs[4 + count : 4 + 2 * count]
    sought, rows, send_a, recv_a, send_b, recv_b, own_sem, send_g, recv_g = refs[4 + 2 * count :]
    n = nu * nd
    grid = grid_of(nu, nd)
    place = grid_place(grid)
    gathers = [
        Gather(
            grid,
            place,
            GATHER_ORDERS[i % 2],
            parts[i],
            wholes[i],
            send_g.at[i],
            recv_g.at[i],
        )
        for i in range(count)
    ]
    my_unit = lax.axis_index("unit")
    my_dp = lax.axis_index("dp")
    me = my_unit * nd + my_dp
    vocab = table.shape[1]
    block = 1280 if vocab % 1280 == 0 else vocab
    greet_all(nu, nd, me)

    def ask(peer, slot):
        return pltpu.make_async_remote_copy(
            src_ref=wanted.at[peer // nd],
            dst_ref=asked.at[slot],
            send_sem=send_a.at[peer],
            recv_sem=recv_a.at[slot],
            device_id={"unit": peer // nd, "dp": lax.rem(peer, nd)},
            device_id_type=MESH,
        )

    def answer(unit, dp, from_unit, from_dp):
        peer = unit * nd + dp
        return pltpu.make_async_remote_copy(
            src_ref=rows.at[peer],
            dst_ref=out.at[from_dp, from_unit],
            send_sem=send_b.at[peer],
            recv_sem=recv_b.at[from_unit * nd + from_dp],
            device_id={"unit": unit, "dp": dp},
            device_id_type=MESH,
        )

    def ask_start(j, carry):
        ask(lax.rem(me + j, n), me).start()
        return carry

    def ask_wait(j, carry):
        peer = lax.rem(me + j, n)
        ask(peer, me).wait_send()
        ask(peer, peer).wait_recv()
        return carry

    lax.fori_loop(1, n, ask_start, 0)
    for gather in gathers:
        gather.start(0)
    asked[me] = wanted[my_unit]
    lax.fori_loop(1, n, ask_wait, 0)

    def one_group(g):
        dp = lax.rem(my_dp + g, nd)
        part = table.shape[0]
        total = jnp.zeros((part, nu * cap), jnp.float32)
        for start in range(0, vocab, block):
            lines = lax.broadcasted_iota(jnp.int32, (block, nu * cap), 0) + start
            hit = jnp.where(lines == sought[pl.ds(dp, 1), :], 1.0, 0.0).astype(jnp.bfloat16)
            total = total + product(table[:, start : start + block], hit)
        found = jnp.swapaxes(total, 0, 1).astype(jnp.bfloat16)
        head, tails = pack_rows(found, nu, cap, part, 0, part)
        for unit in range(nu):
            rows[unit * nd + dp, :cap] = head[unit]
            for tail in tails:
                rows[unit * nd + dp, cap:] = tail[unit]

        def send(unit, carry):
            @pl.when(jnp.logical_or(unit != my_unit, dp != my_dp))
            def _():
                answer(unit, dp, my_unit, my_dp).start()

            return carry

        lax.fori_loop(0, nu, send, 0)

    def advance(t):
        for i, gather in enumerate(gathers):
            stage = t - i // 2
            if 0 <= stage < 4:
                gather.finish(stage)
                if stage < 3:
                    gather.start(stage + 1)

    for dp in range(nd):
        sought[dp : dp + 1, :] = jnp.concatenate(
            [asked[unit * nd + dp][:, :cap] for unit in range(nu)], 1
        )
    for g in range(nd):
        one_group(g)
        advance(g)
    for t in range(nd, 4 + (count - 1) // 2):
        advance(t)
    own = pltpu.make_async_copy(rows.at[me], out.at[my_dp, my_unit], own_sem)
    own.start()
    own.wait()

    def answer_wait(j, carry):
        peer = lax.rem(me + j, n)
        unit, dp = peer // nd, lax.rem(peer, nd)
        answer(unit, dp, my_unit, my_dp).wait_send()
        answer(unit, dp, unit, dp).wait_recv()
        return carry

    lax.fori_loop(1, n, answer_wait, 0)


def fetch_rows(wanted, table, parts, nu, nd, cap, collective):
    n = nu * nd
    part, vocab = table.shape
    count = len(parts)
    grid = grid_of(nu, nd)
    reach = max(grid)
    return pl.pallas_call(
        functools.partial(fetch_kernel, nu, nd, cap, count),
        out_shape=(
            jax.ShapeDtypeStruct((nd, nu, *packed_shape(cap, part)), jnp.bfloat16),
            jax.ShapeDtypeStruct((n, 1, 128), jnp.int32),
            *(jax.ShapeDtypeStruct((*grid, *x.shape), x.dtype) for x in parts),
        ),
        in_specs=[on_chip()] * (2 + count),
        out_specs=(on_chip(),) * (2 + count),
        scratch_shapes=[
            pltpu.VMEM((nd, nu * cap), jnp.int32),
            pltpu.VMEM((n, *packed_shape(cap, part)), jnp.bfloat16),
            pltpu.SemaphoreType.DMA((n,)),
            pltpu.SemaphoreType.DMA((n,)),
            pltpu.SemaphoreType.DMA((n,)),
            pltpu.SemaphoreType.DMA((n,)),
            pltpu.SemaphoreType.DMA,
            pltpu.SemaphoreType.DMA((count, 4, reach)),
            pltpu.SemaphoreType.DMA((count, 4, reach)),
        ],
        compiler_params=call_params(collective),
    )(wanted, table, *parts)


def return_kernel(nu, nd, count, extras, *refs):
    x_ref, ids_ref, base_ref, more_ref, lag_vecs, lag_small, known_ref = refs[:7]
    n_all = count + extras
    grads = refs[7 : 7 + n_all]
    table_ref, totals_ref = refs[7 + n_all : 9 + n_all]
    shares = refs[9 + n_all : 9 + 2 * n_all]
    out_ref, rows_ref, mine_ref, held_ref = refs[9 + 2 * n_all : 13 + 2 * n_all]
    rest = refs[13 + 2 * n_all :]
    helds, sums = rest[: 4 * count], rest[4 * count : 7 * count]
    rest = rest[7 * count :]
    dp_helds, dp_sums = rest[: 2 * extras], rest[2 * extras : 3 * extras]
    send_sem, recv_sem, own_sem, send_r, recv_r, send_t, recv_t = rest[3 * extras :]
    n = nu * nd
    my_unit = lax.axis_index("unit")
    my_dp = lax.axis_index("dp")
    me = my_unit * nd + my_dp
    grid = grid_of(nu, nd)
    place = grid_place(grid)
    reduces = [
        Reduce(
            grid,
            place,
            REDUCE_ORDERS[i % 2],
            grads[i],
            helds[4 * i : 4 * i + 4],
            sums[3 * i : 3 * i + 3],
            shares[i],
            send_r.at[i],
            recv_r.at[i],
        )
        for i in range(count)
    ]
    part_grid, part_place, part_device = dp_grid(grid, place)
    part_reduces = [
        Reduce(
            part_grid,
            part_place,
            DP_ORDER,
            grads[count + i],
            dp_helds[2 * i : 2 * i + 2],
            dp_sums[i : i + 1],
            shares[count + i],
            send_r.at[count + i],
            recv_r.at[count + i],
            part_device,
        )
        for i in range(extras)
    ]
    greet_all(nu, nd, me)

    def peer_id(peer):
        return {"unit": peer // nd, "dp": lax.rem(peer, nd)}

    def copy(peer, slot):
        return pltpu.make_async_remote_copy(
            src_ref=x_ref.at[lax.rem(peer, nd), peer // nd],
            dst_ref=out_ref.at[slot],
            send_sem=send_sem.at[peer],
            recv_sem=recv_sem.at[slot],
            device_id=peer_id(peer),
            device_id_type=MESH,
        )

    def total_copy(peer, slot):
        return pltpu.make_async_remote_copy(
            src_ref=mine_ref,
            dst_ref=held_ref.at[slot],
            send_sem=send_t.at[peer],
            recv_sem=recv_t.at[slot],
            device_id=peer_id(peer),
            device_id_type=MESH,
        )

    def others(step):
        lax.fori_loop(1, n, lambda j, carry: (step(lax.rem(me + j, n)), carry)[1], 0)

    def wait(peer):
        copy(peer, me).wait_send()
        copy(peer, peer).wait_recv()

    def total_wait(peer):
        total_copy(peer, me).wait_send()
        total_copy(peer, peer).wait_recv()

    for reduce in reduces:
        reduce.start(0)
    others(lambda peer: copy(peer, me).start())
    for reduce in part_reduces:
        reduce.start(0)
    own = pltpu.make_async_copy(x_ref.at[my_dp, my_unit], out_ref.at[me], own_sem)
    own.start()
    own.wait()

    tiles, part, tile = base_ref.shape
    vocab = tiles * tile
    halves = 2 if tile % 256 == 0 else 1
    block = tile // halves

    def add_rows(b):
        first = b * block
        v, at = divmod(first, tile)
        lanes = lax.broadcasted_iota(jnp.int32, (ids_ref.shape[0], block), 1) + first
        hit = jnp.where(ids_ref[...] == lanes, 1.0, 0.0).astype(jnp.bfloat16)
        where = slice(first, first + block)
        both = (
            base_ref[v, :, at : at + block]
            + more_ref[:, where].astype(jnp.float32)
            + product(rows_ref[...], hit)
        )
        table_ref[:, where] = both
        return row_sum(both * both)

    steps = 4 + (count - 1) // 2
    blocks = vocab // block
    squares = jnp.zeros((1, block), jnp.float32)
    for t in range(steps):
        for i, reduce in enumerate(reduces):
            stage = t - i // 2
            if 0 <= stage < 4:
                reduce.finish(stage)
                if stage < 3:
                    reduce.start(stage + 1)
        if t < 2:
            for reduce in part_reduces:
                reduce.finish(t)
                if t == 0:
                    reduce.start(1)
        if t == 1:
            others(wait)
            arrived = unpack_rows(out_ref, ids_ref.shape[0] // n, part, 0, part)
            rows_ref[...] = jnp.swapaxes(arrived, 0, 1).astype(jnp.bfloat16)
        if t >= 1:
            done, left = t - 1, steps - 1
            for b in range(blocks * done // left, blocks * (done + 1) // left):
                squares = squares + add_rows(b)
    last = shares[count - 1]
    seq = last.shape[1] - 128
    last[:, seq:] += lag_vecs[...]
    shares[n_all - 1][...] += lag_small[...]
    square = jnp.sum(squares, 1, keepdims=True)
    for share in shares:
        square = square + jnp.sum(row_sum(share[...] * share[...]), 1, keepdims=True)
    lane = lax.broadcasted_iota(jnp.int32, (8, 128), 1)
    mine_ref[...] = jnp.where(lane == 127, square, known_ref[...])
    others(lambda peer: total_copy(peer, me).start())
    held_ref[me] = mine_ref[...]
    others(total_wait)
    totals_ref[...] = jnp.zeros_like(totals_ref)

    def add_total(j, carry):
        totals_ref[...] += held_ref[j]
        return carry

    lax.fori_loop(0, n, add_total, 0)


def return_rows(
    x, ids, base, more, lag_vecs, lag_small, known, grads, dp_grads, nu, nd, collective
):
    n = nu * nd
    grid = grid_of(nu, nd)
    part_grid = (1, 1, *grid[2:])
    count, extras = len(grads), len(dp_grads)
    reach = max(grid)
    shapes = [(g.shape[0] // n, g.shape[1]) for g in grads]
    dp_shapes = [(g.shape[0] // nd, g.shape[1]) for g in dp_grads]
    helds, sums = reduce_scratch(grid, [REDUCE_ORDERS[i % 2] for i in range(count)], shapes)
    dp_helds, dp_sums = reduce_scratch(part_grid, [DP_ORDER] * extras, dp_shapes)
    tiles, part, tile = base.shape
    return pl.pallas_call(
        functools.partial(return_kernel, nu, nd, count, extras),
        out_shape=(
            jax.ShapeDtypeStruct((part, tiles * tile), jnp.float32),
            jax.ShapeDtypeStruct((8, 128), jnp.float32),
            *(jax.ShapeDtypeStruct(shape, jnp.float32) for shape in shapes + dp_shapes),
        ),
        in_specs=[on_chip()] * (7 + count + extras),
        out_specs=(on_chip(),) * (2 + count + extras),
        scratch_shapes=[
            pltpu.VMEM((n,) + x.shape[2:], x.dtype),
            pltpu.VMEM((part, ids.shape[0]), x.dtype),
            pltpu.VMEM((8, 128), jnp.float32),
            pltpu.VMEM((n, 8, 128), jnp.float32),
            *helds,
            *sums,
            *dp_helds,
            *dp_sums,
            pltpu.SemaphoreType.DMA((n,)),
            pltpu.SemaphoreType.DMA((n,)),
            pltpu.SemaphoreType.DMA,
            pltpu.SemaphoreType.DMA((count + extras, 4, reach)),
            pltpu.SemaphoreType.DMA((count + extras, 4, reach)),
            pltpu.SemaphoreType.DMA((n,)),
            pltpu.SemaphoreType.DMA((n,)),
        ],
        compiler_params=call_params(collective),
    )(
        x,
        ids,
        base,
        more,
        lag_vecs,
        lag_small,
        known,
        *(g.reshape(*grid, *shape) for g, shape in zip(grads, shapes, strict=True)),
        *(g.reshape(*part_grid, *shape) for g, shape in zip(dp_grads, dp_shapes, strict=True)),
    )


def update_kernel(scalars, mats, table, *refs):
    coef, first_scale, second_scale = scalars[0:1, 0:1], scalars[1:2, 0:1], scalars[2:3, 0:1]

    def step(share, weight, first, second, rate):
        grad = share * coef
        first = BETA_ONE * first + (1.0 - BETA_ONE) * grad
        second = BETA_TWO * second + (1.0 - BETA_TWO) * grad * grad
        first_hat = first / first_scale
        second_hat = second / second_scale
        new = weight - rate * (first_hat / (jnp.sqrt(second_hat) + ADAM_EPS) + DECAY * weight)
        return grad, new

    shares = refs[: mats + 2]
    share_t, mw, mf, ms, fw, ff, fs, tw, tf, ts = refs[mats + 2 : mats + 12]
    m_new, m_grad, f_new, f_grad, t_new, t_grad = refs[mats + 12 :]
    t_grad[...], t_new[...] = step(share_t[...], tw[...], tf[...], ts[...], RATE_TABLE)

    @pl.when(pl.program_id(0) == 0)
    def _():
        first = 0
        for k in range(mats):
            length = min(shares[k].shape[1], mw.shape[1] - first)
            where = slice(first, first + length)
            m_grad[:, where], m_new[:, where] = step(
                shares[k][:, :length], mw[:, where], mf[:, where], ms[:, where], RATE_MATS
            )
            first += length

    @pl.when(pl.program_id(0) == 1)
    def _():
        for k in range(2):
            f_grad[k], f_new[k] = step(shares[mats + k][...], fw[k], ff[k], fs[k], RATE_MATS)


def update_step(scalars, map_shares, ffn_shares, share_table, mats, ffn, table):
    part, vocab = share_table.shape
    blocks = 4
    row = pl.BlockSpec((part // blocks, vocab), lambda i: (i, 0))

    def whole(x):
        zeros = (0,) * len(x.shape)
        return pl.BlockSpec(x.shape, lambda i: zeros)

    args = [scalars, *map_shares, *ffn_shares, share_table, *mats, *ffn, *table]
    specs = [whole(x) for x in args]
    for k in (len(args) - 1, len(args) - 2, len(args) - 3, len(args) - 10):
        specs[k] = row
    outs = [mats[0], mats[0], ffn[0], ffn[0], table[0], table[0]]
    return pl.pallas_call(
        lambda scal, *refs: update_kernel(scal, len(map_shares), None, *refs),
        grid=(blocks,),
        out_shape=tuple(jax.ShapeDtypeStruct(x.shape, x.dtype) for x in outs),
        in_specs=specs,
        out_specs=tuple(row if k >= 4 else whole(x) for k, x in enumerate(outs)),
        compiler_params=pltpu.CompilerParams(vmem_limit_bytes=VMEM_LIMIT),
    )(*args)


def row_sum(values):
    return jnp.sum(values, 0, keepdims=True)


class UnitGather:
    def __init__(self, n, me, buf, send_sem, recv_sem):
        self.n, self.me, self.buf = n, me, buf
        self.send_sem, self.recv_sem = send_sem, recv_sem
        self.inner = n // 2
        self.half, self.idx = me // self.inner, lax.rem(me, self.inner)
        self.mirror = (1 - self.half) * self.inner + self.idx

    def near(self, hop):
        return self.half * self.inner + lax.rem(self.idx + hop, self.inner)

    def copy(self, block, to, kind, hop):
        return pltpu.make_async_remote_copy(
            src_ref=self.buf.at[block],
            dst_ref=self.buf.at[block],
            send_sem=self.send_sem.at[kind, hop],
            recv_sem=self.recv_sem.at[block],
            device_id={"unit": to},
            device_id_type=MESH,
        )

    def hops(self, step):
        lax.fori_loop(1, self.inner, lambda hop, carry: (step(hop), carry)[1], 0)

    def start(self):
        self.copy(self.me, self.mirror, 0, 0).start()
        self.hops(lambda hop: self.copy(self.me, self.near(hop), 0, hop).start())

    def forward(self):
        self.copy(self.mirror, self.mirror, 0, 0).wait_recv()
        self.hops(lambda hop: self.copy(self.mirror, self.near(hop), 1, hop).start())

    def wait_half(self):
        self.hops(lambda hop: self.copy(self.near(hop), self.mirror, 0, 0).wait_recv())

    def wait_rest(self):
        far = (1 - self.half) * self.inner

        def step(hop):
            block = far + lax.rem(self.idx + hop, self.inner)
            self.copy(block, self.mirror, 0, 0).wait_recv()

        self.hops(step)

    def finish(self):
        self.copy(self.me, self.mirror, 0, 0).wait_send()

        def step(hop):
            self.copy(self.me, self.near(hop), 0, hop).wait_send()
            self.copy(self.mirror, self.near(hop), 1, hop).wait_send()

        self.hops(step)


class UnitReduce:
    def __init__(self, n, me, part, held, mine, other, send_sem, recv_sem):
        self.n, self.me, self.part = n, me, part
        self.held, self.mine, self.other = held, mine, other
        self.send_sem, self.recv_sem = send_sem, recv_sem
        self.inner = n // 2
        self.half, self.idx = me // self.inner, lax.rem(me, self.inner)
        self.mirror = (1 - self.half) * self.inner + self.idx

    def copy(self, kind, hop):
        index = lax.rem(self.idx + hop, self.inner)
        half = self.half if kind else 1 - self.half
        return pltpu.make_async_remote_copy(
            src_ref=self.part.at[half * self.inner + index],
            dst_ref=self.held.at[kind, hop - 1],
            send_sem=self.send_sem.at[kind, hop],
            recv_sem=self.recv_sem.at[kind, hop],
            device_id={"unit": self.half * self.inner + index},
            device_id_type=MESH,
        )

    def across(self):
        return pltpu.make_async_remote_copy(
            src_ref=self.mine,
            dst_ref=self.other,
            send_sem=self.send_sem.at[0, 0],
            recv_sem=self.recv_sem.at[0, 0],
            device_id={"unit": self.mirror},
            device_id_type=MESH,
        )

    def start(self, kind):
        def step(hop, carry):
            self.copy(kind, hop).start()
            return carry

        lax.fori_loop(1, self.inner, step, 0)

    def wait(self, kind):
        def step(hop, carry):
            self.copy(kind, hop).wait()
            return carry

        lax.fori_loop(1, self.inner, step, 0)

    def total(self, kind, block):
        result = self.part[block].astype(jnp.float32)
        for hop in range(1, self.inner):
            result = result + self.held[kind, hop - 1].astype(jnp.float32)
        return result

    def middle(self):
        self.wait(0)
        self.mine[...] = self.total(0, self.mirror).astype(jnp.bfloat16)
        self.across().start()

    def finish(self):
        self.wait(1)
        result = self.total(1, self.me)
        self.across().wait()
        return result + self.other[...].astype(jnp.float32)


def mid_kernel(n, nd, npos, *refs):
    middle_ref, up_ref, down_ref, unit_ref, table_ref, vbias_ref, teach_ref, wt_ref, vecs_ref = refs[
        :9
    ]
    share, gvbias, gup, gdown, gunit, gwt, gmid, gvecs, stat_out = refs[9:18]
    rows, backs, trans, hpre, hid, ghp, student, glow, acc, tmax, statc, stats = refs[18:30]
    part, mine, helds, others = refs[30], refs[31], refs[32:35], refs[35:38]
    gather_send, gather_recv, reduce_send, reduce_recv, stat_send, stat_recv = refs[38:44]
    gtable, dp_send, dp_recv = refs[44:47]
    dp_scratch = refs[47:]
    me = lax.axis_index("unit")
    all_grid = grid_of(n, nd)
    grid, place, device = dp_grid(all_grid, grid_place(all_grid))
    low, full = jnp.bfloat16, jnp.float32
    count, width = middle_ref.shape
    vocab = table_ref.shape[1]
    tile = 768 if vocab % 768 == 0 else vocab
    tiles = vocab // tile
    group = max(1, 256 // count)
    block = group * count
    per_half = n // 2 // group
    half = me // (n // 2)
    table_reduces = [
        Reduce(
            grid,
            place,
            DP_ORDER,
            gtable.at[v],
            dp_scratch[3 * v : 3 * v + 2],
            dp_scratch[3 * v + 2 : 3 * v + 3],
            share.at[v],
            dp_send.at[v],
            dp_recv.at[v],
            device,
        )
        for v in range(tiles)
    ]
    own_blocks = (half * per_half, (half + 1) * per_half)
    far_blocks = ((1 - half) * per_half, (2 - half) * per_half)
    greet_all(n, nd, me * nd + lax.axis_index("dp"))
    gathers = [
        UnitGather(n, me, buf, gather_send.at[i], gather_recv.at[i])
        for i, buf in enumerate((rows, trans, backs))
    ]
    reduces = [
        UnitReduce(
            n, me, part, helds[i], mine, others[i], reduce_send.at[i], reduce_recv.at[i]
        )
        for i in range(3)
    ]

    def vec(k):
        return vecs_ref[k : k + 1, :]

    def loop(span, step):
        lax.fori_loop(span[0], span[1], lambda b, carry: (step(b), carry)[1], 0)

    def lines(b):
        return pl.ds(pl.multiple_of(b * block, block), block)

    def columns(v):
        return pl.ds(pl.multiple_of(v * tile, 128), tile)

    def gathered(buf, b):
        return buf[pl.ds(b * group, group)].reshape(block, width)

    def put_part(b, values):
        part[pl.ds(b * group, group)] = values.astype(low).reshape(group, count, width)

    middle = middle_ref[...]
    rows[me] = middle.astype(low)
    gathers[0].start()

    def teacher_top(b):
        top = jnp.max(teach_ref[lines(b), :].astype(full), 1, keepdims=True) / TEMPER
        tmax[lines(b), :] = jnp.broadcast_to(top, (block, 128))

    loop((0, n // group), teacher_top)
    gathers[0].forward()
    gathers[0].wait_half()

    def up_down(b):
        pre = (
            jnp.dot(gathered(rows, b), up_ref[...], preferred_element_type=full)
            + unit_ref[0:1, :]
        )
        hpre[lines(b), :] = pre
        hidden = (jax.nn.gelu(pre) * unit_ref[1:2, :]).astype(low)
        hid[lines(b), :] = hidden
        put_part(
            b,
            lax.dot_general(
                hidden, down_ref[...], (((1,), (1,)), ((), ())), preferred_element_type=full
            ),
        )

    loop(own_blocks, up_down)
    reduces[0].start(1)
    gathers[0].wait_rest()
    loop(far_blocks, up_down)
    reduces[0].start(0)
    reduces[0].middle()
    ffn_res = reduces[0].finish() + vec(7)
    final_in = middle + ffn_res * vec(14)
    final = layer_norm(final_in, vec(8), vec(9))
    picked = final.astype(low)
    trans_pre = jnp.dot(picked, wt_ref[...], preferred_element_type=full) + vec(10)
    trans_gelu = jax.nn.gelu(trans_pre)
    trans[me] = layer_norm(trans_gelu, vec(11), vec(12)).astype(low)
    gathers[1].start()
    gathers[0].finish()
    gathers[1].forward()
    gathers[1].wait_half()

    def head(b):
        these = gathered(trans, b)
        t_top = tmax[lines(b), :1]

        def one(v, carry):
            s_max, s_sum, t_sum, cross = carry
            logits = (
                jnp.dot(these, table_ref[:, columns(v)], preferred_element_type=full)
                + vbias_ref[:, columns(v)]
            ) / TEMPER
            student[lines(b), columns(v)] = logits
            teach = teach_ref[lines(b), columns(v)].astype(full) / TEMPER
            top = jnp.maximum(s_max, jnp.max(logits, 1, keepdims=True))
            s_sum = s_sum * jnp.exp(s_max - top) + jnp.sum(
                jnp.exp(logits - top), 1, keepdims=True
            )
            t_exp = jnp.exp(teach - t_top)
            t_sum = t_sum + jnp.sum(t_exp, 1, keepdims=True)
            cross = cross + jnp.sum(t_exp * (teach - logits), 1, keepdims=True)
            return top, s_sum, t_sum, cross

        zero = jnp.zeros((block, 1), full)
        s_max, s_sum, t_sum, cross = lax.fori_loop(
            0, tiles, one, (jnp.full((block, 1), -1e30, full), zero, zero, zero)
        )
        lane = lax.broadcasted_iota(jnp.int32, (block, 128), 1)
        packed = jnp.where(lane == 0, s_max, unit_ref[2:3, 0:1])
        for k, item in ((1, s_sum), (2, t_top), (3, t_sum), (4, cross)):
            packed = jnp.where(lane == k, item, packed)
        statc[lines(b), :] = packed

    loop(own_blocks, head)
    gathers[1].wait_rest()
    loop(far_blocks, head)
    stats[me] = jnp.swapaxes(statc[...], 0, 1)[:8]

    def stat_copy(peer, slot):
        return pltpu.make_async_remote_copy(
            src_ref=stats.at[me],
            dst_ref=stats.at[slot],
            send_sem=stat_send.at[peer],
            recv_sem=stat_recv.at[slot],
            device_id={"unit": peer},
            device_id_type=MESH,
        )

    def stat_wait(j):
        peer = lax.rem(me + j, n)
        stat_copy(peer, me).wait_send()
        stat_copy(peer, peer).wait_recv()

    loop((1, n), lambda j: stat_copy(lax.rem(me + j, n), me).start())
    gathers[1].finish()
    loop((1, n), stat_wait)
    s_top, t_top = stats[0, 0:1], stats[0, 2:3]
    for k in range(1, n):
        s_top = jnp.maximum(s_top, stats[k, 0:1])
        t_top = jnp.maximum(t_top, stats[k, 2:3])
    s_all = t_all = cross_all = jnp.zeros_like(s_top)
    unit_all = jnp.zeros((1, 1), full)
    for k in range(n):
        s_all = s_all + stats[k, 1:2] * jnp.exp(stats[k, 0:1] - s_top)
        scale = jnp.exp(stats[k, 2:3] - t_top)
        t_all = t_all + stats[k, 3:4] * scale
        cross_all = cross_all + stats[k, 4:5] * scale
        unit_all = unit_all + stats[k, 5:6, 0:1]
    lse_student = s_top + jnp.log(s_all)
    lse_teach = t_top + jnp.log(t_all)
    kl_rows = cross_all / t_all - lse_teach + lse_student
    place = lax.broadcasted_iota(jnp.int32, kl_rows.shape, 1)
    is_own = jnp.logical_and(place >= me * count, place < (me + 1) * count)
    kl_own = jnp.sum(jnp.where(is_own, kl_rows, 0.0), 1, keepdims=True)
    line = lax.broadcasted_iota(jnp.int32, (8, 128), 0)
    stat_out[...] = jnp.where(line == 0, kl_own, unit_all)
    both = jnp.where(
        lax.broadcasted_iota(jnp.int32, (8, n * count), 0) == 0, lse_student, lse_teach
    )
    statc[:, :8] = jnp.swapaxes(both, 0, 1)

    gvbias[...] = jnp.zeros_like(gvbias)

    def head_back(b):
        acc[...] = jnp.zeros_like(acc)
        from_student, from_teach = statc[lines(b), 0:1], statc[lines(b), 1:2]

        def one(v):
            teach = teach_ref[lines(b), columns(v)].astype(full) / TEMPER
            grad = (
                TEMPER
                / npos
                * (
                    jnp.exp(student[lines(b), columns(v)] - from_student)
                    - jnp.exp(teach - from_teach)
                )
            )
            gvbias[:, columns(v)] += row_sum(grad)
            grad_low = grad.astype(low)
            glow[lines(b), columns(v)] = grad_low
            acc[...] += lax.dot_general(
                grad_low,
                table_ref[:, columns(v)],
                (((1,), (1,)), ((), ())),
                preferred_element_type=full,
            )

        loop((0, tiles), one)
        put_part(b, acc[...])

    loop(far_blocks, head_back)
    reduces[1].start(0)
    loop(own_blocks, head_back)
    reduces[1].start(1)
    reduces[1].middle()

    for v in range(tiles):
        gtable[v] = (
            contract_rows(
                trans[...].reshape(n * count, width), glow[:, v * tile : (v + 1) * tile]
            )
            .astype(low)
            .reshape(gtable.shape[1:])
        )
        table_reduces[v].start(0)
    grad_trans = reduces[1].finish()
    grad_tgelu, grad_hgain, grad_hshift = norm_back(trans_gelu, vec(11), vec(12), grad_trans)
    grad_tpre = gelu_back(trans_pre, grad_tgelu)
    grad_tpre_low = grad_tpre.astype(low)
    grad_final = lax.dot_general(
        grad_tpre_low, wt_ref[...], (((1,), (1,)), ((), ())), preferred_element_type=full
    )
    grad_final_in, grad_gain2, grad_shift2 = norm_back(final_in, vec(8), vec(9), grad_final)
    grad_fres = grad_final_in * vec(14)
    backs[me] = grad_fres.astype(low)
    gathers[2].start()
    gvecs[0:7, :] = jnp.zeros((7, width), full)
    gvecs[7:8, :] = row_sum(grad_fres)
    gvecs[8:9, :] = grad_gain2
    gvecs[9:10, :] = grad_shift2
    gvecs[10:11, :] = row_sum(grad_tpre)
    gvecs[11:12, :] = grad_hgain
    gvecs[12:13, :] = grad_hshift
    gvecs[13:14, :] = row_sum(grad_final_in * ffn_res)
    gvecs[14:16, :] = jnp.zeros((2, width), full)
    gwt[...] = contract_rows(picked, grad_tpre_low).astype(low)
    for table_reduce in table_reduces:
        table_reduce.finish(0)
        table_reduce.start(1)
    gathers[2].forward()
    gathers[2].wait_half()
    gunit[...] = jnp.zeros_like(gunit)

    def up_down_back(b):
        grad_hidden = jnp.dot(gathered(backs, b), down_ref[...], preferred_element_type=full)
        pre = hpre[lines(b), :]
        gunit[1:2, :] += row_sum(grad_hidden * jax.nn.gelu(pre))
        grad_pre = gelu_back(pre, grad_hidden * unit_ref[1:2, :])
        gunit[0:1, :] += row_sum(grad_pre)
        grad_pre_low = grad_pre.astype(low)
        ghp[lines(b), :] = grad_pre_low
        put_part(
            b,
            lax.dot_general(
                grad_pre_low, up_ref[...], (((1,), (1,)), ((), ())), preferred_element_type=full
            ),
        )

    loop(own_blocks, up_down_back)
    reduces[2].start(1)
    gathers[2].wait_rest()
    loop(far_blocks, up_down_back)
    reduces[2].start(0)
    gup[...] = contract_rows(rows[...].reshape(n * count, width), ghp[...]).astype(low)
    reduces[2].middle()
    gdown[...] = contract_rows(backs[...].reshape(n * count, width), hid[...]).astype(low)
    gmid[...] = grad_final_in + reduces[2].finish()
    gathers[2].finish()
    for table_reduce in table_reduces:
        table_reduce.finish(1)


def mid_step(
    middle, up_w, down_w, unit_rows, table, vbias, teach, w_trans, vec_rows, n, nd, npos, collective
):
    count, width = middle.shape
    vocab, units = table.shape[1], up_w.shape[1]
    low, full = jnp.bfloat16, jnp.float32
    rows = n * count
    inner = n // 2
    blocks = pltpu.VMEM((n, count, width), low)
    one = pltpu.VMEM((count, width), low)
    tile = 768 if vocab % 768 == 0 else vocab
    tiles = vocab // tile
    grid = (1, 1, *grid_of(n, nd)[2:])
    helds, sums = reduce_scratch(grid, [DP_ORDER] * tiles, [(width // nd, tile)] * tiles)
    dp_scratch = []
    for v in range(tiles):
        dp_scratch += [helds[2 * v], helds[2 * v + 1], sums[v]]
    return pl.pallas_call(
        functools.partial(mid_kernel, n, nd, npos),
        out_shape=(
            jax.ShapeDtypeStruct((tiles, width // nd, tile), full),
            jax.ShapeDtypeStruct((1, vocab), full),
            jax.ShapeDtypeStruct((width, units), low),
            jax.ShapeDtypeStruct((width, units), low),
            jax.ShapeDtypeStruct((8, units), full),
            jax.ShapeDtypeStruct((width, width), low),
            jax.ShapeDtypeStruct((count, width), full),
            jax.ShapeDtypeStruct((16, width), full),
            jax.ShapeDtypeStruct((8, 128), full),
        ),
        in_specs=[on_chip()] * 9,
        out_specs=(on_chip(),) * 9,
        scratch_shapes=[
            blocks,
            blocks,
            blocks,
            pltpu.VMEM((rows, units), full),
            pltpu.VMEM((rows, units), low),
            pltpu.VMEM((rows, units), low),
            pltpu.VMEM((rows, vocab), full),
            pltpu.VMEM((rows, vocab), low),
            pltpu.VMEM((max(256, count), width), full),
            pltpu.VMEM((rows, 128), full),
            pltpu.VMEM((rows, 128), full),
            pltpu.VMEM((n, 8, rows), full),
            blocks,
            one,
            *[pltpu.VMEM((2, inner - 1, count, width), low)] * 3,
            *[one] * 3,
            pltpu.SemaphoreType.DMA((3, 2, inner)),
            pltpu.SemaphoreType.DMA((3, n)),
            pltpu.SemaphoreType.DMA((3, 2, inner)),
            pltpu.SemaphoreType.DMA((3, 2, inner)),
            pltpu.SemaphoreType.DMA((n,)),
            pltpu.SemaphoreType.DMA((n,)),
            pltpu.VMEM((tiles, *grid, width // nd, tile), low),
            pltpu.SemaphoreType.DMA((tiles, 2, max(grid))),
            pltpu.SemaphoreType.DMA((tiles, 2, max(grid))),
            *dp_scratch,
        ],
        compiler_params=call_params(collective),
    )(middle, up_w, down_w, unit_rows, table, vbias, teach, w_trans, vec_rows)


def split_low(values):
    parts = []
    for _ in range(3):
        part = values.astype(jnp.bfloat16)
        parts.append(part)
        values = values - part.astype(jnp.float32)
    return parts


def picked_lines(pos_ref, seq):
    count = pos_ref.shape[0]
    return pos_ref[...] == lax.broadcasted_iota(jnp.int32, (count, seq), 1)


def per_head(values, heads):
    rows, width = values.shape
    size = width // heads
    shape = (heads, rows, width)
    lane = lax.broadcasted_iota(jnp.int32, shape, 2) // size
    keep = lane == lax.broadcasted_iota(jnp.int32, shape, 0)
    return jnp.where(keep, jnp.broadcast_to(values[None], shape), 0.0).reshape(
        heads * rows, width
    )


def from_heads(values, heads):
    total, width = values.shape
    size = width // heads
    shape = (heads, total // heads, width)
    lane = lax.broadcasted_iota(jnp.int32, shape, 2) // size
    keep = lane == lax.broadcasted_iota(jnp.int32, shape, 0)
    return jnp.sum(jnp.where(keep, values.reshape(shape), 0.0), 0)


def attend_kernel(heads, cap, *refs):
    (
        words_ref,
        extra_ref,
        code_ref,
        pos_ref,
        seg_ref,
        noise_ref,
        gates_ref,
        pos_vecs,
        w_q,
        w_k,
        w_v,
        w_out,
    ) = refs[:12]
    middle_ref, vecs, embed_ref, start_ref, keys, values, queries, probs_ref, small = refs[12:]
    low, full = jnp.bfloat16, jnp.float32
    seq, width = embed_ref.shape
    nd, nu = words_ref.shape[:2]
    part = width // nd
    count = pos_ref.shape[0]
    n_vecs = 14
    turned = jnp.swapaxes(pos_vecs[:, seq:].astype(full), 0, 1)
    vecs[...] = turned[:16]
    zhid = gate(vecs[13:14, :], noise_ref[...])
    zmlp_hid = gates_ref[2:3, :] * zhid
    vecs[n_vecs : n_vecs + 1, :] = zmlp_hid
    vecs[n_vecs + 1 : n_vecs + 2, :] = zhid

    def vec(k):
        return vecs[k : k + 1, :]

    found = jnp.zeros((nu * cap, width), full)
    for d in range(nd):
        found = found + unpack_rows(words_ref.at[d], cap, width, d * part, part)
    spread = jnp.where(
        code_ref[...] == lax.broadcasted_iota(jnp.int32, (seq, nu * cap), 1), 1.0, 0.0
    ).astype(low)
    embed = (
        product(spread, found.astype(low))
        + extra_ref[...].astype(full)
        + jnp.swapaxes(pos_vecs[:, :seq].astype(full), 0, 1)
    )
    embed_ref[...] = embed
    start = layer_norm(embed, vec(0), vec(1)) * zhid
    start_low = start.astype(low)
    start_ref[...] = start_low
    pick_mask = picked_lines(pos_ref, seq)
    pick = jnp.where(pick_mask, 1.0, 0.0).astype(low)
    start_p = sum(product(pick, item) for item in split_low(start))
    start_p_low = start_p.astype(low)
    query = (product(start_p_low, w_q[...]) + vec(2)).astype(low)
    keys[...] = product(start_low, w_k[...]).astype(low)
    values[...] = (product(start_low, w_v[...]) + vec(3)).astype(low)
    queries[...] = query
    seg = seg_ref[...]
    seg_p = jnp.sum(jnp.where(pick_mask, seg, 0), 1, keepdims=True)
    same = jnp.broadcast_to((seg_p == seg)[None], (heads, count, seq)).reshape(
        heads * count, seq
    )
    scale = (width // heads) ** (-0.5)
    scores = (
        product(per_head(query.astype(full), heads).astype(low), keys[...], 1, 1) * scale
    )
    scores = jnp.where(same, scores, -1000000000.0)
    lifted = jnp.exp(scores - jnp.max(scores, 1, keepdims=True))
    probs = lifted / jnp.sum(lifted, 1, keepdims=True)
    probs_ref[...] = probs
    context = from_heads(product(probs.astype(low), values[...]), heads)
    scaled = (context * gates_ref[0:1, :]).astype(low)
    attn_res = product(scaled, w_out[...]) + vec(4)
    middle_in = start_p + attn_res * gates_ref[1:2, :] * zhid
    middle_ref[...] = layer_norm(middle_in, vec(5), vec(6))
    small[0] = start_p
    small[1] = context
    small[2] = attn_res
    small[3] = middle_in


def attend_step(heads, cap, words, extra, code, pos, seg, noise, gates, pos_vecs, maps):
    low, full = jnp.bfloat16, jnp.float32
    seq, width = extra.shape
    count = pos.shape[0]
    return pl.pallas_call(
        functools.partial(attend_kernel, heads, cap),
        out_shape=(
            jax.ShapeDtypeStruct((count, width), full),
            jax.ShapeDtypeStruct((16, width), full),
            jax.ShapeDtypeStruct((seq, width), full),
            jax.ShapeDtypeStruct((seq, width), low),
            jax.ShapeDtypeStruct((seq, width), low),
            jax.ShapeDtypeStruct((seq, width), low),
            jax.ShapeDtypeStruct((count, width), low),
            jax.ShapeDtypeStruct((heads * count, seq), full),
            jax.ShapeDtypeStruct((4, count, width), full),
        ),
        in_specs=[on_chip()] * 12,
        out_specs=(on_chip(),) * 9,
        compiler_params=pltpu.CompilerParams(vmem_limit_bytes=VMEM_LIMIT),
    )(words, extra, code, pos, seg, noise, gates, pos_vecs, *maps)


def attend_back_kernel(heads, nd, cap, *refs):
    (
        gmid_ref,
        mid_vecs,
        vecs,
        embed_ref,
        start_ref,
        keys,
        values,
        queries,
        probs_ref,
        small,
        code_ref,
        pos_ref,
        noise_ref,
        gates_ref,
        w_q,
        w_k,
        w_v,
        w_out,
    ) = refs[:18]
    g_q, g_k, g_v, g_out, g_last, sent, low_embed, sums, lines = refs[18:]
    low, full = jnp.bfloat16, jnp.float32
    seq, width = embed_ref.shape
    nu, part = sent.shape[1], width // nd

    def vec(k):
        return vecs[k : k + 1, :]

    zhid = vec(15)
    zcols, zmha = gates_ref[0:1, :], gates_ref[1:2, :]
    start_p, context, attn_res, middle_in = small[0], small[1], small[2], small[3]
    grad_middle_in, grad_gain1, grad_shift1 = norm_back(middle_in, vec(5), vec(6), gmid_ref[...])
    grad_ares = grad_middle_in * zmha * zhid
    grad_ares_low = grad_ares.astype(low)
    through = row_sum(grad_middle_in * attn_res)
    scaled = (context * zcols).astype(low)
    g_out[...] = contract_rows(scaled, grad_ares_low).astype(low)
    grad_scaled = product(grad_ares_low, w_out[...], 1, 1)
    sums[...] = jnp.zeros_like(sums)
    sums[0:1, :] = row_sum(grad_scaled * context)
    sums[1:2, :] = through * zhid
    sums[2:3, :] = mid_vecs[13:14, :] * zhid
    grad_context = per_head((grad_scaled * zcols).astype(low).astype(full), heads).astype(low)
    scale = (width // heads) ** (-0.5)
    probs = probs_ref[...]
    grad_probs = product(grad_context, values[...], 1, 1)
    grad_scores = (
        probs * (grad_probs - jnp.sum(grad_probs * probs, 1, keepdims=True))
    ).astype(low)
    grad_q = (from_heads(product(grad_scores, keys[...]), heads) * scale).astype(low)
    grad_k = (
        contract_rows(grad_scores, per_head(queries[...].astype(full), heads).astype(low)) * scale
    ).astype(low)
    grad_v = contract_rows(probs.astype(low), grad_context).astype(low)
    start_low = start_ref[...]
    g_q[...] = contract_rows(start_p.astype(low), grad_q).astype(low)
    g_k[...] = contract_rows(start_low, grad_k).astype(low)
    g_v[...] = contract_rows(start_low, grad_v).astype(low)
    grad_start_p = grad_middle_in + product(grad_q, w_q[...], 1, 1)
    pick = jnp.where(picked_lines(pos_ref, seq), 1.0, 0.0).astype(low)
    grad_start = (
        sum(contract_rows(pick, item) for item in split_low(grad_start_p))
        + product(grad_k, w_k[...], 1, 1)
        + product(grad_v, w_v[...], 1, 1)
    )
    embed = embed_ref[...]
    center = embed - jnp.mean(embed, 1, keepdims=True)
    unit_norm = center * lax.rsqrt(jnp.mean(center * center, 1, keepdims=True) + EPS_NORM)
    start_norm = unit_norm * vec(0) + vec(1)
    grad_zhid = (
        mid_vecs[13:14, :] * gates_ref[2:3, :]
        + through * zmha
        + row_sum(grad_start * start_norm)
    )
    grad_embed, grad_gain0, grad_shift0 = norm_back(embed, vec(0), vec(1), grad_start * zhid)
    embed_low = grad_embed.astype(low)
    low_embed[...] = embed_low
    match = jnp.where(
        code_ref[...] == lax.broadcasted_iota(jnp.int32, (nu * cap, seq), 0), 1.0, 0.0
    ).astype(low)
    gathered = product(match, embed_low).astype(low)
    for d in range(nd):
        head, tails = pack_rows(gathered, nu, cap, width, d * part, part)
        sent[d, :, :cap] = head
        for tail in tails:
            sent[d, :, cap:] = tail
    lines[...] = jnp.zeros_like(lines)
    items = (
        grad_gain0,
        grad_shift0,
        row_sum(grad_q.astype(full)),
        row_sum(grad_v.astype(full)),
        row_sum(grad_ares),
        grad_gain1,
        grad_shift1,
    )
    for k, item in enumerate(items):
        lines[k : k + 1, :] = item.reshape(1, width)
    lines[7:13, :] = mid_vecs[7:13, :]
    lines[13:14, :] = gate_back(vec(13), noise_ref[...], grad_zhid)
    g_last[:, :seq] = jnp.swapaxes(grad_embed, 0, 1).astype(low)
    g_last[:, seq:] = jnp.swapaxes(lines[...], 0, 1).astype(low)


def attend_back_step(heads, nd, nu, cap, gmid, mid_vecs, kept, code, pos, noise, gates, maps):
    low, full = jnp.bfloat16, jnp.float32
    seq, width = kept[1].shape
    square = jax.ShapeDtypeStruct((width, width), low)
    return pl.pallas_call(
        functools.partial(attend_back_kernel, heads, nd, cap),
        out_shape=(
            square,
            square,
            square,
            square,
            jax.ShapeDtypeStruct((width, seq + 128), low),
            jax.ShapeDtypeStruct((nd, nu, *packed_shape(cap, width // nd)), low),
            jax.ShapeDtypeStruct((seq, width), low),
            jax.ShapeDtypeStruct((8, width), full),
        ),
        in_specs=[on_chip()] * 18,
        out_specs=(on_chip(),) * 8,
        scratch_shapes=[pltpu.VMEM((128, width), full)],
        compiler_params=pltpu.CompilerParams(vmem_limit_bytes=VMEM_LIMIT),
    )(gmid, mid_vecs, *kept, code, pos, noise, gates, *maps)


def adamw(weight, first, second, grad, rate, count):
    first = BETA_ONE * first + (1.0 - BETA_ONE) * grad
    second = BETA_TWO * second + (1.0 - BETA_TWO) * grad * grad
    first_hat = first / (1.0 - BETA_ONE**count)
    second_hat = second / (1.0 - BETA_TWO**count)
    return weight - rate * (first_hat / (jnp.sqrt(second_hat) + ADAM_EPS) + DECAY * weight)


def on_device(
    token_ids,
    segments,
    positions,
    teacher,
    gate_noise,
    unit_noise,
    multipliers,
    step_count,
    layer_mats,
    mats_first,
    mats_second,
    layer_vecs,
    vecs_first,
    vecs_second,
    ffn_mats,
    ffn_first,
    ffn_second,
    unit_vecs,
    unit_first,
    unit_second,
    word_table,
    table_first,
    table_second,
    word_bias,
    bias_first,
    bias_second,
    mask_logits,
    mask_first,
    mask_second,
):
    low_type = jnp.bfloat16
    full_type = jnp.float32
    exact = lax.Precision.HIGHEST
    units_n = lax.axis_size("unit")
    groups_n = lax.axis_size("dp")
    everyone = ("unit", "dp")
    heads = mask_logits.shape[0] - 2
    share_rows = layer_mats.shape[0]
    width = share_rows * units_n * groups_n
    head_size = width // heads
    seq_len = segments.shape[2]
    nmask = positions.shape[2]
    unit_idx = lax.axis_index("unit")
    n_vecs = layer_vecs.shape[0]
    vec_pad = -n_vecs % 128
    table_turned = word_table.T
    vocab_slice = word_table.shape[0]
    table_part = word_table.shape[1]
    cap = 16 * -(-seq_len // (16 * units_n))

    mats_low = layer_mats.astype(low_type)
    trans_end = 5 * width
    table_low = table_turned.astype(low_type)
    map_parts = [mats_low[:, k * width : (k + 1) * width] for k in range(5)] + [
        jnp.concatenate(
            [
                mats_low[:, trans_end:],
                jnp.pad(layer_vecs.T, ((0, 0), (0, vec_pad))).astype(low_type),
            ],
            1,
        )
    ]
    small_len = unit_vecs.size + word_bias.size
    ffn_cols = ffn_mats.shape[2]
    small_rows = -(-small_len // (16 * ffn_cols)) * 16
    ffn_rows = ffn_mats.shape[1]
    slice_pack = jnp.concatenate(
        [
            ffn_mats.reshape(2 * ffn_rows, ffn_cols),
            jnp.pad(
                jnp.concatenate([unit_vecs.reshape(-1), word_bias]),
                (0, small_rows * ffn_cols - small_len),
            ).reshape(small_rows, ffn_cols),
        ],
        0,
    ).astype(low_type)
    ids = lax.dynamic_index_in_dim(token_ids[0], unit_idx, 0, keepdims=False)
    place = jnp.arange(seq_len, dtype=jnp.int32)
    same_id = ids[:, None] == ids[None, :]
    first_place = jnp.min(jnp.where(same_id, place[None, :], seq_len), 1)
    is_first = first_place == place
    owner = ids // vocab_slice
    slot = jnp.sum(
        (
            is_first[None, :]
            & (owner[None, :] == owner[:, None])
            & (place[None, :] < first_place[:, None])
        ).astype(jnp.int32),
        1,
    )
    slots_used = jnp.max(slot) + 1
    local_id = ids - owner * vocab_slice
    entry = jnp.arange(units_n * cap, dtype=jnp.int32)

    def round_code(k):
        here = slot - k * cap
        return jnp.where((here >= 0) & (here < cap), owner * cap + here, -1)

    def round_match(k):
        return entry[:, None] == round_code(k)[None, :]

    def round_wanted(match):
        return jnp.max(
            jnp.where(match & is_first[None, :], local_id[None, :], -1), 1
        ).reshape(units_n, cap)

    match_0 = round_match(0)
    wanted_0 = jnp.concatenate(
        [
            round_wanted(match_0),
            jnp.broadcast_to(slots_used, (units_n, 128 - cap)),
        ],
        1,
    )[:, None, :]
    fetched, asked, *maps = fetch_rows(
        wanted_0, table_low, map_parts, units_n, groups_n, cap, 1
    )
    w_q, w_k, w_v, w_out, w_trans, pos_vecs = [part.reshape(width, -1) for part in maps]
    asked = asked[:, 0, :]
    slice_all = lax.all_gather(slice_pack, "dp", axis=0)
    table_cols = lax.all_gather(table_low, "dp", axis=0, tiled=True)
    rounds = (jnp.max(asked[:, cap:]) + cap - 1) // cap
    code_0 = round_code(0)

    def spread(match, parts):
        return jnp.concatenate(
            [
                contract_rows(match, parts[d].reshape(units_n * cap, table_part))
                for d in range(groups_n)
            ],
            1,
        )

    def round_asked(match):
        wanted_all = lax.all_gather(round_wanted(match), everyone, axis=0)
        return lax.dynamic_index_in_dim(wanted_all, unit_idx, 1, keepdims=False)

    def more_words(k, words):
        match = round_match(k)
        mine = round_asked(match)
        found = jnp.where(
            (mine >= 0)[:, :, None],
            jnp.moveaxis(jnp.take(table_low, jnp.maximum(mine, 0), axis=1), 0, 2),
            0,
        )
        found = lax.all_to_all(found, everyone, 0, 0, tiled=True)
        found = jnp.swapaxes(
            found.reshape(units_n, groups_n, cap, table_part), 0, 1
        )
        return words + spread(match.astype(low_type), found).astype(low_type)

    extra = lax.fori_loop(1, rounds, more_words, jnp.zeros((seq_len, width), low_type))

    masks_r = rounded(mask_logits)
    noise_head = gate_noise[width : width + heads]
    noise_hid = gate_noise[:width][None]
    zhead = gate(masks_r[:heads], noise_head)
    zmha = gate(masks_r[heads], gate_noise[width + heads])
    zmlp = gate(masks_r[heads + 1], gate_noise[width + heads + 1])
    gates = jnp.concatenate(
        [
            jnp.repeat(zhead, head_size)[None],
            jnp.full((1, width), zmha),
            jnp.full((6, width), zmlp),
        ],
        0,
    )
    picks = positions.reshape(-1, 1)
    middle, vec_rows, *kept_rows = attend_step(
        heads,
        cap,
        fetched,
        extra,
        code_0[:, None],
        picks,
        segments.reshape(1, -1),
        noise_hid,
        gates,
        pos_vecs,
        (w_q, w_k, w_v, w_out),
    )
    hid_logit = vec_rows[13]

    up_w = slice_all[:, :ffn_rows].reshape(width, ffn_cols)
    down_w = slice_all[:, ffn_rows : 2 * ffn_rows].reshape(width, ffn_cols)
    small = slice_all[:, 2 * ffn_rows :].reshape(groups_n, -1)
    unit_group = jnp.swapaxes(
        small[:, : unit_vecs.size].reshape(groups_n, 2, unit_vecs.shape[1]), 0, 1
    ).reshape(2, -1)
    bias_group = small[:, unit_vecs.size : small_len].reshape(-1).astype(full_type)
    unit_bias = unit_group[0].astype(full_type)
    unit_logit = unit_group[1].astype(full_type)
    slice_units = unit_bias.shape[0]
    ffn_width = slice_units * units_n
    noise_units = lax.dynamic_slice_in_dim(unit_noise, unit_idx * slice_units, slice_units, 0)
    zunit = gate(unit_logit, noise_units)
    npos = groups_n * units_n * nmask
    (
        share_head,
        grad_bias,
        grad_up,
        grad_down,
        grad_units,
        grad_wtrans,
        grad_middle,
        mid_vecs,
        mid_stats,
    ) = mid_step(
        middle,
        up_w,
        down_w,
        jnp.concatenate(
            [
                unit_bias[None],
                zunit[None],
                jnp.full((6, slice_units), jnp.sum(keep_score(unit_logit))),
            ],
            0,
        ),
        table_cols,
        bias_group[None],
        teacher.reshape(-1, vocab_slice),
        w_trans,
        vec_rows,
        units_n,
        groups_n,
        npos,
        2,
    )
    kl_own = mid_stats[0, 0]
    unit_score = mid_stats[1, 0]
    grad_bias = grad_bias[0]

    hid_sum = jnp.sum(keep_score(hid_logit))
    head_scores = keep_score(masks_r[:heads])
    mha_score = keep_score(masks_r[heads])
    mlp_score = keep_score(masks_r[heads + 1])
    head_sum = jnp.sum(head_scores) * mha_score
    unit_sum = unit_score * mlp_score
    full_size = 4.0 * width * width + 2.0 * width * ffn_width
    kept = (4.0 * head_size * hid_sum * head_sum + 2.0 * hid_sum * unit_sum) / full_size
    sparsity = 1.0 - kept
    lagrange = multipliers[0] * (sparsity - TARGET) + multipliers[1] * (sparsity - TARGET) ** 2
    lag_slope = -(multipliers[0] + 2.0 * multipliers[1] * (sparsity - TARGET))
    grad_ubias = grad_units[0]
    grad_ulogit = gate_back(unit_logit, noise_units, grad_units[1])
    small_grads = jnp.concatenate(
        [
            jnp.swapaxes(
                jnp.stack([grad_ubias, grad_ulogit]).reshape(2, groups_n, -1), 0, 1
            ).reshape(groups_n, -1),
            grad_bias.reshape(groups_n, -1),
        ],
        1,
    )
    pack_lines = 16 * -(-small_len // 2048)

    def packed(values):
        return jnp.pad(
            values, ((0, 0), (0, pack_lines * 128 - small_len))
        ).reshape(-1, 128)

    small_low = packed(small_grads).astype(low_type)

    grad_wq, grad_wk, grad_wv, grad_wout, grad_last, word_grads, embed_low, gate_sums = (
        attend_back_step(
            heads,
            groups_n,
            units_n,
            cap,
            grad_middle,
            mid_vecs,
            (vec_rows, *kept_rows),
            code_0[None],
            picks,
            noise_hid,
            gates,
            (w_q, w_k, w_v, w_out),
        )
    )
    grad_zhead = jnp.sum(gate_sums[0].reshape(heads, head_size), 1)
    grad_zmha = jnp.sum(gate_sums[1])
    grad_zmlp = jnp.sum(gate_sums[2])

    def word_parts(match):
        return jnp.stack(
            [
                jnp.dot(
                    match,
                    embed_low[:, d * table_part : (d + 1) * table_part],
                    preferred_element_type=full_type,
                )
                .astype(low_type)
                .reshape(units_n, cap, table_part)
                for d in range(groups_n)
            ]
        )

    def more_grads(k, total):
        match = round_match(k)
        mine = round_asked(match).reshape(-1)
        back = jnp.swapaxes(word_parts(match.astype(low_type)), 0, 1).reshape(
            units_n * groups_n, cap, table_part
        )
        back = lax.all_to_all(back, everyone, 0, 0, tiled=True).reshape(-1, table_part)
        target = jnp.where(mine >= 0, mine, vocab_slice)
        added = total.astype(full_type).at[:, target].add(
            back.T.astype(full_type), mode="drop"
        )
        return added.astype(low_type)

    more = lax.fori_loop(
        1, rounds, more_grads, jnp.zeros((table_part, vocab_slice), low_type)
    )

    grad_head = gate_back(masks_r[:heads], noise_head, grad_zhead)
    grad_mha = gate_back(masks_r[heads], gate_noise[width + heads], grad_zmha)
    grad_mlp = gate_back(masks_r[heads + 1], gate_noise[width + heads + 1], grad_zmlp)
    own_hid = rounded(layer_vecs[13])
    own_unit = rounded(unit_vecs[1])
    lag_hid = (
        lag_slope * (4.0 * head_size * head_sum + 2.0 * unit_sum) / full_size * score_slope(own_hid)
    )
    lag_unit = lag_slope * 2.0 * hid_sum * mlp_score / full_size * score_slope(own_unit)
    lag_head = (
        lag_slope * 4.0 * head_size * hid_sum * mha_score / full_size * score_slope(masks_r[:heads])
    )
    lag_mha = (
        lag_slope
        * 4.0
        * head_size
        * hid_sum
        * jnp.sum(head_scores)
        / full_size
        * score_slope(masks_r[heads])
    )
    lag_mlp = lag_slope * 2.0 * hid_sum * unit_score / full_size * score_slope(masks_r[heads + 1])
    lag_masks = jnp.concatenate([lag_head, lag_mha[None], lag_mlp[None]])
    mine = jnp.concatenate([grad_head, grad_mha[None], grad_mlp[None], kl_own[None]])
    n_masks = heads + 2
    share_table, totals, *shares = return_rows(
        word_grads,
        asked[:, :cap].reshape(-1, 1),
        share_head,
        more,
        jnp.pad(lag_hid[:, None], ((0, 0), (n_vecs - 1, 128 - n_vecs))),
        packed(jnp.pad(lag_unit, (unit_vecs.shape[1], small_len - unit_vecs.size))[None]),
        jnp.broadcast_to(jnp.pad(mine, (0, 128 - mine.shape[0])), (8, 128)),
        (grad_wq, grad_wk, grad_wv, grad_wout, grad_wtrans, grad_last),
        (grad_up, grad_down, small_low),
        units_n,
        groups_n,
        9,
    )
    totals = totals[0]
    share_vecs = shares[5][:, seq_len : seq_len + n_vecs].T
    share_small = shares[8].reshape(-1)
    share_unit = share_small[: unit_vecs.size].reshape(unit_vecs.shape)
    share_bias = share_small[unit_vecs.size : small_len]
    share_masks = totals[:n_masks] + lag_masks
    grad_norm = jnp.sqrt(totals[127] + jnp.sum(share_masks * share_masks))
    loss = TEMPER * TEMPER * totals[n_masks] / npos + lagrange
    coef = jnp.minimum(1.0, MAX_NORM / (grad_norm + 1e-06))
    count = step_count[0].astype(full_type)
    vecs_grad = share_vecs * coef
    unit_grad = share_unit * coef
    bias_grad = share_bias * coef
    mask_grad = share_masks * coef
    mats_new, mats_grad, ffn_new, ffn_grad, table_new, table_grad = update_step(
        jnp.broadcast_to(
            jnp.pad(
                jnp.stack([coef, 1.0 - BETA_ONE**count, 1.0 - BETA_TWO**count]), (0, 5)
            )[:, None],
            (8, 128),
        ),
        (*shares[:5], shares[5]),
        shares[6:8],
        share_table,
        (layer_mats, mats_first, mats_second),
        (ffn_mats, ffn_first, ffn_second),
        (table_turned, table_first.T, table_second.T),
    )
    table_new, table_grad = table_new.T, table_grad.T
    vecs_new = adamw(layer_vecs, vecs_first, vecs_second, vecs_grad, RATE_VECS, count)
    unit_new = adamw(unit_vecs, unit_first, unit_second, unit_grad, RATE_VECS, count)
    bias_new = adamw(word_bias, bias_first, bias_second, bias_grad, RATE_VECS, count)
    mask_new = adamw(mask_logits, mask_first, mask_second, mask_grad, RATE_VECS, count)
    return (
        loss,
        kept,
        grad_norm,
        mats_new,
        mats_grad,
        vecs_new,
        vecs_grad,
        ffn_new,
        ffn_grad,
        unit_new,
        unit_grad,
        table_new,
        table_grad,
        bias_new,
        bias_grad,
        mask_new,
        mask_grad,
    )


def solution(mesh):
    return jax.shard_map(
        on_device,
        mesh=mesh,
        in_specs=(
            P("dp", None, None),
            P("dp", "unit", None),
            P("dp", "unit", None),
            P("dp", None, None, "unit"),
            P(),
            P(),
            P(),
            P(),
            P(("unit", "dp"), None),
            P(("unit", "dp"), None),
            P(("unit", "dp"), None),
            P(None, ("unit", "dp")),
            P(None, ("unit", "dp")),
            P(None, ("unit", "dp")),
            P(None, "dp", "unit"),
            P(None, "dp", "unit"),
            P(None, "dp", "unit"),
            P(None, ("unit", "dp")),
            P(None, ("unit", "dp")),
            P(None, ("unit", "dp")),
            P("unit", "dp"),
            P("unit", "dp"),
            P("unit", "dp"),
            P(("unit", "dp")),
            P(("unit", "dp")),
            P(("unit", "dp")),
            P(),
            P(),
            P(),
        ),
        out_specs=(
            P(),
            P(),
            P(),
            P(("unit", "dp"), None),
            P(("unit", "dp"), None),
            P(None, ("unit", "dp")),
            P(None, ("unit", "dp")),
            P(None, "dp", "unit"),
            P(None, "dp", "unit"),
            P(None, ("unit", "dp")),
            P(None, ("unit", "dp")),
            P("unit", "dp"),
            P("unit", "dp"),
            P(("unit", "dp")),
            P(("unit", "dp")),
            P(),
            P(),
        ),
        check_vma=False,
    )
```

```python
import functools
import math

import jax
import jax.numpy as jnp
from jax import lax
from jax.experimental import pallas as pl
from jax.experimental.pallas import tpu as pltpu
from jax.sharding import PartitionSpec as P

EPS_NORM = 1e-12
GAMMA = -0.1
ZETA = 1.1
BETA = 2.0 / 3.0
TARGET = 0.95
TEMPER = 2.0
MAX_NORM = 0.0001
BETA_ONE = 0.9
BETA_TWO = 0.999
ADAM_EPS = 1e-08
DECAY = 0.01
RATE_MATS = 0.5
RATE_VECS = 5.0
RATE_TABLE = 1.0


def rounded(values):
    return lax.optimization_barrier(values.astype(jnp.bfloat16)).astype(jnp.float32)


def layer_norm(values, gain, shift):
    center = values - jnp.mean(values, -1, keepdims=True)
    spread = jnp.mean(center * center, -1, keepdims=True)
    return center * lax.rsqrt(spread + EPS_NORM) * gain + shift


def norm_back(values, gain, shift, grad):
    _, pull = jax.vjp(layer_norm, values, gain, shift)
    return pull(grad)


def gelu_back(values, grad):
    _, pull = jax.vjp(jax.nn.gelu, values)
    return pull(grad)[0]


def gate(logit, noise):
    soft = jax.nn.sigmoid((jnp.log(noise) - jnp.log(1.0 - noise) + logit) / BETA)
    return jnp.clip(soft * (ZETA - GAMMA) + GAMMA, 0.0, 1.0)


def gate_back(logit, noise, grad):
    _, pull = jax.vjp(gate, logit, noise)
    return pull(grad)[0]


def keep_score(logit):
    return jax.nn.sigmoid(logit - BETA * math.log(-GAMMA / ZETA))


def score_slope(logit):
    score = keep_score(logit)
    return score * (1.0 - score)


def contract_rows(left, right):
    return lax.dot_general(
        left, right, (((0,), (0,)), ((), ())), preferred_element_type=jnp.float32
    )


MESH = pl.DeviceIdType.MESH
VMEM_LIMIT = 60 * 1024 * 1024


def on_chip():
    return pl.BlockSpec(memory_space=pltpu.VMEM)


def call_params(collective):
    return pltpu.CompilerParams(
        collective_id=collective, has_side_effects=True, vmem_limit_bytes=VMEM_LIMIT
    )


def greet_unit(n, me):
    barrier = pltpu.get_barrier_semaphore()

    def step(j, carry):
        pl.semaphore_signal(
            barrier, inc=1, device_id={"unit": lax.rem(me + j, n)}, device_id_type=MESH
        )
        return carry

    lax.fori_loop(1, n, step, 0)
    pl.semaphore_wait(barrier, n - 1)


def greet_all(nu, nd, me):
    barrier = pltpu.get_barrier_semaphore()

    def step(j, carry):
        peer = lax.rem(me + j, nu * nd)
        pl.semaphore_signal(
            barrier,
            inc=1,
            device_id={"unit": peer // nd, "dp": lax.rem(peer, nd)},
            device_id_type=MESH,
        )
        return carry

    lax.fori_loop(1, nu * nd, step, 0)
    pl.semaphore_wait(barrier, nu * nd - 1)


def gather_kernel(n, x_ref, out_ref, send_sem, recv_sem):
    me = lax.axis_index("unit")
    greet_unit(n, me)

    def copy(peer, slot):
        return pltpu.make_async_remote_copy(
            src_ref=x_ref,
            dst_ref=out_ref.at[slot],
            send_sem=send_sem.at[peer],
            recv_sem=recv_sem.at[slot],
            device_id={"unit": peer},
            device_id_type=MESH,
        )

    def start(j, carry):
        copy(lax.rem(me + j, n), me).start()
        return carry

    def wait(j, carry):
        peer = lax.rem(me + j, n)
        copy(peer, me).wait_send()
        copy(peer, peer).wait_recv()
        return carry

    lax.fori_loop(1, n, start, 0)
    out_ref[me] = x_ref[...]
    lax.fori_loop(1, n, wait, 0)


def gather_unit(x, n, collective):
    return pl.pallas_call(
        functools.partial(gather_kernel, n),
        out_shape=jax.ShapeDtypeStruct((n,) + x.shape, x.dtype),
        in_specs=[on_chip()],
        out_specs=on_chip(),
        scratch_shapes=[pltpu.SemaphoreType.DMA((n,)), pltpu.SemaphoreType.DMA((n,))],
        compiler_params=call_params(collective),
    )(x)


def scatter_kernel(n, x_ref, out_ref, held, send_sem, recv_sem):
    me = lax.axis_index("unit")
    greet_unit(n, me)

    def copy(peer, slot):
        return pltpu.make_async_remote_copy(
            src_ref=x_ref.at[peer],
            dst_ref=held.at[slot],
            send_sem=send_sem.at[peer],
            recv_sem=recv_sem.at[slot],
            device_id={"unit": peer},
            device_id_type=MESH,
        )

    def start(j, carry):
        copy(lax.rem(me + j, n), me).start()
        return carry

    def wait(j, carry):
        peer = lax.rem(me + j, n)
        copy(peer, me).wait_send()
        copy(peer, peer).wait_recv()
        return carry

    lax.fori_loop(1, n, start, 0)
    held[me] = x_ref[me]
    lax.fori_loop(1, n, wait, 0)
    out_ref[...] = jnp.zeros_like(out_ref)

    def add(j, carry):
        out_ref[...] += held[j].astype(jnp.float32)
        return carry

    lax.fori_loop(0, n, add, 0)


def scatter_unit(x, n, collective):
    return pl.pallas_call(
        functools.partial(scatter_kernel, n),
        out_shape=jax.ShapeDtypeStruct(x.shape[1:], jnp.float32),
        in_specs=[on_chip()],
        out_specs=on_chip(),
        scratch_shapes=[
            pltpu.VMEM(x.shape, x.dtype),
            pltpu.SemaphoreType.DMA((n,)),
            pltpu.SemaphoreType.DMA((n,)),
        ],
        compiler_params=call_params(collective),
    )(x)


def total_kernel(nu, nd, x_ref, out_ref, held, send_sem, recv_sem):
    n = nu * nd
    me = lax.axis_index("unit") * nd + lax.axis_index("dp")
    greet_all(nu, nd, me)

    def copy(peer, slot):
        return pltpu.make_async_remote_copy(
            src_ref=x_ref,
            dst_ref=held.at[slot],
            send_sem=send_sem.at[peer],
            recv_sem=recv_sem.at[slot],
            device_id={"unit": peer // nd, "dp": lax.rem(peer, nd)},
            device_id_type=MESH,
        )

    def start(j, carry):
        copy(lax.rem(me + j, n), me).start()
        return carry

    def wait(j, carry):
        peer = lax.rem(me + j, n)
        copy(peer, me).wait_send()
        copy(peer, peer).wait_recv()
        return carry

    lax.fori_loop(1, n, start, 0)
    held[me] = x_ref[...]
    lax.fori_loop(1, n, wait, 0)
    out_ref[...] = jnp.zeros_like(out_ref)

    def add(j, carry):
        out_ref[...] += held[j]
        return carry

    lax.fori_loop(0, n, add, 0)


def total_all(x, nu, nd, collective):
    n = nu * nd
    return pl.pallas_call(
        functools.partial(total_kernel, nu, nd),
        out_shape=jax.ShapeDtypeStruct(x.shape, x.dtype),
        in_specs=[on_chip()],
        out_specs=on_chip(),
        scratch_shapes=[
            pltpu.VMEM((n,) + x.shape, x.dtype),
            pltpu.SemaphoreType.DMA((n,)),
            pltpu.SemaphoreType.DMA((n,)),
        ],
        compiler_params=call_params(collective),
    )(x)


def packed_shape(cap, part):
    return (cap + cap // 2, 128) if part == 192 and cap % 32 == 0 else (cap, part)


def lane_place(part, width, first):
    lines = lax.broadcasted_iota(jnp.int32, (part, width), 0) + first
    return jnp.where(
        lines == lax.broadcasted_iota(jnp.int32, (part, width), 1), 1.0, 0.0
    ).astype(jnp.bfloat16)


def half_place(width, first, upper):
    lines = lax.broadcasted_iota(jnp.int32, (128, width), 0)
    lanes = lax.broadcasted_iota(jnp.int32, (128, width), 1)
    low_end, shift = (64, first - 64) if upper else (0, first)
    inside = jnp.logical_and(lines >= low_end, lines < low_end + 64)
    return jnp.where(jnp.logical_and(inside, lines + shift == lanes), 1.0, 0.0).astype(
        jnp.bfloat16
    )


def product(left, right, left_dim=1, right_dim=0):
    return lax.dot_general(
        left,
        right,
        (((left_dim,), (right_dim,)), ((), ())),
        preferred_element_type=jnp.float32,
    )


def pack_rows(values, count, cap, width, first, part):
    full = product(values, lane_place(min(part, 128), width, first), 1, 1)
    if packed_shape(cap, part)[0] == cap:
        rest = []
        if part > 128:
            full = product(values, lane_place(part, width, first), 1, 1)
        return full.astype(jnp.bfloat16).reshape(count, cap, part), rest
    left = product(values, half_place(width, first + 128, False), 1, 1)
    right = product(values, half_place(width, first + 128, True), 1, 1)
    shape = (count, cap, 128)
    tail = left.reshape(shape)[:, : cap // 2] + right.reshape(shape)[:, cap // 2 :]
    return full.astype(jnp.bfloat16).reshape(shape), [tail.astype(jnp.bfloat16)]


def unpack_rows(ref, cap, width, first, part):
    count = ref.shape[0]
    if packed_shape(cap, part)[0] == cap:
        return product(ref[...].reshape(count * cap, part), lane_place(part, width, first))
    full = product(ref[:, :cap, :].reshape(count * cap, 128), lane_place(128, width, first))
    tail = ref[:, cap:, :].reshape(count * cap // 2, 128)
    shape = (count, cap // 2, width)
    both = jnp.concatenate(
        [
            product(tail, half_place(width, first + 128, False)).reshape(shape),
            product(tail, half_place(width, first + 128, True)).reshape(shape),
        ],
        1,
    )
    return full + both.reshape(count * cap, width)


def grid_of(nu, nd):
    ny = 2 if nu % 2 == 0 else 1
    nc = 2 if nd % 2 == 0 else 1
    return (nu // ny, ny, nd // nc, nc)


def grid_place(grid):
    unit, dp = lax.axis_index("unit"), lax.axis_index("dp")
    return (unit // grid[1], lax.rem(unit, grid[1]), dp // grid[3], lax.rem(dp, grid[3]))


def grid_device(grid, place):
    return {"unit": place[0] * grid[1] + place[1], "dp": place[2] * grid[3] + place[3]}


def loader(ref):
    return lambda: ref[...]


def column_loader(ref, first, length):
    return lambda: ref[:, first : first + length]


def low_loader(ref, *where):
    return lambda: ref[where].astype(jnp.bfloat16)


def tile_of(vocab):
    return 768 if vocab % 768 == 0 else vocab


def early_tiles(vocab):
    return min(1, vocab // tile_of(vocab))


def dp_grid(grid, place):
    return (
        (1, 1, grid[2], grid[3]),
        (0, 0, place[2], place[3]),
        lambda at: {"dp": at[2] * grid[3] + at[3]},
    )


def moved(place, axis, index):
    return tuple(index if k == axis else place[k] for k in range(4))


GATHER_ORDERS = ((0, 1, 2, 3), (0, 2, 1, 3))
REDUCE_ORDERS = ((3, 2, 1, 0), (3, 1, 2, 0))
DP_ORDER = (3, 2)
DP_GATHER = (2, 3)


class Gather:
    def __init__(self, grid, place, order, load, out, send_sem, recv_sem, device=None):
        self.grid, self.place, self.order = grid, place, order
        self.device = device or (lambda at: grid_device(grid, at))
        self.load, self.out, self.send_sem, self.recv_sem = load, out, send_sem, recv_sem

    def window(self, stage, index):
        axis = self.order[stage]
        where = []
        for k in range(4):
            if k == axis:
                where.append(pl.ds(index, 1))
            elif k in self.order[:stage]:
                where.append(pl.ds(0, self.grid[k]))
            else:
                where.append(pl.ds(self.place[k], 1))
        return self.out.at[tuple(where)]

    def copy(self, stage, hop, arriving):
        axis = self.order[stage]
        n = self.grid[axis]
        mine = self.place[axis]
        to = lax.rem(mine + hop, n)
        held = self.window(stage, lax.rem(mine + n - hop, n) if arriving else mine)
        return pltpu.make_async_remote_copy(
            src_ref=held,
            dst_ref=held,
            send_sem=self.send_sem.at[stage, hop],
            recv_sem=self.recv_sem.at[stage, hop],
            device_id=self.device(moved(self.place, axis, to)),
            device_id_type=MESH,
        )

    def start(self, stage):
        if stage == 0:
            self.out[self.place] = self.load()
        for hop in range(1, self.grid[self.order[stage]]):
            self.copy(stage, hop, False).start()

    def finish(self, stage):
        for hop in range(1, self.grid[self.order[stage]]):
            self.copy(stage, hop, False).wait_send()
            self.copy(stage, hop, True).wait_recv()


class Reduce:
    def __init__(self, grid, place, order, x, helds, sums, out, send_sem, recv_sem, device=None):
        self.grid, self.place, self.order = grid, place, order
        self.device = device or (lambda at: grid_device(grid, at))
        self.refs = (x,) + tuple(sums)
        self.helds, self.out = helds, out
        self.send_sem, self.recv_sem = send_sem, recv_sem

    def window(self, stage, index):
        axis = self.order[stage]
        where = []
        for k in range(4):
            if k == axis:
                where.append(pl.ds(index, 1))
            elif k in self.order[:stage]:
                where.append(pl.ds(0, 1))
            else:
                where.append(pl.ds(0, self.grid[k]))
        return self.refs[stage].at[tuple(where)]

    def copy(self, stage, hop):
        axis = self.order[stage]
        to = lax.rem(self.place[axis] + hop, self.grid[axis])
        return pltpu.make_async_remote_copy(
            src_ref=self.window(stage, to),
            dst_ref=self.helds[stage].at[hop - 1],
            send_sem=self.send_sem.at[stage, hop],
            recv_sem=self.recv_sem.at[stage, hop],
            device_id=self.device(moved(self.place, axis, to)),
            device_id_type=MESH,
        )

    def start(self, stage):
        for hop in range(1, self.grid[self.order[stage]]):
            self.copy(stage, hop).start()

    def finish(self, stage):
        axis = self.order[stage]
        n = self.grid[axis]
        for hop in range(1, n):
            self.copy(stage, hop).wait()
        left = [
            1 if k in self.order[: stage + 1] else self.grid[k] for k in range(4)
        ]
        last = stage == len(self.order) - 1

        def add(i, carry):
            where = []
            for k in (3, 2, 1, 0):
                where.insert(0, lax.rem(i, left[k]))
                i = i // left[k]
            own = moved(tuple(where), axis, self.place[axis])
            total = self.refs[stage][own].astype(jnp.float32)
            for hop in range(1, n):
                total = total + self.helds[stage][(hop - 1, *where)].astype(jnp.float32)
            if last:
                self.out[...] = total
            else:
                self.refs[stage + 1][tuple(where)] = total.astype(jnp.bfloat16)
            return carry

        lax.fori_loop(0, math.prod(left), add, 0)


def reduce_scratch(grid, orders, shapes):
    helds, sums = [], []
    for order, shape in zip(orders, shapes, strict=True):
        left = list(grid)
        for stage, axis in enumerate(order):
            n = left[axis]
            left[axis] = 1
            helds.append(pltpu.VMEM((max(n - 1, 1), *left, *shape), jnp.bfloat16))
            if stage < len(order) - 1:
                sums.append(pltpu.VMEM((*left, *shape), jnp.bfloat16))
    return helds, sums


def fetch_kernel(nu, nd, cap, count, *refs):
    wanted, table = refs[:2]
    parts = refs[2 : 2 + count]
    out, asked = refs[2 + count : 4 + count]
    wholes = refs[4 + count : 4 + 2 * count]
    tab = refs[4 + 2 * count]
    sought, rows, send_a, recv_a, send_b, recv_b, own_sem, send_g, recv_g = refs[5 + 2 * count :]
    n = nu * nd
    grid = grid_of(nu, nd)
    place = grid_place(grid)
    gathers = [
        Gather(
            grid,
            place,
            GATHER_ORDERS[i % 2],
            loader(parts[i]),
            wholes[i],
            send_g.at[i],
            recv_g.at[i],
        )
        for i in range(count)
    ]
    part_grid, part_place, part_device = dp_grid(grid, place)
    tile = tab.shape[-1]
    tables = [
        Gather(
            part_grid,
            part_place,
            DP_GATHER,
            column_loader(table, v * tile, tile),
            tab.at[v],
            send_g.at[count + v],
            recv_g.at[count + v],
            part_device,
        )
        for v in range(tab.shape[0])
    ]
    my_unit = lax.axis_index("unit")
    my_dp = lax.axis_index("dp")
    me = my_unit * nd + my_dp
    vocab = table.shape[1]
    block = 1280 if vocab % 1280 == 0 else vocab
    greet_all(nu, nd, me)

    def ask(peer, slot):
        return pltpu.make_async_remote_copy(
            src_ref=wanted.at[peer // nd],
            dst_ref=asked.at[slot],
            send_sem=send_a.at[peer],
            recv_sem=recv_a.at[slot],
            device_id={"unit": peer // nd, "dp": lax.rem(peer, nd)},
            device_id_type=MESH,
        )

    def answer(unit, dp, from_unit, from_dp):
        peer = unit * nd + dp
        return pltpu.make_async_remote_copy(
            src_ref=rows.at[peer],
            dst_ref=out.at[from_dp, from_unit],
            send_sem=send_b.at[peer],
            recv_sem=recv_b.at[from_unit * nd + from_dp],
            device_id={"unit": unit, "dp": dp},
            device_id_type=MESH,
        )

    def ask_start(j, carry):
        ask(lax.rem(me + j, n), me).start()
        return carry

    def ask_wait(j, carry):
        peer = lax.rem(me + j, n)
        ask(peer, me).wait_send()
        ask(peer, peer).wait_recv()
        return carry

    lax.fori_loop(1, n, ask_start, 0)
    for gather in gathers:
        gather.start(0)
    for gather in tables:
        gather.start(0)
    asked[me] = wanted[my_unit]
    lax.fori_loop(1, n, ask_wait, 0)

    def one_group(g):
        dp = lax.rem(my_dp + g, nd)
        part = table.shape[0]
        total = jnp.zeros((part, nu * cap), jnp.float32)
        for start in range(0, vocab, block):
            lines = lax.broadcasted_iota(jnp.int32, (block, nu * cap), 0) + start
            hit = jnp.where(lines == sought[pl.ds(dp, 1), :], 1.0, 0.0).astype(jnp.bfloat16)
            total = total + product(table[:, start : start + block], hit)
        found = jnp.swapaxes(total, 0, 1).astype(jnp.bfloat16)
        head, tails = pack_rows(found, nu, cap, part, 0, part)
        for unit in range(nu):
            rows[unit * nd + dp, :cap] = head[unit]
            for tail in tails:
                rows[unit * nd + dp, cap:] = tail[unit]

        def send(unit, carry):
            @pl.when(jnp.logical_or(unit != my_unit, dp != my_dp))
            def _():
                answer(unit, dp, my_unit, my_dp).start()

            return carry

        lax.fori_loop(0, nu, send, 0)

    def advance(t):
        for i, gather in enumerate(gathers):
            stage = t - i // 2
            if 0 <= stage < 4:
                gather.finish(stage)
                if stage < 3:
                    gather.start(stage + 1)

    for dp in range(nd):
        sought[dp : dp + 1, :] = jnp.concatenate(
            [asked[unit * nd + dp][:, :cap] for unit in range(nu)], 1
        )
    for g in range(nd):
        one_group(g)
        advance(g)
    for t in range(nd, 4 + (count - 1) // 2):
        advance(t)
    for gather in tables:
        gather.finish(0)
        gather.start(1)
    for gather in tables:
        gather.finish(1)
    own = pltpu.make_async_copy(rows.at[me], out.at[my_dp, my_unit], own_sem)
    own.start()
    own.wait()

    def answer_wait(j, carry):
        peer = lax.rem(me + j, n)
        unit, dp = peer // nd, lax.rem(peer, nd)
        answer(unit, dp, my_unit, my_dp).wait_send()
        answer(unit, dp, unit, dp).wait_recv()
        return carry

    lax.fori_loop(1, n, answer_wait, 0)


def fetch_rows(wanted, table, parts, nu, nd, cap, collective):
    n = nu * nd
    part, vocab = table.shape
    early = early_tiles(vocab)
    count = len(parts)
    grid = grid_of(nu, nd)
    reach = max(grid)
    return pl.pallas_call(
        functools.partial(fetch_kernel, nu, nd, cap, count),
        out_shape=(
            jax.ShapeDtypeStruct((nd, nu, *packed_shape(cap, part)), jnp.bfloat16),
            jax.ShapeDtypeStruct((n, 1, 128), jnp.int32),
            *(jax.ShapeDtypeStruct((*grid, *x.shape), x.dtype) for x in parts),
            jax.ShapeDtypeStruct((early, 1, 1, *grid[2:], part, tile_of(vocab)), jnp.bfloat16),
        ),
        in_specs=[on_chip()] * (2 + count),
        out_specs=(on_chip(),) * (3 + count),
        scratch_shapes=[
            pltpu.VMEM((nd, nu * cap), jnp.int32),
            pltpu.VMEM((n, *packed_shape(cap, part)), jnp.bfloat16),
            pltpu.SemaphoreType.DMA((n,)),
            pltpu.SemaphoreType.DMA((n,)),
            pltpu.SemaphoreType.DMA((n,)),
            pltpu.SemaphoreType.DMA((n,)),
            pltpu.SemaphoreType.DMA,
            pltpu.SemaphoreType.DMA((count + early, 4, reach)),
            pltpu.SemaphoreType.DMA((count + early, 4, reach)),
        ],
        compiler_params=call_params(collective),
    )(wanted, table, *parts)


def return_kernel(nu, nd, count, extras, units, *refs):
    x_ref, asked_ref, base_ref, more_ref, vec_own, small_own, info = refs[:7]
    n_all = count + extras
    grads = refs[7 : 7 + n_all]
    table_ref, totals_ref = refs[7 + n_all : 9 + n_all]
    shares = refs[9 + n_all : 9 + 2 * n_all]
    out_ref, rows_ref, mine_ref, held_ref, ids_ref = refs[9 + 2 * n_all : 14 + 2 * n_all]
    rest = refs[14 + 2 * n_all :]
    helds, sums = rest[: 4 * count], rest[4 * count : 7 * count]
    rest = rest[7 * count :]
    dp_helds, dp_sums = rest[: 2 * extras], rest[2 * extras : 3 * extras]
    send_sem, recv_sem, own_sem, send_r, recv_r, send_t, recv_t = rest[3 * extras :]
    n = nu * nd
    my_unit = lax.axis_index("unit")
    my_dp = lax.axis_index("dp")
    me = my_unit * nd + my_dp
    grid = grid_of(nu, nd)
    place = grid_place(grid)
    reduces = [
        Reduce(
            grid,
            place,
            REDUCE_ORDERS[i % 2],
            grads[i],
            helds[4 * i : 4 * i + 4],
            sums[3 * i : 3 * i + 3],
            shares[i],
            send_r.at[i],
            recv_r.at[i],
        )
        for i in range(count)
    ]
    part_grid, part_place, part_device = dp_grid(grid, place)
    part_reduces = [
        Reduce(
            part_grid,
            part_place,
            DP_ORDER,
            grads[count + i],
            dp_helds[2 * i : 2 * i + 2],
            dp_sums[i : i + 1],
            shares[count + i],
            send_r.at[count + i],
            recv_r.at[count + i],
            part_device,
        )
        for i in range(extras)
    ]
    greet_all(nu, nd, me)

    def peer_id(peer):
        return {"unit": peer // nd, "dp": lax.rem(peer, nd)}

    def copy(peer, slot):
        return pltpu.make_async_remote_copy(
            src_ref=x_ref.at[lax.rem(peer, nd), peer // nd],
            dst_ref=out_ref.at[slot],
            send_sem=send_sem.at[peer],
            recv_sem=recv_sem.at[slot],
            device_id=peer_id(peer),
            device_id_type=MESH,
        )

    def total_copy(peer, slot):
        return pltpu.make_async_remote_copy(
            src_ref=mine_ref,
            dst_ref=held_ref.at[slot],
            send_sem=send_t.at[peer],
            recv_sem=recv_t.at[slot],
            device_id=peer_id(peer),
            device_id_type=MESH,
        )

    def others(step):
        lax.fori_loop(1, n, lambda j, carry: (step(lax.rem(me + j, n)), carry)[1], 0)

    def wait(peer):
        copy(peer, me).wait_send()
        copy(peer, peer).wait_recv()

    def total_wait(peer):
        total_copy(peer, me).wait_send()
        total_copy(peer, peer).wait_recv()

    for reduce in reduces:
        reduce.start(0)
    others(lambda peer: copy(peer, me).start())
    for reduce in part_reduces:
        reduce.start(0)
    own = pltpu.make_async_copy(x_ref.at[my_dp, my_unit], out_ref.at[me], own_sem)
    own.start()
    own.wait()

    tiles, part, tile = base_ref.shape
    vocab = tiles * tile
    cap = ids_ref.shape[0] // n
    turned = jnp.swapaxes(asked_ref[...], 0, 1)
    for p in range(n):
        ids_ref[p * cap : (p + 1) * cap, :] = turned[:cap, p : p + 1]
    halves = 2 if tile % 256 == 0 else 1
    block = tile // halves

    def add_rows(b):
        first = b * block
        v, at = divmod(first, tile)
        lanes = lax.broadcasted_iota(jnp.int32, (ids_ref.shape[0], block), 1) + first
        hit = jnp.where(ids_ref[...] == lanes, 1.0, 0.0).astype(jnp.bfloat16)
        where = slice(first, first + block)
        both = (
            base_ref[v, :, at : at + block]
            + more_ref[:, where].astype(jnp.float32)
            + product(rows_ref[...], hit)
        )
        table_ref[:, where] = both
        return row_sum(both * both)

    steps = 4 + (count - 1) // 2
    blocks = vocab // block
    squares = jnp.zeros((1, block), jnp.float32)
    for t in range(steps):
        for i, reduce in enumerate(reduces):
            stage = t - i // 2
            if 0 <= stage < 4:
                reduce.finish(stage)
                if stage < 3:
                    reduce.start(stage + 1)
        if t < 2:
            for reduce in part_reduces:
                reduce.finish(t)
                if t == 0:
                    reduce.start(1)
        if t == 1:
            others(wait)
            arrived = unpack_rows(out_ref, ids_ref.shape[0] // n, part, 0, part)
            rows_ref[...] = jnp.swapaxes(arrived, 0, 1).astype(jnp.bfloat16)
        if t >= 1:
            done, left = t - 1, steps - 1
            for b in range(blocks * done // left, blocks * (done + 1) // left):
                squares = squares + add_rows(b)
    last = shares[count - 1]
    seq = last.shape[1] - 128
    own_slope = score_slope(vec_own[...].astype(jnp.bfloat16).astype(jnp.float32))
    column = lax.broadcasted_iota(jnp.int32, own_slope.shape, 1)
    last[:, seq:] += jnp.where(column == 13, info[2:3, 0:1] * own_slope, 0.0)
    own_slope = score_slope(small_own[...].astype(jnp.bfloat16).astype(jnp.float32))
    line = lax.broadcasted_iota(jnp.int32, own_slope.shape, 0)
    column = lax.broadcasted_iota(jnp.int32, own_slope.shape, 1)
    is_unit = jnp.logical_and(line == 1, column < units)
    shares[n_all - 1][...] += jnp.where(is_unit, info[3:4, 0:1] * own_slope, 0.0)
    square = jnp.sum(squares, 1, keepdims=True)
    for share in shares:
        square = square + jnp.sum(row_sum(share[...] * share[...]), 1, keepdims=True)
    lane = lax.broadcasted_iota(jnp.int32, (8, 128), 1)
    mine_ref[...] = jnp.where(lane == 127, square, info[0:1, :])
    others(lambda peer: total_copy(peer, me).start())
    held_ref[me] = mine_ref[...]
    others(total_wait)
    totals_ref[...] = jnp.zeros_like(totals_ref)

    def add_total(j, carry):
        totals_ref[...] += held_ref[j]
        return carry

    lax.fori_loop(0, n, add_total, 0)


def return_rows(
    x, asked, base, more, vec_own, small_own, info, grads, dp_grads, units, cap, nu, nd, collective
):
    n = nu * nd
    grid = grid_of(nu, nd)
    part_grid = (1, 1, *grid[2:])
    count, extras = len(grads), len(dp_grads)
    reach = max(grid)
    shapes = [(g.shape[0] // n, g.shape[1]) for g in grads]
    dp_shapes = [(g.shape[0] // nd, g.shape[1]) for g in dp_grads]
    helds, sums = reduce_scratch(grid, [REDUCE_ORDERS[i % 2] for i in range(count)], shapes)
    dp_helds, dp_sums = reduce_scratch(part_grid, [DP_ORDER] * extras, dp_shapes)
    tiles, part, tile = base.shape
    return pl.pallas_call(
        functools.partial(return_kernel, nu, nd, count, extras, units),
        out_shape=(
            jax.ShapeDtypeStruct((part, tiles * tile), jnp.float32),
            jax.ShapeDtypeStruct((8, 128), jnp.float32),
            *(jax.ShapeDtypeStruct(shape, jnp.float32) for shape in shapes + dp_shapes),
        ),
        in_specs=[on_chip()] * (7 + count + extras),
        out_specs=(on_chip(),) * (2 + count + extras),
        scratch_shapes=[
            pltpu.VMEM((n,) + x.shape[2:], x.dtype),
            pltpu.VMEM((part, n * cap), x.dtype),
            pltpu.VMEM((8, 128), jnp.float32),
            pltpu.VMEM((n, 8, 128), jnp.float32),
            pltpu.VMEM((n * cap, 1), jnp.int32),
            *helds,
            *sums,
            *dp_helds,
            *dp_sums,
            pltpu.SemaphoreType.DMA((n,)),
            pltpu.SemaphoreType.DMA((n,)),
            pltpu.SemaphoreType.DMA,
            pltpu.SemaphoreType.DMA((count + extras, 4, reach)),
            pltpu.SemaphoreType.DMA((count + extras, 4, reach)),
            pltpu.SemaphoreType.DMA((n,)),
            pltpu.SemaphoreType.DMA((n,)),
        ],
        compiler_params=call_params(collective),
    )(
        x,
        asked,
        base,
        more,
        vec_own,
        small_own,
        info,
        *(g.reshape(*grid, *shape) for g, shape in zip(grads, shapes, strict=True)),
        *(g.reshape(*part_grid, *shape) for g, shape in zip(dp_grads, dp_shapes, strict=True)),
    )


def update_kernel(heads, npos, mats, *refs):
    totals, info, scal = refs[:3]
    shares = refs[3 : mats + 6]
    share_t = refs[mats + 6]
    mw, mf, ms, vw, vf, vs, fw, ff, fs, uw, uf, us, bw, bf, bs, kw, kf, ks, tw, tf, ts = refs[
        mats + 7 : mats + 28
    ]
    outs = refs[mats + 28 :]
    m_new, m_grad, v_new, v_grad, f_new, f_grad = outs[:6]
    u_new, u_grad, b_new, b_grad, k_new, k_grad, stat, t_new, t_grad = outs[6:]
    lane = lax.broadcasted_iota(jnp.int32, (1, 128), 1)
    share_k = jnp.where(lane < heads + 2, totals[0:1, :] + info[1:2, :], 0.0)
    norm = jnp.sqrt(totals[0:1, 127:128] + jnp.sum(share_k * share_k, 1, keepdims=True))
    coef = jnp.minimum(1.0, MAX_NORM / (norm + 1e-06))
    first_scale, second_scale = scal[3:4, 0:1], scal[3:4, 1:2]

    def step(share, weight, first, second, rate):
        grad = share * coef
        first = BETA_ONE * first + (1.0 - BETA_ONE) * grad
        second = BETA_TWO * second + (1.0 - BETA_TWO) * grad * grad
        first_hat = first / first_scale
        second_hat = second / second_scale
        new = weight - rate * (first_hat / (jnp.sqrt(second_hat) + ADAM_EPS) + DECAY * weight)
        return grad, new

    t_grad[...], t_new[...] = step(share_t[...], tw[...], tf[...], ts[...], RATE_TABLE)

    @pl.when(pl.program_id(0) == 0)
    def _():
        first = 0
        for k in range(mats):
            length = min(shares[k].shape[1], mw.shape[1] - first)
            where = slice(first, first + length)
            m_grad[:, where], m_new[:, where] = step(
                shares[k][:, :length], mw[:, where], mf[:, where], ms[:, where], RATE_MATS
            )
            first += length

    @pl.when(pl.program_id(0) == 1)
    def _():
        for k in range(2):
            f_grad[k], f_new[k] = step(shares[mats + k][...], fw[k], ff[k], fs[k], RATE_MATS)

    @pl.when(pl.program_id(0) == 2)
    def _():
        last, small = shares[mats - 1], shares[mats + 2]
        turned = jnp.swapaxes(last[:, last.shape[1] - 128 :], 0, 1)[: vw.shape[0]]
        v_grad[...], v_new[...] = step(turned, vw[...], vf[...], vs[...], RATE_VECS)
        u_grad[...], u_new[...] = step(
            small[0:2, : uw.shape[1]], uw[...], uf[...], us[...], RATE_VECS
        )
        b_grad[...], b_new[...] = step(
            small[2:3, : bw.shape[1]], bw[...], bf[...], bs[...], RATE_VECS
        )
        k_grad[...], k_new[...] = step(
            share_k[:, : kw.shape[1]], kw[...], kf[...], ks[...], RATE_VECS
        )
        kl_all = totals[0:1, heads + 2 : heads + 3]
        loss = TEMPER * TEMPER * kl_all / npos + info[5:6, 0:1]
        line = lax.broadcasted_iota(jnp.int32, (8, 128), 0)
        stat[...] = jnp.where(line == 0, loss, jnp.where(line == 1, info[4:5, 0:1], norm))


def update_step(heads, npos, totals, info, scal, shares, share_table, small, table):
    part, vocab = share_table.shape
    blocks = 4
    row = pl.BlockSpec((part // blocks, vocab), lambda i: (i, 0))

    def whole(x):
        zeros = (0,) * len(x.shape)
        return pl.BlockSpec(x.shape, lambda i: zeros)

    args = [totals, info, scal, *shares, share_table]
    specs = [whole(x) for x in args[:-1]] + [row]
    for trio in small:
        args += trio
        specs += [whole(x) for x in trio]
    args += table
    specs += [row] * 3
    outs = [x for trio in small for x in (trio[0], trio[0])] + [totals, table[0], table[0]]
    return pl.pallas_call(
        functools.partial(update_kernel, heads, npos, len(shares) - 3),
        grid=(blocks,),
        out_shape=tuple(jax.ShapeDtypeStruct(x.shape, x.dtype) for x in outs),
        in_specs=specs,
        out_specs=tuple(whole(x) for x in outs[:-2]) + (row, row),
        compiler_params=pltpu.CompilerParams(vmem_limit_bytes=VMEM_LIMIT),
    )(*args)


def row_sum(values):
    return jnp.sum(values, 0, keepdims=True)


class UnitGather:
    def __init__(self, n, me, buf, send_sem, recv_sem):
        self.n, self.me, self.buf = n, me, buf
        self.send_sem, self.recv_sem = send_sem, recv_sem
        self.inner = n // 2
        self.half, self.idx = me // self.inner, lax.rem(me, self.inner)
        self.mirror = (1 - self.half) * self.inner + self.idx

    def near(self, hop):
        return self.half * self.inner + lax.rem(self.idx + hop, self.inner)

    def copy(self, block, to, kind, hop):
        return pltpu.make_async_remote_copy(
            src_ref=self.buf.at[block],
            dst_ref=self.buf.at[block],
            send_sem=self.send_sem.at[kind, hop],
            recv_sem=self.recv_sem.at[block],
            device_id={"unit": to},
            device_id_type=MESH,
        )

    def hops(self, step):
        lax.fori_loop(1, self.inner, lambda hop, carry: (step(hop), carry)[1], 0)

    def start(self):
        self.copy(self.me, self.mirror, 0, 0).start()
        self.hops(lambda hop: self.copy(self.me, self.near(hop), 0, hop).start())

    def forward(self):
        self.copy(self.mirror, self.mirror, 0, 0).wait_recv()
        self.hops(lambda hop: self.copy(self.mirror, self.near(hop), 1, hop).start())

    def wait_half(self):
        self.hops(lambda hop: self.copy(self.near(hop), self.mirror, 0, 0).wait_recv())

    def wait_rest(self):
        far = (1 - self.half) * self.inner

        def step(hop):
            block = far + lax.rem(self.idx + hop, self.inner)
            self.copy(block, self.mirror, 0, 0).wait_recv()

        self.hops(step)

    def finish(self):
        self.copy(self.me, self.mirror, 0, 0).wait_send()

        def step(hop):
            self.copy(self.me, self.near(hop), 0, hop).wait_send()
            self.copy(self.mirror, self.near(hop), 1, hop).wait_send()

        self.hops(step)


class UnitReduce:
    def __init__(self, n, me, part, held, mine, other, send_sem, recv_sem):
        self.n, self.me, self.part = n, me, part
        self.held, self.mine, self.other = held, mine, other
        self.send_sem, self.recv_sem = send_sem, recv_sem
        self.inner = n // 2
        self.half, self.idx = me // self.inner, lax.rem(me, self.inner)
        self.mirror = (1 - self.half) * self.inner + self.idx

    def copy(self, kind, hop):
        index = lax.rem(self.idx + hop, self.inner)
        half = self.half if kind else 1 - self.half
        return pltpu.make_async_remote_copy(
            src_ref=self.part.at[half * self.inner + index],
            dst_ref=self.held.at[kind, hop - 1],
            send_sem=self.send_sem.at[kind, hop],
            recv_sem=self.recv_sem.at[kind, hop],
            device_id={"unit": self.half * self.inner + index},
            device_id_type=MESH,
        )

    def across(self):
        return pltpu.make_async_remote_copy(
            src_ref=self.mine,
            dst_ref=self.other,
            send_sem=self.send_sem.at[0, 0],
            recv_sem=self.recv_sem.at[0, 0],
            device_id={"unit": self.mirror},
            device_id_type=MESH,
        )

    def start(self, kind):
        def step(hop, carry):
            self.copy(kind, hop).start()
            return carry

        lax.fori_loop(1, self.inner, step, 0)

    def wait(self, kind):
        def step(hop, carry):
            self.copy(kind, hop).wait()
            return carry

        lax.fori_loop(1, self.inner, step, 0)

    def total(self, kind, block):
        result = self.part[block].astype(jnp.float32)
        for hop in range(1, self.inner):
            result = result + self.held[kind, hop - 1].astype(jnp.float32)
        return result

    def middle(self):
        self.wait(0)
        self.mine[...] = self.total(0, self.mirror).astype(jnp.bfloat16)
        self.across().start()

    def finish(self):
        self.wait(1)
        result = self.total(1, self.me)
        self.across().wait()
        return result + self.other[...].astype(jnp.float32)


def mid_kernel(n, nd, npos, *refs):
    middle_ref, ffn_ref, pack_ref, noise_ref, own_ref, tab_in, teach_ref, wt_ref, vecs_ref = refs[
        :9
    ]
    share, small_out, gup, gdown, gwt, gmid, gvecs, stat_out = refs[9:17]
    unit_ref = refs[17]
    rows, backs, trans, hpre, hid, ghp, student, glow, acc, tmax, statc, stats = refs[18:30]
    part, mine, helds, others = refs[30], refs[31], refs[32:35], refs[35:38]
    gather_send, gather_recv, reduce_send, reduce_recv, stat_send, stat_recv = refs[38:44]
    gtable, dp_send, dp_recv, tab, halves, packs, vbias_ref, gvbias, gunit = refs[44:53]
    part_send, part_recv, tab_sem = refs[53:56]
    dp_scratch = refs[56:]
    me = lax.axis_index("unit")
    all_grid = grid_of(n, nd)
    grid, place, device = dp_grid(all_grid, grid_place(all_grid))
    low, full = jnp.bfloat16, jnp.float32
    count, width = middle_ref.shape
    vocab = own_ref.shape[1]
    tiles, tile = tab.shape[0], tab.shape[-1]
    early = tab_in.shape[0]
    group = max(1, 256 // count)
    block = group * count
    per_half = n // 2 // group
    half = me // (n // 2)
    table_reduces = [
        Reduce(
            grid,
            place,
            DP_ORDER,
            gtable.at[v],
            dp_scratch[3 * v : 3 * v + 2],
            dp_scratch[3 * v + 2 : 3 * v + 3],
            share.at[v],
            dp_send.at[v],
            dp_recv.at[v],
            device,
        )
        for v in range(tiles)
    ]
    own_blocks = (half * per_half, (half + 1) * per_half)
    far_blocks = ((1 - half) * per_half, (2 - half) * per_half)
    greet_all(n, nd, me * nd + lax.axis_index("dp"))
    gathers = [
        UnitGather(n, me, buf, gather_send.at[i], gather_recv.at[i])
        for i, buf in enumerate((rows, trans, backs))
    ]
    reduces = [
        UnitReduce(
            n, me, part, helds[i], mine, others[i], reduce_send.at[i], reduce_recv.at[i]
        )
        for i in range(3)
    ]

    loads = [
        (low_loader(ffn_ref, 0), halves.at[0]),
        (low_loader(ffn_ref, 1), halves.at[1]),
        (low_loader(pack_ref, slice(None)), packs),
        *((column_loader(own_ref, v * tile, tile), tab.at[v]) for v in range(early, tiles)),
    ]
    parts_in = [
        Gather(
            grid, place, DP_GATHER, load, out, part_send.at[i], part_recv.at[i], device
        )
        for i, (load, out) in enumerate(loads)
    ]
    tab_copy = pltpu.make_async_copy(tab_in, tab.at[pl.ds(0, early)], tab_sem)

    def up_w():
        return halves[0].reshape(width, -1)

    def down_w():
        return halves[1].reshape(width, -1)

    def table_tile(v):
        return tab[v].reshape(width, tile)

    def vec(k):
        return vecs_ref[k : k + 1, :]

    def loop(span, step):
        lax.fori_loop(span[0], span[1], lambda b, carry: (step(b), carry)[1], 0)

    def lines(b):
        return pl.ds(pl.multiple_of(b * block, block), block)

    def columns(v):
        return pl.ds(pl.multiple_of(v * tile, 128), tile)

    def gathered(buf, b):
        return buf[pl.ds(b * group, group)].reshape(block, width)

    def put_part(b, values):
        part[pl.ds(b * group, group)] = values.astype(low).reshape(group, count, width)

    middle = middle_ref[...]
    rows[me] = middle.astype(low)
    gathers[0].start()
    for one in parts_in:
        one.start(0)
    tab_copy.start()

    def teacher_top(b):
        top = jnp.max(teach_ref[lines(b), :].astype(full), 1, keepdims=True) / TEMPER
        tmax[lines(b), :] = jnp.broadcast_to(top, (block, 128))

    loop((0, n // group), teacher_top)
    gathers[0].forward()
    for one in parts_in[:3]:
        one.finish(0)
        one.start(1)
    gathers[0].wait_half()
    for one in parts_in[:3]:
        one.finish(1)
    blocks_in = [packs[0, 0, d // grid[3], d % grid[3]].astype(full) for d in range(nd)]
    units, biases = unit_ref.shape[1] // nd, vocab // nd
    logit = jnp.concatenate([item[1:2, :units] for item in blocks_in], 1)
    unit_ref[0:1, :] = jnp.concatenate([item[0:1, :units] for item in blocks_in], 1)
    unit_ref[1:2, :] = gate(logit, noise_ref[...])
    unit_ref[2:3, :] = jnp.broadcast_to(
        jnp.sum(keep_score(logit), 1, keepdims=True), logit.shape
    )
    vbias_ref[...] = jnp.concatenate([item[2:3, :biases] for item in blocks_in], 1)

    def up_down(b):
        pre = (
            jnp.dot(gathered(rows, b), up_w(), preferred_element_type=full)
            + unit_ref[0:1, :]
        )
        hpre[lines(b), :] = pre
        hidden = (jax.nn.gelu(pre) * unit_ref[1:2, :]).astype(low)
        hid[lines(b), :] = hidden
        put_part(
            b,
            lax.dot_general(
                hidden, down_w(), (((1,), (1,)), ((), ())), preferred_element_type=full
            ),
        )

    loop(own_blocks, up_down)
    reduces[0].start(1)
    gathers[0].wait_rest()
    loop(far_blocks, up_down)
    reduces[0].start(0)
    for one in parts_in[3:]:
        one.finish(0)
        one.start(1)
    reduces[0].middle()
    ffn_res = reduces[0].finish() + vec(7)
    final_in = middle + ffn_res * vec(14)
    final = layer_norm(final_in, vec(8), vec(9))
    picked = final.astype(low)
    trans_pre = jnp.dot(picked, wt_ref[...], preferred_element_type=full) + vec(10)
    trans_gelu = jax.nn.gelu(trans_pre)
    trans[me] = layer_norm(trans_gelu, vec(11), vec(12)).astype(low)
    gathers[1].start()
    gathers[0].finish()
    gathers[1].forward()
    for one in parts_in[3:]:
        one.finish(1)
    tab_copy.wait()
    gathers[1].wait_half()

    def head(b):
        these = gathered(trans, b)
        t_top = tmax[lines(b), :1]

        def one(v, carry):
            s_max, s_sum, t_sum, cross = carry
            logits = (
                jnp.dot(these, table_tile(v), preferred_element_type=full)
                + vbias_ref[:, columns(v)]
            ) / TEMPER
            student[lines(b), columns(v)] = logits
            teach = teach_ref[lines(b), columns(v)].astype(full) / TEMPER
            top = jnp.maximum(s_max, jnp.max(logits, 1, keepdims=True))
            s_sum = s_sum * jnp.exp(s_max - top) + jnp.sum(
                jnp.exp(logits - top), 1, keepdims=True
            )
            t_exp = jnp.exp(teach - t_top)
            t_sum = t_sum + jnp.sum(t_exp, 1, keepdims=True)
            cross = cross + jnp.sum(t_exp * (teach - logits), 1, keepdims=True)
            return top, s_sum, t_sum, cross

        zero = jnp.zeros((block, 1), full)
        s_max, s_sum, t_sum, cross = lax.fori_loop(
            0, tiles, one, (jnp.full((block, 1), -1e30, full), zero, zero, zero)
        )
        lane = lax.broadcasted_iota(jnp.int32, (block, 128), 1)
        packed = jnp.where(lane == 0, s_max, unit_ref[2:3, 0:1])
        for k, item in ((1, s_sum), (2, t_top), (3, t_sum), (4, cross)):
            packed = jnp.where(lane == k, item, packed)
        statc[lines(b), :] = packed

    loop(own_blocks, head)
    gathers[1].wait_rest()
    loop(far_blocks, head)
    stats[me] = jnp.swapaxes(statc[...], 0, 1)[:8]

    def stat_copy(peer, slot):
        return pltpu.make_async_remote_copy(
            src_ref=stats.at[me],
            dst_ref=stats.at[slot],
            send_sem=stat_send.at[peer],
            recv_sem=stat_recv.at[slot],
            device_id={"unit": peer},
            device_id_type=MESH,
        )

    def stat_wait(j):
        peer = lax.rem(me + j, n)
        stat_copy(peer, me).wait_send()
        stat_copy(peer, peer).wait_recv()

    loop((1, n), lambda j: stat_copy(lax.rem(me + j, n), me).start())
    gathers[1].finish()
    loop((1, n), stat_wait)
    s_top, t_top = stats[0, 0:1], stats[0, 2:3]
    for k in range(1, n):
        s_top = jnp.maximum(s_top, stats[k, 0:1])
        t_top = jnp.maximum(t_top, stats[k, 2:3])
    s_all = t_all = cross_all = jnp.zeros_like(s_top)
    unit_all = jnp.zeros((1, 1), full)
    for k in range(n):
        s_all = s_all + stats[k, 1:2] * jnp.exp(stats[k, 0:1] - s_top)
        scale = jnp.exp(stats[k, 2:3] - t_top)
        t_all = t_all + stats[k, 3:4] * scale
        cross_all = cross_all + stats[k, 4:5] * scale
        unit_all = unit_all + stats[k, 5:6, 0:1]
    lse_student = s_top + jnp.log(s_all)
    lse_teach = t_top + jnp.log(t_all)
    kl_rows = cross_all / t_all - lse_teach + lse_student
    place = lax.broadcasted_iota(jnp.int32, kl_rows.shape, 1)
    is_own = jnp.logical_and(place >= me * count, place < (me + 1) * count)
    kl_own = jnp.sum(jnp.where(is_own, kl_rows, 0.0), 1, keepdims=True)
    line = lax.broadcasted_iota(jnp.int32, (8, 128), 0)
    stat_out[...] = jnp.where(line == 0, kl_own, unit_all)
    both = jnp.where(
        lax.broadcasted_iota(jnp.int32, (8, n * count), 0) == 0, lse_student, lse_teach
    )
    statc[:, :8] = jnp.swapaxes(both, 0, 1)

    gvbias[...] = jnp.zeros_like(gvbias)

    def head_back(b):
        acc[...] = jnp.zeros_like(acc)
        from_student, from_teach = statc[lines(b), 0:1], statc[lines(b), 1:2]

        def one(v):
            teach = teach_ref[lines(b), columns(v)].astype(full) / TEMPER
            grad = (
                TEMPER
                / npos
                * (
                    jnp.exp(student[lines(b), columns(v)] - from_student)
                    - jnp.exp(teach - from_teach)
                )
            )
            gvbias[:, columns(v)] += row_sum(grad)
            grad_low = grad.astype(low)
            glow[lines(b), columns(v)] = grad_low
            acc[...] += lax.dot_general(
                grad_low,
                table_tile(v),
                (((1,), (1,)), ((), ())),
                preferred_element_type=full,
            )

        loop((0, tiles), one)
        put_part(b, acc[...])

    loop(far_blocks, head_back)
    reduces[1].start(0)
    loop(own_blocks, head_back)
    reduces[1].start(1)
    reduces[1].middle()

    for v in range(tiles):
        gtable[v] = (
            contract_rows(
                trans[...].reshape(n * count, width), glow[:, v * tile : (v + 1) * tile]
            )
            .astype(low)
            .reshape(gtable.shape[1:])
        )
        table_reduces[v].start(0)
    grad_trans = reduces[1].finish()
    grad_tgelu, grad_hgain, grad_hshift = norm_back(trans_gelu, vec(11), vec(12), grad_trans)
    grad_tpre = gelu_back(trans_pre, grad_tgelu)
    grad_tpre_low = grad_tpre.astype(low)
    grad_final = lax.dot_general(
        grad_tpre_low, wt_ref[...], (((1,), (1,)), ((), ())), preferred_element_type=full
    )
    grad_final_in, grad_gain2, grad_shift2 = norm_back(final_in, vec(8), vec(9), grad_final)
    grad_fres = grad_final_in * vec(14)
    backs[me] = grad_fres.astype(low)
    gathers[2].start()
    gvecs[0:7, :] = jnp.zeros((7, width), full)
    gvecs[7:8, :] = row_sum(grad_fres)
    gvecs[8:9, :] = grad_gain2
    gvecs[9:10, :] = grad_shift2
    gvecs[10:11, :] = row_sum(grad_tpre)
    gvecs[11:12, :] = grad_hgain
    gvecs[12:13, :] = grad_hshift
    gvecs[13:14, :] = row_sum(grad_final_in * ffn_res)
    gvecs[14:16, :] = jnp.zeros((2, width), full)
    gwt[...] = contract_rows(picked, grad_tpre_low).astype(low)
    for table_reduce in table_reduces:
        table_reduce.finish(0)
        table_reduce.start(1)
    gathers[2].forward()
    gathers[2].wait_half()
    gunit[...] = jnp.zeros_like(gunit)

    def up_down_back(b):
        grad_hidden = jnp.dot(gathered(backs, b), down_w(), preferred_element_type=full)
        pre = hpre[lines(b), :]
        gunit[1:2, :] += row_sum(grad_hidden * jax.nn.gelu(pre))
        grad_pre = gelu_back(pre, grad_hidden * unit_ref[1:2, :])
        gunit[0:1, :] += row_sum(grad_pre)
        grad_pre_low = grad_pre.astype(low)
        ghp[lines(b), :] = grad_pre_low
        put_part(
            b,
            lax.dot_general(
                grad_pre_low, up_w(), (((1,), (1,)), ((), ())), preferred_element_type=full
            ),
        )

    loop(own_blocks, up_down_back)
    reduces[2].start(1)
    gathers[2].wait_rest()
    loop(far_blocks, up_down_back)
    reduces[2].start(0)
    gup[...] = contract_rows(rows[...].reshape(n * count, width), ghp[...]).astype(low)
    reduces[2].middle()
    gdown[...] = contract_rows(backs[...].reshape(n * count, width), hid[...]).astype(low)
    grad_logit = gate_back(logit, noise_ref[...], gunit[1:2, :])
    small_out[...] = jnp.zeros_like(small_out)
    for d in range(nd):
        cut, wide = slice(d * units, (d + 1) * units), slice(d * biases, (d + 1) * biases)
        small_out[d, 0:1, :units] = gunit[0:1, :][:, cut].astype(low)
        small_out[d, 1:2, :units] = grad_logit[:, cut].astype(low)
        small_out[d, 2:3, :biases] = gvbias[...][:, wide].astype(low)
    gmid[...] = grad_final_in + reduces[2].finish()
    gathers[2].finish()
    for table_reduce in table_reduces:
        table_reduce.finish(1)


def mid_step(
    middle, ffn, pack, noise, own, tab_in, teach, w_trans, vec_rows, n, nd, npos, collective
):
    count, width = middle.shape
    vocab, units = own.shape[1], ffn.shape[2]
    low, full = jnp.bfloat16, jnp.float32
    rows = n * count
    inner = n // 2
    blocks = pltpu.VMEM((n, count, width), low)
    one = pltpu.VMEM((count, width), low)
    tile = tile_of(vocab)
    tiles = vocab // tile
    late = tiles - early_tiles(vocab)
    grid = (1, 1, *grid_of(n, nd)[2:])
    helds, sums = reduce_scratch(grid, [DP_ORDER] * tiles, [(width // nd, tile)] * tiles)
    dp_scratch = []
    for v in range(tiles):
        dp_scratch += [helds[2 * v], helds[2 * v + 1], sums[v]]
    return pl.pallas_call(
        functools.partial(mid_kernel, n, nd, npos),
        out_shape=(
            jax.ShapeDtypeStruct((tiles, width // nd, tile), full),
            jax.ShapeDtypeStruct((nd, *pack.shape), low),
            jax.ShapeDtypeStruct((width, units), low),
            jax.ShapeDtypeStruct((width, units), low),
            jax.ShapeDtypeStruct((width, width), low),
            jax.ShapeDtypeStruct((count, width), full),
            jax.ShapeDtypeStruct((16, width), full),
            jax.ShapeDtypeStruct((8, 128), full),
        ),
        in_specs=[on_chip()] * 5 + [pl.BlockSpec(memory_space=pl.ANY)] + [on_chip()] * 3,
        out_specs=(on_chip(),) * 8,
        scratch_shapes=[
            pltpu.VMEM((8, units), full),
            blocks,
            blocks,
            blocks,
            pltpu.VMEM((rows, units), full),
            pltpu.VMEM((rows, units), low),
            pltpu.VMEM((rows, units), low),
            pltpu.VMEM((rows, vocab), full),
            pltpu.VMEM((rows, vocab), low),
            pltpu.VMEM((max(256, count), width), full),
            pltpu.VMEM((rows, 128), full),
            pltpu.VMEM((rows, 128), full),
            pltpu.VMEM((n, 8, rows), full),
            blocks,
            one,
            *[pltpu.VMEM((2, inner - 1, count, width), low)] * 3,
            *[one] * 3,
            pltpu.SemaphoreType.DMA((3, 2, inner)),
            pltpu.SemaphoreType.DMA((3, n)),
            pltpu.SemaphoreType.DMA((3, 2, inner)),
            pltpu.SemaphoreType.DMA((3, 2, inner)),
            pltpu.SemaphoreType.DMA((n,)),
            pltpu.SemaphoreType.DMA((n,)),
            pltpu.VMEM((tiles, *grid, width // nd, tile), low),
            pltpu.SemaphoreType.DMA((tiles, 2, max(grid))),
            pltpu.SemaphoreType.DMA((tiles, 2, max(grid))),
            pltpu.VMEM((tiles, *grid, width // nd, tile), low),
            pltpu.VMEM((2, *grid, *ffn.shape[1:]), low),
            pltpu.VMEM((*grid, *pack.shape), low),
            pltpu.VMEM((1, vocab), full),
            pltpu.VMEM((1, vocab), full),
            pltpu.VMEM((8, units), full),
            pltpu.SemaphoreType.DMA((3 + late, 2, max(grid))),
            pltpu.SemaphoreType.DMA((3 + late, 2, max(grid))),
            pltpu.SemaphoreType.DMA,
            *dp_scratch,
        ],
        compiler_params=call_params(collective),
    )(middle, ffn, pack, noise, own, tab_in, teach, w_trans, vec_rows)


def split_low(values):
    parts = []
    for _ in range(3):
        part = values.astype(jnp.bfloat16)
        parts.append(part)
        values = values - part.astype(jnp.float32)
    return parts


def picked_lines(pos_ref, seq):
    count = pos_ref.shape[0]
    return pos_ref[...] == lax.broadcasted_iota(jnp.int32, (count, seq), 1)


def per_head(values, heads):
    rows, width = values.shape
    size = width // heads
    shape = (heads, rows, width)
    lane = lax.broadcasted_iota(jnp.int32, shape, 2) // size
    keep = lane == lax.broadcasted_iota(jnp.int32, shape, 0)
    return jnp.where(keep, jnp.broadcast_to(values[None], shape), 0.0).reshape(
        heads * rows, width
    )


def from_heads(values, heads):
    total, width = values.shape
    size = width // heads
    shape = (heads, total // heads, width)
    lane = lax.broadcasted_iota(jnp.int32, shape, 2) // size
    keep = lane == lax.broadcasted_iota(jnp.int32, shape, 0)
    return jnp.sum(jnp.where(keep, values.reshape(shape), 0.0), 0)


def mask_row(scal):
    return scal[0:1, :].astype(jnp.bfloat16).astype(jnp.float32)


def attend_kernel(heads, cap, *refs):
    (
        words_ref,
        extra_ref,
        code_ref,
        pos_ref,
        seg_ref,
        noise_ref,
        scal,
        pos_vecs,
        w_q,
        w_k,
        w_v,
        w_out,
    ) = refs[:12]
    middle_ref, gates_ref = refs[12:14]
    vecs, embed_ref, start_ref, keys, values, queries, probs_ref, small = refs[14:]
    low, full = jnp.bfloat16, jnp.float32
    seq, width = embed_ref.shape
    nd, nu = words_ref.shape[:2]
    part = width // nd
    count = pos_ref.shape[0]
    n_vecs = 14
    turned = jnp.swapaxes(pos_vecs[:, seq:].astype(full), 0, 1)
    vecs[...] = turned[:16]
    zhid = gate(vecs[13:14, :], noise_ref[...])
    open_masks = gate(mask_row(scal), scal[1:2, :])
    of_head = lax.broadcasted_iota(jnp.int32, (1, width), 1) // (width // heads)
    zcols = jnp.zeros((1, width), full)
    for h in range(heads):
        zcols = jnp.where(of_head == h, open_masks[:, h : h + 1], zcols)
    gates_ref[0:1, :] = zcols
    gates_ref[1:2, :] = jnp.broadcast_to(open_masks[:, heads : heads + 1], (1, width))
    gates_ref[2:8, :] = jnp.broadcast_to(open_masks[:, heads + 1 : heads + 2], (6, width))
    zmlp_hid = gates_ref[2:3, :] * zhid
    vecs[n_vecs : n_vecs + 1, :] = zmlp_hid
    vecs[n_vecs + 1 : n_vecs + 2, :] = zhid

    def vec(k):
        return vecs[k : k + 1, :]

    found = jnp.zeros((nu * cap, width), full)
    for d in range(nd):
        found = found + unpack_rows(words_ref.at[d], cap, width, d * part, part)
    spread = jnp.where(
        code_ref[...] == lax.broadcasted_iota(jnp.int32, (seq, nu * cap), 1), 1.0, 0.0
    ).astype(low)
    embed = (
        product(spread, found.astype(low))
        + extra_ref[...].astype(full)
        + jnp.swapaxes(pos_vecs[:, :seq].astype(full), 0, 1)
    )
    embed_ref[...] = embed
    start = layer_norm(embed, vec(0), vec(1)) * zhid
    start_low = start.astype(low)
    start_ref[...] = start_low
    pick_mask = picked_lines(pos_ref, seq)
    pick = jnp.where(pick_mask, 1.0, 0.0).astype(low)
    start_p = sum(product(pick, item) for item in split_low(start))
    start_p_low = start_p.astype(low)
    query = (product(start_p_low, w_q[...]) + vec(2)).astype(low)
    keys[...] = product(start_low, w_k[...]).astype(low)
    values[...] = (product(start_low, w_v[...]) + vec(3)).astype(low)
    queries[...] = query
    seg = seg_ref[...]
    seg_p = jnp.sum(jnp.where(pick_mask, seg, 0), 1, keepdims=True)
    same = jnp.broadcast_to((seg_p == seg)[None], (heads, count, seq)).reshape(
        heads * count, seq
    )
    scale = (width // heads) ** (-0.5)
    scores = (
        product(per_head(query.astype(full), heads).astype(low), keys[...], 1, 1) * scale
    )
    scores = jnp.where(same, scores, -1000000000.0)
    lifted = jnp.exp(scores - jnp.max(scores, 1, keepdims=True))
    probs = lifted / jnp.sum(lifted, 1, keepdims=True)
    probs_ref[...] = probs
    context = from_heads(product(probs.astype(low), values[...]), heads)
    scaled = (context * gates_ref[0:1, :]).astype(low)
    attn_res = product(scaled, w_out[...]) + vec(4)
    middle_in = start_p + attn_res * gates_ref[1:2, :] * zhid
    middle_ref[...] = layer_norm(middle_in, vec(5), vec(6))
    small[0] = start_p
    small[1] = context
    small[2] = attn_res
    small[3] = middle_in


def attend_step(heads, cap, words, extra, code, pos, seg, noise, scal, pos_vecs, maps):
    low, full = jnp.bfloat16, jnp.float32
    seq, width = extra.shape
    count = pos.shape[0]
    return pl.pallas_call(
        functools.partial(attend_kernel, heads, cap),
        out_shape=(
            jax.ShapeDtypeStruct((count, width), full),
            jax.ShapeDtypeStruct((8, width), full),
            jax.ShapeDtypeStruct((16, width), full),
            jax.ShapeDtypeStruct((seq, width), full),
            jax.ShapeDtypeStruct((seq, width), low),
            jax.ShapeDtypeStruct((seq, width), low),
            jax.ShapeDtypeStruct((seq, width), low),
            jax.ShapeDtypeStruct((count, width), low),
            jax.ShapeDtypeStruct((heads * count, seq), full),
            jax.ShapeDtypeStruct((4, count, width), full),
        ),
        in_specs=[on_chip()] * 12,
        out_specs=(on_chip(),) * 10,
        compiler_params=pltpu.CompilerParams(vmem_limit_bytes=VMEM_LIMIT),
    )(words, extra, code, pos, seg, noise, scal, pos_vecs, *maps)


def attend_back_kernel(heads, nd, cap, ffn_width, *refs):
    (
        gmid_ref,
        mid_vecs,
        vecs,
        embed_ref,
        start_ref,
        keys,
        values,
        queries,
        probs_ref,
        small,
        code_ref,
        pos_ref,
        noise_ref,
        gates_ref,
        scal,
        mid_stats,
        w_q,
        w_k,
        w_v,
        w_out,
    ) = refs[:20]
    g_q, g_k, g_v, g_out, g_last, sent, low_embed, info, lines = refs[20:]
    low, full = jnp.bfloat16, jnp.float32
    seq, width = embed_ref.shape
    nu, part = sent.shape[1], width // nd

    def vec(k):
        return vecs[k : k + 1, :]

    zhid = vec(15)
    zcols, zmha = gates_ref[0:1, :], gates_ref[1:2, :]
    start_p, context, attn_res, middle_in = small[0], small[1], small[2], small[3]
    grad_middle_in, grad_gain1, grad_shift1 = norm_back(middle_in, vec(5), vec(6), gmid_ref[...])
    grad_ares = grad_middle_in * zmha * zhid
    grad_ares_low = grad_ares.astype(low)
    through = row_sum(grad_middle_in * attn_res)
    scaled = (context * zcols).astype(low)
    g_out[...] = contract_rows(scaled, grad_ares_low).astype(low)
    grad_scaled = product(grad_ares_low, w_out[...], 1, 1)
    lane = lax.broadcasted_iota(jnp.int32, (1, 128), 1)
    of_head = lax.broadcasted_iota(jnp.int32, (1, width), 1) // (width // heads)
    head_terms = row_sum(grad_scaled * context)
    grad_open = jnp.zeros((1, 128), full)
    for h in range(heads):
        one = jnp.sum(jnp.where(of_head == h, head_terms, 0.0), 1, keepdims=True)
        grad_open = jnp.where(lane == h, one, grad_open)
    for k, terms in ((heads, through * zhid), (heads + 1, mid_vecs[13:14, :] * zhid)):
        grad_open = jnp.where(lane == k, jnp.sum(terms, 1, keepdims=True), grad_open)
    masks = mask_row(scal)
    grad_masks = gate_back(masks, scal[1:2, :], grad_open)
    scores = keep_score(masks)
    mha, mlp = scores[:, heads : heads + 1], scores[:, heads + 1 : heads + 2]
    plain_heads = jnp.sum(jnp.where(lane < heads, scores, 0.0), 1, keepdims=True)
    hid_sum = jnp.sum(keep_score(vec(13)), 1, keepdims=True)
    unit_score = mid_stats[1:2, 0:1]
    full_size = 4.0 * width * width + 2.0 * width * ffn_width
    per_head_size = 4.0 * (width // heads)
    head_sum, unit_sum = plain_heads * mha, unit_score * mlp
    kept_share = (per_head_size * hid_sum * head_sum + 2.0 * hid_sum * unit_sum) / full_size
    over = 1.0 - kept_share - TARGET
    first_mult, second_mult = scal[2:3, 0:1], scal[2:3, 1:2]
    slope = -(first_mult + 2.0 * second_mult * over) / full_size
    lag = slope * per_head_size * hid_sum * jnp.where(lane < heads, mha, plain_heads)
    lag = jnp.where(lane == heads + 1, slope * 2.0 * hid_sum * unit_score, lag)
    lag = jnp.where(lane < heads + 2, lag * score_slope(masks), 0.0)
    info[...] = jnp.zeros_like(info)
    info[0:1, :] = jnp.where(
        lane < heads + 2, grad_masks, jnp.where(lane == heads + 2, mid_stats[0:1, :], 0.0)
    )
    info[1:2, :] = lag
    for k, item in (
        (2, slope * (per_head_size * head_sum + 2.0 * unit_sum)),
        (3, slope * 2.0 * hid_sum * mlp),
        (4, kept_share),
        (5, first_mult * over + second_mult * over * over),
    ):
        info[k : k + 1, :] = jnp.broadcast_to(item, (1, 128))
    grad_context = per_head((grad_scaled * zcols).astype(low).astype(full), heads).astype(low)
    scale = (width // heads) ** (-0.5)
    probs = probs_ref[...]
    grad_probs = product(grad_context, values[...], 1, 1)
    grad_scores = (
        probs * (grad_probs - jnp.sum(grad_probs * probs, 1, keepdims=True))
    ).astype(low)
    grad_q = (from_heads(product(grad_scores, keys[...]), heads) * scale).astype(low)
    grad_k = (
        contract_rows(grad_scores, per_head(queries[...].astype(full), heads).astype(low)) * scale
    ).astype(low)
    grad_v = contract_rows(probs.astype(low), grad_context).astype(low)
    start_low = start_ref[...]
    g_q[...] = contract_rows(start_p.astype(low), grad_q).astype(low)
    g_k[...] = contract_rows(start_low, grad_k).astype(low)
    g_v[...] = contract_rows(start_low, grad_v).astype(low)
    grad_start_p = grad_middle_in + product(grad_q, w_q[...], 1, 1)
    pick = jnp.where(picked_lines(pos_ref, seq), 1.0, 0.0).astype(low)
    grad_start = (
        sum(contract_rows(pick, item) for item in split_low(grad_start_p))
        + product(grad_k, w_k[...], 1, 1)
        + product(grad_v, w_v[...], 1, 1)
    )
    embed = embed_ref[...]
    center = embed - jnp.mean(embed, 1, keepdims=True)
    unit_norm = center * lax.rsqrt(jnp.mean(center * center, 1, keepdims=True) + EPS_NORM)
    start_norm = unit_norm * vec(0) + vec(1)
    grad_zhid = (
        mid_vecs[13:14, :] * gates_ref[2:3, :]
        + through * zmha
        + row_sum(grad_start * start_norm)
    )
    grad_embed, grad_gain0, grad_shift0 = norm_back(embed, vec(0), vec(1), grad_start * zhid)
    embed_low = grad_embed.astype(low)
    low_embed[...] = embed_low
    match = jnp.where(
        code_ref[...] == lax.broadcasted_iota(jnp.int32, (nu * cap, seq), 0), 1.0, 0.0
    ).astype(low)
    gathered = product(match, embed_low).astype(low)
    for d in range(nd):
        head, tails = pack_rows(gathered, nu, cap, width, d * part, part)
        sent[d, :, :cap] = head
        for tail in tails:
            sent[d, :, cap:] = tail
    lines[...] = jnp.zeros_like(lines)
    items = (
        grad_gain0,
        grad_shift0,
        row_sum(grad_q.astype(full)),
        row_sum(grad_v.astype(full)),
        row_sum(grad_ares),
        grad_gain1,
        grad_shift1,
    )
    for k, item in enumerate(items):
        lines[k : k + 1, :] = item.reshape(1, width)
    lines[7:13, :] = mid_vecs[7:13, :]
    lines[13:14, :] = gate_back(vec(13), noise_ref[...], grad_zhid)
    g_last[:, :seq] = jnp.swapaxes(grad_embed, 0, 1).astype(low)
    g_last[:, seq:] = jnp.swapaxes(lines[...], 0, 1).astype(low)


def attend_back_step(
    heads, nd, nu, cap, ffn_width, gmid, mid_vecs, kept, code, pos, noise, gates, scal, stats, maps
):
    low, full = jnp.bfloat16, jnp.float32
    seq, width = kept[1].shape
    square = jax.ShapeDtypeStruct((width, width), low)
    return pl.pallas_call(
        functools.partial(attend_back_kernel, heads, nd, cap, ffn_width),
        out_shape=(
            square,
            square,
            square,
            square,
            jax.ShapeDtypeStruct((width, seq + 128), low),
            jax.ShapeDtypeStruct((nd, nu, *packed_shape(cap, width // nd)), low),
            jax.ShapeDtypeStruct((seq, width), low),
            jax.ShapeDtypeStruct((8, 128), full),
        ),
        in_specs=[on_chip()] * 20,
        out_specs=(on_chip(),) * 8,
        scratch_shapes=[pltpu.VMEM((128, width), full)],
        compiler_params=pltpu.CompilerParams(vmem_limit_bytes=VMEM_LIMIT),
    )(gmid, mid_vecs, *kept, code, pos, noise, gates, scal, stats, *maps)


def adamw(weight, first, second, grad, rate, count):
    first = BETA_ONE * first + (1.0 - BETA_ONE) * grad
    second = BETA_TWO * second + (1.0 - BETA_TWO) * grad * grad
    first_hat = first / (1.0 - BETA_ONE**count)
    second_hat = second / (1.0 - BETA_TWO**count)
    return weight - rate * (first_hat / (jnp.sqrt(second_hat) + ADAM_EPS) + DECAY * weight)


def on_device(
    token_ids,
    segments,
    positions,
    teacher,
    gate_noise,
    unit_noise,
    multipliers,
    step_count,
    layer_mats,
    mats_first,
    mats_second,
    layer_vecs,
    vecs_first,
    vecs_second,
    ffn_mats,
    ffn_first,
    ffn_second,
    unit_vecs,
    unit_first,
    unit_second,
    word_table,
    table_first,
    table_second,
    word_bias,
    bias_first,
    bias_second,
    mask_logits,
    mask_first,
    mask_second,
):
    low_type = jnp.bfloat16
    full_type = jnp.float32
    exact = lax.Precision.HIGHEST
    units_n = lax.axis_size("unit")
    groups_n = lax.axis_size("dp")
    everyone = ("unit", "dp")
    heads = mask_logits.shape[0] - 2
    share_rows = layer_mats.shape[0]
    width = share_rows * units_n * groups_n
    head_size = width // heads
    seq_len = segments.shape[2]
    nmask = positions.shape[2]
    unit_idx = lax.axis_index("unit")
    n_vecs = layer_vecs.shape[0]
    vec_pad = -n_vecs % 128
    table_turned = word_table.T
    vocab_slice = word_table.shape[0]
    table_part = word_table.shape[1]
    cap = 16 * -(-seq_len // (16 * units_n))

    count = step_count[0].astype(full_type)
    n_masks = heads + 2

    def line_of(values, rest=0.0):
        return jnp.pad(values, (0, 128 - values.shape[0]), constant_values=rest)

    scal = jnp.concatenate(
        [
            line_of(mask_logits)[None],
            line_of(gate_noise[width:], 0.5)[None],
            line_of(multipliers)[None],
            line_of(jnp.stack([1.0 - BETA_ONE**count, 1.0 - BETA_TWO**count]))[None],
            jnp.zeros((4, 128), full_type),
        ],
        0,
    )
    vec_own = jnp.pad(layer_vecs.T, ((0, 0), (0, vec_pad)))

    mats_low = layer_mats.astype(low_type)
    trans_end = 5 * width
    table_low = table_turned.astype(low_type)
    map_parts = [mats_low[:, k * width : (k + 1) * width] for k in range(5)] + [
        jnp.concatenate(
            [
                mats_low[:, trans_end:],
                vec_own.astype(low_type),
            ],
            1,
        )
    ]
    pack_lanes = 128 * -(-max(unit_vecs.shape[1], word_bias.shape[0]) // 128)
    small_pack = jnp.concatenate(
        [
            jnp.pad(unit_vecs, ((0, 0), (0, pack_lanes - unit_vecs.shape[1]))),
            jnp.pad(word_bias, (0, pack_lanes - word_bias.shape[0]))[None],
            jnp.zeros((13, pack_lanes), full_type),
        ],
        0,
    )
    ids = lax.dynamic_index_in_dim(token_ids[0], unit_idx, 0, keepdims=False)
    place = jnp.arange(seq_len, dtype=jnp.int32)
    same_id = ids[:, None] == ids[None, :]
    first_place = jnp.min(jnp.where(same_id, place[None, :], seq_len), 1)
    is_first = first_place == place
    owner = ids // vocab_slice
    slot = jnp.sum(
        (
            is_first[None, :]
            & (owner[None, :] == owner[:, None])
            & (place[None, :] < first_place[:, None])
        ).astype(jnp.int32),
        1,
    )
    slots_used = jnp.max(slot) + 1
    local_id = ids - owner * vocab_slice
    entry = jnp.arange(units_n * cap, dtype=jnp.int32)

    def round_code(k):
        here = slot - k * cap
        return jnp.where((here >= 0) & (here < cap), owner * cap + here, -1)

    def round_match(k):
        return entry[:, None] == round_code(k)[None, :]

    def round_wanted(match):
        return jnp.max(
            jnp.where(match & is_first[None, :], local_id[None, :], -1), 1
        ).reshape(units_n, cap)

    match_0 = round_match(0)
    wanted_0 = jnp.concatenate(
        [
            round_wanted(match_0),
            jnp.broadcast_to(slots_used, (units_n, 128 - cap)),
        ],
        1,
    )[:, None, :]
    fetched, asked, *maps = fetch_rows(
        wanted_0, table_low, map_parts, units_n, groups_n, cap, 1
    )
    *maps, table_early = maps
    w_q, w_k, w_v, w_out, w_trans, pos_vecs = [part.reshape(width, -1) for part in maps]
    asked = asked[:, 0, :]
    rounds = (jnp.max(asked[:, cap:]) + cap - 1) // cap
    code_0 = round_code(0)

    def spread(match, parts):
        return jnp.concatenate(
            [
                contract_rows(match, parts[d].reshape(units_n * cap, table_part))
                for d in range(groups_n)
            ],
            1,
        )

    def round_asked(match):
        wanted_all = lax.all_gather(round_wanted(match), everyone, axis=0)
        return lax.dynamic_index_in_dim(wanted_all, unit_idx, 1, keepdims=False)

    def more_words(k, words):
        match = round_match(k)
        mine = round_asked(match)
        found = jnp.where(
            (mine >= 0)[:, :, None],
            jnp.moveaxis(jnp.take(table_low, jnp.maximum(mine, 0), axis=1), 0, 2),
            0,
        )
        found = lax.all_to_all(found, everyone, 0, 0, tiled=True)
        found = jnp.swapaxes(
            found.reshape(units_n, groups_n, cap, table_part), 0, 1
        )
        return words + spread(match.astype(low_type), found).astype(low_type)

    extra = lax.fori_loop(1, rounds, more_words, jnp.zeros((seq_len, width), low_type))

    noise_hid = gate_noise[:width][None]
    picks = positions.reshape(-1, 1)
    middle, gates, vec_rows, *kept_rows = attend_step(
        heads,
        cap,
        fetched,
        extra,
        code_0[:, None],
        picks,
        segments.reshape(1, -1),
        noise_hid,
        scal,
        pos_vecs,
        (w_q, w_k, w_v, w_out),
    )
    slice_units = unit_vecs.shape[1] * groups_n
    ffn_width = slice_units * units_n
    noise_units = lax.dynamic_slice_in_dim(unit_noise, unit_idx * slice_units, slice_units, 0)
    npos = groups_n * units_n * nmask
    (
        share_head,
        small_grads,
        grad_up,
        grad_down,
        grad_wtrans,
        grad_middle,
        mid_vecs,
        mid_stats,
    ) = mid_step(
        middle,
        ffn_mats,
        small_pack,
        noise_units[None],
        table_low,
        table_early,
        teacher.reshape(-1, vocab_slice),
        w_trans,
        vec_rows,
        units_n,
        groups_n,
        npos,
        2,
    )
    grad_wq, grad_wk, grad_wv, grad_wout, grad_last, word_grads, embed_low, info = (
        attend_back_step(
            heads,
            groups_n,
            units_n,
            cap,
            ffn_width,
            grad_middle,
            mid_vecs,
            (vec_rows, *kept_rows),
            code_0[None],
            picks,
            noise_hid,
            gates,
            scal,
            mid_stats,
            (w_q, w_k, w_v, w_out),
        )
    )
    def word_parts(match):
        return jnp.stack(
            [
                jnp.dot(
                    match,
                    embed_low[:, d * table_part : (d + 1) * table_part],
                    preferred_element_type=full_type,
                )
                .astype(low_type)
                .reshape(units_n, cap, table_part)
                for d in range(groups_n)
            ]
        )

    def more_grads(k, total):
        match = round_match(k)
        mine = round_asked(match).reshape(-1)
        back = jnp.swapaxes(word_parts(match.astype(low_type)), 0, 1).reshape(
            units_n * groups_n, cap, table_part
        )
        back = lax.all_to_all(back, everyone, 0, 0, tiled=True).reshape(-1, table_part)
        target = jnp.where(mine >= 0, mine, vocab_slice)
        added = total.astype(full_type).at[:, target].add(
            back.T.astype(full_type), mode="drop"
        )
        return added.astype(low_type)

    more = lax.fori_loop(
        1, rounds, more_grads, jnp.zeros((table_part, vocab_slice), low_type)
    )

    share_table, totals, *shares = return_rows(
        word_grads,
        asked,
        share_head,
        more,
        vec_own,
        small_pack,
        info,
        (grad_wq, grad_wk, grad_wv, grad_wout, grad_wtrans, grad_last),
        (grad_up, grad_down, small_grads.reshape(-1, pack_lanes)),
        unit_vecs.shape[1],
        cap,
        units_n,
        groups_n,
        9,
    )
    news = update_step(
        heads,
        npos,
        totals,
        info,
        scal,
        shares,
        share_table,
        [
            (layer_mats, mats_first, mats_second),
            (layer_vecs, vecs_first, vecs_second),
            (ffn_mats, ffn_first, ffn_second),
            (unit_vecs, unit_first, unit_second),
            (word_bias[None], bias_first[None], bias_second[None]),
            (mask_logits[None], mask_first[None], mask_second[None]),
        ],
        (table_turned, table_first.T, table_second.T),
    )
    mats_new, mats_grad, vecs_new, vecs_grad, ffn_new, ffn_grad, unit_new, unit_grad = news[:8]
    bias_new, bias_grad, mask_new, mask_grad, stat, table_new, table_grad = news[8:]
    return (
        stat[0, 0],
        stat[1, 0],
        stat[2, 0],
        mats_new,
        mats_grad,
        vecs_new,
        vecs_grad,
        ffn_new,
        ffn_grad,
        unit_new,
        unit_grad,
        table_new.T,
        table_grad.T,
        bias_new[0],
        bias_grad[0],
        mask_new[0],
        mask_grad[0],
    )


def solution(mesh):
    return jax.shard_map(
        on_device,
        mesh=mesh,
        in_specs=(
            P("dp", None, None),
            P("dp", "unit", None),
            P("dp", "unit", None),
            P("dp", None, None, "unit"),
            P(),
            P(),
            P(),
            P(),
            P(("unit", "dp"), None),
            P(("unit", "dp"), None),
            P(("unit", "dp"), None),
            P(None, ("unit", "dp")),
            P(None, ("unit", "dp")),
            P(None, ("unit", "dp")),
            P(None, "dp", "unit"),
            P(None, "dp", "unit"),
            P(None, "dp", "unit"),
            P(None, ("unit", "dp")),
            P(None, ("unit", "dp")),
            P(None, ("unit", "dp")),
            P("unit", "dp"),
            P("unit", "dp"),
            P("unit", "dp"),
            P(("unit", "dp")),
            P(("unit", "dp")),
            P(("unit", "dp")),
            P(),
            P(),
            P(),
        ),
        out_specs=(
            P(),
            P(),
            P(),
            P(("unit", "dp"), None),
            P(("unit", "dp"), None),
            P(None, ("unit", "dp")),
            P(None, ("unit", "dp")),
            P(None, "dp", "unit"),
            P(None, "dp", "unit"),
            P(None, ("unit", "dp")),
            P(None, ("unit", "dp")),
            P("unit", "dp"),
            P("unit", "dp"),
            P(("unit", "dp")),
            P(("unit", "dp")),
            P(),
            P(),
        ),
        check_vma=False,
    )
```

```python
import functools
import math

import jax
import jax.numpy as jnp
from jax import lax
from jax.experimental import pallas as pl
from jax.experimental.pallas import tpu as pltpu
from jax.sharding import PartitionSpec as P

EPS_NORM = 1e-12
GAMMA = -0.1
ZETA = 1.1
BETA = 2.0 / 3.0
TARGET = 0.95
TEMPER = 2.0
MAX_NORM = 0.0001
BETA_ONE = 0.9
BETA_TWO = 0.999
ADAM_EPS = 1e-08
DECAY = 0.01
RATE_MATS = 0.5
RATE_VECS = 5.0
RATE_TABLE = 1.0


def rounded(values):
    return lax.optimization_barrier(values.astype(jnp.bfloat16)).astype(jnp.float32)


def layer_norm(values, gain, shift):
    center = values - jnp.mean(values, -1, keepdims=True)
    spread = jnp.mean(center * center, -1, keepdims=True)
    return center * lax.rsqrt(spread + EPS_NORM) * gain + shift


def norm_back(values, gain, shift, grad):
    _, pull = jax.vjp(layer_norm, values, gain, shift)
    return pull(grad)


def gelu_back(values, grad):
    _, pull = jax.vjp(jax.nn.gelu, values)
    return pull(grad)[0]


def gate(logit, noise):
    soft = jax.nn.sigmoid((jnp.log(noise) - jnp.log(1.0 - noise) + logit) / BETA)
    return jnp.clip(soft * (ZETA - GAMMA) + GAMMA, 0.0, 1.0)


def gate_back(logit, noise, grad):
    _, pull = jax.vjp(gate, logit, noise)
    return pull(grad)[0]


def keep_score(logit):
    return jax.nn.sigmoid(logit - BETA * math.log(-GAMMA / ZETA))


def score_slope(logit):
    score = keep_score(logit)
    return score * (1.0 - score)


def contract_rows(left, right):
    return lax.dot_general(
        left, right, (((0,), (0,)), ((), ())), preferred_element_type=jnp.float32
    )


MESH = pl.DeviceIdType.MESH
VMEM_LIMIT = 60 * 1024 * 1024


def on_chip():
    return pl.BlockSpec(memory_space=pltpu.VMEM)


def call_params(collective):
    return pltpu.CompilerParams(
        collective_id=collective, has_side_effects=True, vmem_limit_bytes=VMEM_LIMIT
    )


def greet_unit(n, me):
    barrier = pltpu.get_barrier_semaphore()

    def step(j, carry):
        pl.semaphore_signal(
            barrier, inc=1, device_id={"unit": lax.rem(me + j, n)}, device_id_type=MESH
        )
        return carry

    lax.fori_loop(1, n, step, 0)
    pl.semaphore_wait(barrier, n - 1)


def greet_all(nu, nd, me, wait=True):
    barrier = pltpu.get_barrier_semaphore()

    def step(j, carry):
        peer = lax.rem(me + j, nu * nd)
        pl.semaphore_signal(
            barrier,
            inc=1,
            device_id={"unit": peer // nd, "dp": lax.rem(peer, nd)},
            device_id_type=MESH,
        )
        return carry

    lax.fori_loop(1, nu * nd, step, 0)
    if wait:
        pl.semaphore_wait(barrier, nu * nd - 1)


def gather_kernel(n, x_ref, out_ref, send_sem, recv_sem):
    me = lax.axis_index("unit")
    greet_unit(n, me)

    def copy(peer, slot):
        return pltpu.make_async_remote_copy(
            src_ref=x_ref,
            dst_ref=out_ref.at[slot],
            send_sem=send_sem.at[peer],
            recv_sem=recv_sem.at[slot],
            device_id={"unit": peer},
            device_id_type=MESH,
        )

    def start(j, carry):
        copy(lax.rem(me + j, n), me).start()
        return carry

    def wait(j, carry):
        peer = lax.rem(me + j, n)
        copy(peer, me).wait_send()
        copy(peer, peer).wait_recv()
        return carry

    lax.fori_loop(1, n, start, 0)
    out_ref[me] = x_ref[...]
    lax.fori_loop(1, n, wait, 0)


def gather_unit(x, n, collective):
    return pl.pallas_call(
        functools.partial(gather_kernel, n),
        out_shape=jax.ShapeDtypeStruct((n,) + x.shape, x.dtype),
        in_specs=[on_chip()],
        out_specs=on_chip(),
        scratch_shapes=[pltpu.SemaphoreType.DMA((n,)), pltpu.SemaphoreType.DMA((n,))],
        compiler_params=call_params(collective),
    )(x)


def scatter_kernel(n, x_ref, out_ref, held, send_sem, recv_sem):
    me = lax.axis_index("unit")
    greet_unit(n, me)

    def copy(peer, slot):
        return pltpu.make_async_remote_copy(
            src_ref=x_ref.at[peer],
            dst_ref=held.at[slot],
            send_sem=send_sem.at[peer],
            recv_sem=recv_sem.at[slot],
            device_id={"unit": peer},
            device_id_type=MESH,
        )

    def start(j, carry):
        copy(lax.rem(me + j, n), me).start()
        return carry

    def wait(j, carry):
        peer = lax.rem(me + j, n)
        copy(peer, me).wait_send()
        copy(peer, peer).wait_recv()
        return carry

    lax.fori_loop(1, n, start, 0)
    held[me] = x_ref[me]
    lax.fori_loop(1, n, wait, 0)
    out_ref[...] = jnp.zeros_like(out_ref)

    def add(j, carry):
        out_ref[...] += held[j].astype(jnp.float32)
        return carry

    lax.fori_loop(0, n, add, 0)


def scatter_unit(x, n, collective):
    return pl.pallas_call(
        functools.partial(scatter_kernel, n),
        out_shape=jax.ShapeDtypeStruct(x.shape[1:], jnp.float32),
        in_specs=[on_chip()],
        out_specs=on_chip(),
        scratch_shapes=[
            pltpu.VMEM(x.shape, x.dtype),
            pltpu.SemaphoreType.DMA((n,)),
            pltpu.SemaphoreType.DMA((n,)),
        ],
        compiler_params=call_params(collective),
    )(x)


def total_kernel(nu, nd, x_ref, out_ref, held, send_sem, recv_sem):
    n = nu * nd
    me = lax.axis_index("unit") * nd + lax.axis_index("dp")
    greet_all(nu, nd, me)

    def copy(peer, slot):
        return pltpu.make_async_remote_copy(
            src_ref=x_ref,
            dst_ref=held.at[slot],
            send_sem=send_sem.at[peer],
            recv_sem=recv_sem.at[slot],
            device_id={"unit": peer // nd, "dp": lax.rem(peer, nd)},
            device_id_type=MESH,
        )

    def start(j, carry):
        copy(lax.rem(me + j, n), me).start()
        return carry

    def wait(j, carry):
        peer = lax.rem(me + j, n)
        copy(peer, me).wait_send()
        copy(peer, peer).wait_recv()
        return carry

    lax.fori_loop(1, n, start, 0)
    held[me] = x_ref[...]
    lax.fori_loop(1, n, wait, 0)
    out_ref[...] = jnp.zeros_like(out_ref)

    def add(j, carry):
        out_ref[...] += held[j]
        return carry

    lax.fori_loop(0, n, add, 0)


def total_all(x, nu, nd, collective):
    n = nu * nd
    return pl.pallas_call(
        functools.partial(total_kernel, nu, nd),
        out_shape=jax.ShapeDtypeStruct(x.shape, x.dtype),
        in_specs=[on_chip()],
        out_specs=on_chip(),
        scratch_shapes=[
            pltpu.VMEM((n,) + x.shape, x.dtype),
            pltpu.SemaphoreType.DMA((n,)),
            pltpu.SemaphoreType.DMA((n,)),
        ],
        compiler_params=call_params(collective),
    )(x)


def packed_shape(cap, part):
    return (cap + cap // 2, 128) if part == 192 and cap % 32 == 0 else (cap, part)


def lane_place(part, width, first):
    lines = lax.broadcasted_iota(jnp.int32, (part, width), 0) + first
    return jnp.where(
        lines == lax.broadcasted_iota(jnp.int32, (part, width), 1), 1.0, 0.0
    ).astype(jnp.bfloat16)


def half_place(width, first, upper):
    lines = lax.broadcasted_iota(jnp.int32, (128, width), 0)
    lanes = lax.broadcasted_iota(jnp.int32, (128, width), 1)
    low_end, shift = (64, first - 64) if upper else (0, first)
    inside = jnp.logical_and(lines >= low_end, lines < low_end + 64)
    return jnp.where(jnp.logical_and(inside, lines + shift == lanes), 1.0, 0.0).astype(
        jnp.bfloat16
    )


def product(left, right, left_dim=1, right_dim=0):
    return lax.dot_general(
        left,
        right,
        (((left_dim,), (right_dim,)), ((), ())),
        preferred_element_type=jnp.float32,
    )


def pack_rows(values, count, cap, width, first, part):
    full = product(values, lane_place(min(part, 128), width, first), 1, 1)
    if packed_shape(cap, part)[0] == cap:
        rest = []
        if part > 128:
            full = product(values, lane_place(part, width, first), 1, 1)
        return full.astype(jnp.bfloat16).reshape(count, cap, part), rest
    left = product(values, half_place(width, first + 128, False), 1, 1)
    right = product(values, half_place(width, first + 128, True), 1, 1)
    shape = (count, cap, 128)
    tail = left.reshape(shape)[:, : cap // 2] + right.reshape(shape)[:, cap // 2 :]
    return full.astype(jnp.bfloat16).reshape(shape), [tail.astype(jnp.bfloat16)]


def unpack_rows(ref, cap, width, first, part):
    count = ref.shape[0]
    if packed_shape(cap, part)[0] == cap:
        return product(ref[...].reshape(count * cap, part), lane_place(part, width, first))
    full = product(ref[:, :cap, :].reshape(count * cap, 128), lane_place(128, width, first))
    tail = ref[:, cap:, :].reshape(count * cap // 2, 128)
    shape = (count, cap // 2, width)
    both = jnp.concatenate(
        [
            product(tail, half_place(width, first + 128, False)).reshape(shape),
            product(tail, half_place(width, first + 128, True)).reshape(shape),
        ],
        1,
    )
    return full + both.reshape(count * cap, width)


def grid_of(nu, nd):
    ny = 2 if nu % 2 == 0 else 1
    nc = 2 if nd % 2 == 0 else 1
    return (nu // ny, ny, nd // nc, nc)


def grid_place(grid):
    unit, dp = lax.axis_index("unit"), lax.axis_index("dp")
    return (unit // grid[1], lax.rem(unit, grid[1]), dp // grid[3], lax.rem(dp, grid[3]))


def grid_device(grid, place):
    return {"unit": place[0] * grid[1] + place[1], "dp": place[2] * grid[3] + place[3]}


def loader(ref):
    return lambda: ref[...]


def column_loader(ref, first, length):
    return lambda: ref[:, first : first + length]


def low_loader(ref, *where):
    return lambda: ref[where].astype(jnp.bfloat16)


def tile_of(vocab):
    return 768 if vocab % 768 == 0 else vocab


def early_tiles(vocab):
    return min(1, vocab // tile_of(vocab))


def dp_grid(grid, place):
    return (
        (1, 1, grid[2], grid[3]),
        (0, 0, place[2], place[3]),
        lambda at: {"dp": at[2] * grid[3] + at[3]},
    )


def moved(place, axis, index):
    return tuple(index if k == axis else place[k] for k in range(4))


GATHER_ORDERS = ((0, 1, 2, 3), (0, 2, 1, 3))
REDUCE_ORDERS = ((3, 2, 1, 0), (3, 1, 2, 0))
DP_ORDER = (3, 2)
DP_GATHER = (2, 3)


class Gather:
    def __init__(self, grid, place, order, load, out, send_sem, recv_sem, device=None):
        self.grid, self.place, self.order = grid, place, order
        self.device = device or (lambda at: grid_device(grid, at))
        self.load, self.out, self.send_sem, self.recv_sem = load, out, send_sem, recv_sem

    def window(self, stage, index):
        axis = self.order[stage]
        where = []
        for k in range(4):
            if k == axis:
                where.append(pl.ds(index, 1))
            elif k in self.order[:stage]:
                where.append(pl.ds(0, self.grid[k]))
            else:
                where.append(pl.ds(self.place[k], 1))
        return self.out.at[tuple(where)]

    def copy(self, stage, hop, arriving):
        axis = self.order[stage]
        n = self.grid[axis]
        mine = self.place[axis]
        to = lax.rem(mine + hop, n)
        held = self.window(stage, lax.rem(mine + n - hop, n) if arriving else mine)
        return pltpu.make_async_remote_copy(
            src_ref=held,
            dst_ref=held,
            send_sem=self.send_sem.at[stage, hop],
            recv_sem=self.recv_sem.at[stage, hop],
            device_id=self.device(moved(self.place, axis, to)),
            device_id_type=MESH,
        )

    def start(self, stage):
        if stage == 0:
            self.out[self.place] = self.load()
        for hop in range(1, self.grid[self.order[stage]]):
            self.copy(stage, hop, False).start()

    def finish(self, stage):
        for hop in range(1, self.grid[self.order[stage]]):
            self.copy(stage, hop, False).wait_send()
            self.copy(stage, hop, True).wait_recv()


class Reduce:
    def __init__(self, grid, place, order, x, helds, sums, out, send_sem, recv_sem, device=None):
        self.grid, self.place, self.order = grid, place, order
        self.device = device or (lambda at: grid_device(grid, at))
        self.refs = (x,) + tuple(sums)
        self.helds, self.out = helds, out
        self.send_sem, self.recv_sem = send_sem, recv_sem

    def window(self, stage, index):
        axis = self.order[stage]
        where = []
        for k in range(4):
            if k == axis:
                where.append(pl.ds(index, 1))
            elif k in self.order[:stage]:
                where.append(pl.ds(0, 1))
            else:
                where.append(pl.ds(0, self.grid[k]))
        return self.refs[stage].at[tuple(where)]

    def copy(self, stage, hop):
        axis = self.order[stage]
        to = lax.rem(self.place[axis] + hop, self.grid[axis])
        return pltpu.make_async_remote_copy(
            src_ref=self.window(stage, to),
            dst_ref=self.helds[stage].at[hop - 1],
            send_sem=self.send_sem.at[stage, hop],
            recv_sem=self.recv_sem.at[stage, hop],
            device_id=self.device(moved(self.place, axis, to)),
            device_id_type=MESH,
        )

    def start(self, stage):
        for hop in range(1, self.grid[self.order[stage]]):
            self.copy(stage, hop).start()

    def finish(self, stage):
        axis = self.order[stage]
        n = self.grid[axis]
        for hop in range(1, n):
            self.copy(stage, hop).wait()
        left = [
            1 if k in self.order[: stage + 1] else self.grid[k] for k in range(4)
        ]
        last = stage == len(self.order) - 1

        def add(i, carry):
            where = []
            for k in (3, 2, 1, 0):
                where.insert(0, lax.rem(i, left[k]))
                i = i // left[k]
            own = moved(tuple(where), axis, self.place[axis])
            total = self.refs[stage][own].astype(jnp.float32)
            for hop in range(1, n):
                total = total + self.helds[stage][(hop - 1, *where)].astype(jnp.float32)
            if last:
                self.out[...] = total
            else:
                self.refs[stage + 1][tuple(where)] = total.astype(jnp.bfloat16)
            return carry

        lax.fori_loop(0, math.prod(left), add, 0)


def reduce_scratch(grid, orders, shapes):
    helds, sums = [], []
    for order, shape in zip(orders, shapes, strict=True):
        left = list(grid)
        for stage, axis in enumerate(order):
            n = left[axis]
            left[axis] = 1
            helds.append(pltpu.VMEM((max(n - 1, 1), *left, *shape), jnp.bfloat16))
            if stage < len(order) - 1:
                sums.append(pltpu.VMEM((*left, *shape), jnp.bfloat16))
    return helds, sums


def fetch_kernel(nu, nd, cap, count, *refs):
    wanted, table = refs[:2]
    parts = refs[2 : 2 + count]
    out, asked = refs[2 + count : 4 + count]
    wholes = refs[4 + count : 4 + 2 * count]
    tab = refs[4 + 2 * count]
    sought, rows, send_a, recv_a, send_b, recv_b, own_sem, send_g, recv_g = refs[5 + 2 * count :]
    n = nu * nd
    grid = grid_of(nu, nd)
    place = grid_place(grid)
    gathers = [
        Gather(
            grid,
            place,
            GATHER_ORDERS[i % len(GATHER_ORDERS)],
            loader(parts[i]),
            wholes[i],
            send_g.at[i],
            recv_g.at[i],
        )
        for i in range(count)
    ]
    part_grid, part_place, part_device = dp_grid(grid, place)
    tile = tab.shape[-1]
    tables = [
        Gather(
            part_grid,
            part_place,
            DP_GATHER,
            column_loader(table, v * tile, tile),
            tab.at[v],
            send_g.at[count + v],
            recv_g.at[count + v],
            part_device,
        )
        for v in range(tab.shape[0])
    ]
    my_unit = lax.axis_index("unit")
    my_dp = lax.axis_index("dp")
    me = my_unit * nd + my_dp
    vocab = table.shape[1]
    block = 1280 if vocab % 1280 == 0 else vocab
    greet_all(nu, nd, me)

    def ask(peer, slot):
        return pltpu.make_async_remote_copy(
            src_ref=wanted.at[peer // nd],
            dst_ref=asked.at[slot],
            send_sem=send_a.at[peer],
            recv_sem=recv_a.at[slot],
            device_id={"unit": peer // nd, "dp": lax.rem(peer, nd)},
            device_id_type=MESH,
        )

    def answer(unit, dp, from_unit, from_dp):
        peer = unit * nd + dp
        return pltpu.make_async_remote_copy(
            src_ref=rows.at[peer],
            dst_ref=out.at[from_dp, from_unit],
            send_sem=send_b.at[peer],
            recv_sem=recv_b.at[from_unit * nd + from_dp],
            device_id={"unit": unit, "dp": dp},
            device_id_type=MESH,
        )

    def ask_start(j, carry):
        ask(lax.rem(me + j, n), me).start()
        return carry

    def ask_wait(j, carry):
        peer = lax.rem(me + j, n)
        ask(peer, me).wait_send()
        ask(peer, peer).wait_recv()
        return carry

    lax.fori_loop(1, n, ask_start, 0)
    for gather in gathers:
        gather.start(0)
    for gather in tables:
        gather.start(0)
    asked[me] = wanted[my_unit]
    lax.fori_loop(1, n, ask_wait, 0)

    def one_group(g):
        dp = lax.rem(my_dp + g, nd)
        part = table.shape[0]
        total = jnp.zeros((part, nu * cap), jnp.float32)
        for start in range(0, vocab, block):
            lines = lax.broadcasted_iota(jnp.int32, (block, nu * cap), 0) + start
            hit = jnp.where(lines == sought[pl.ds(dp, 1), :], 1.0, 0.0).astype(jnp.bfloat16)
            total = total + product(table[:, start : start + block], hit)
        found = jnp.swapaxes(total, 0, 1).astype(jnp.bfloat16)
        head, tails = pack_rows(found, nu, cap, part, 0, part)
        for unit in range(nu):
            rows[unit * nd + dp, :cap] = head[unit]
            for tail in tails:
                rows[unit * nd + dp, cap:] = tail[unit]

        def send(unit, carry):
            @pl.when(jnp.logical_or(unit != my_unit, dp != my_dp))
            def _():
                answer(unit, dp, my_unit, my_dp).start()

            return carry

        lax.fori_loop(0, nu, send, 0)

    def advance(t):
        for i, gather in enumerate(gathers):
            stage = t - i // 2
            if 0 <= stage < 4:
                gather.finish(stage)
                if stage < 3:
                    gather.start(stage + 1)

    for dp in range(nd):
        sought[dp : dp + 1, :] = jnp.concatenate(
            [asked[unit * nd + dp][:, :cap] for unit in range(nu)], 1
        )
    for g in range(nd):
        one_group(g)
        advance(g)
    for t in range(nd, 4 + (count - 1) // 2):
        advance(t)
    for gather in tables:
        gather.finish(0)
        gather.start(1)
    for gather in tables:
        gather.finish(1)
    own = pltpu.make_async_copy(rows.at[me], out.at[my_dp, my_unit], own_sem)
    own.start()
    own.wait()

    def answer_wait(j, carry):
        peer = lax.rem(me + j, n)
        unit, dp = peer // nd, lax.rem(peer, nd)
        answer(unit, dp, my_unit, my_dp).wait_send()
        answer(unit, dp, unit, dp).wait_recv()
        return carry

    lax.fori_loop(1, n, answer_wait, 0)


def fetch_rows(wanted, table, parts, nu, nd, cap, collective):
    n = nu * nd
    part, vocab = table.shape
    early = early_tiles(vocab)
    count = len(parts)
    grid = grid_of(nu, nd)
    reach = max(grid)
    return pl.pallas_call(
        functools.partial(fetch_kernel, nu, nd, cap, count),
        out_shape=(
            jax.ShapeDtypeStruct((nd, nu, *packed_shape(cap, part)), jnp.bfloat16),
            jax.ShapeDtypeStruct((n, 1, 128), jnp.int32),
            *(jax.ShapeDtypeStruct((*grid, *x.shape), x.dtype) for x in parts),
            jax.ShapeDtypeStruct((early, 1, 1, *grid[2:], part, tile_of(vocab)), jnp.bfloat16),
        ),
        in_specs=[on_chip()] * (2 + count),
        out_specs=(on_chip(),) * (3 + count),
        scratch_shapes=[
            pltpu.VMEM((nd, nu * cap), jnp.int32),
            pltpu.VMEM((n, *packed_shape(cap, part)), jnp.bfloat16),
            pltpu.SemaphoreType.DMA((n,)),
            pltpu.SemaphoreType.DMA((n,)),
            pltpu.SemaphoreType.DMA((n,)),
            pltpu.SemaphoreType.DMA((n,)),
            pltpu.SemaphoreType.DMA,
            pltpu.SemaphoreType.DMA((count + early, 4, reach)),
            pltpu.SemaphoreType.DMA((count + early, 4, reach)),
        ],
        compiler_params=call_params(collective),
    )(wanted, table, *parts)


def return_kernel(nu, nd, count, extras, units, *refs):
    x_ref, asked_ref, base_ref, more_hbm, vec_own, small_own, info = refs[:7]
    grads = refs[7 : 7 + count]
    dp_shares = refs[7 + count : 7 + count + extras]
    rest = refs[7 + count + extras :]
    table_ref, totals_ref = rest[:2]
    shares, small_share = rest[2 : 2 + count], rest[2 + count]
    rest = rest[3 + count :]
    out_ref, rows_ref, mine_ref, held_ref, ids_ref, more_ref, more_sem = rest[:7]
    rest = rest[7:]
    helds, sums = rest[: 4 * count], rest[4 * count : 7 * count]
    send_sem, recv_sem, own_sem, send_r, recv_r, send_t, recv_t = rest[7 * count :]
    n = nu * nd
    my_unit = lax.axis_index("unit")
    my_dp = lax.axis_index("dp")
    me = my_unit * nd + my_dp
    grid = grid_of(nu, nd)
    place = grid_place(grid)
    reduces = [
        Reduce(
            grid,
            place,
            REDUCE_ORDERS[i % 2],
            grads[i],
            helds[4 * i : 4 * i + 4],
            sums[3 * i : 3 * i + 3],
            shares[i],
            send_r.at[i],
            recv_r.at[i],
        )
        for i in range(count)
    ]
    greet_all(nu, nd, me)

    def peer_id(peer):
        return {"unit": peer // nd, "dp": lax.rem(peer, nd)}

    def copy(peer, slot):
        return pltpu.make_async_remote_copy(
            src_ref=x_ref.at[lax.rem(peer, nd), peer // nd],
            dst_ref=out_ref.at[slot],
            send_sem=send_sem.at[peer],
            recv_sem=recv_sem.at[slot],
            device_id=peer_id(peer),
            device_id_type=MESH,
        )

    def total_copy(peer, slot):
        return pltpu.make_async_remote_copy(
            src_ref=mine_ref,
            dst_ref=held_ref.at[slot],
            send_sem=send_t.at[peer],
            recv_sem=recv_t.at[slot],
            device_id=peer_id(peer),
            device_id_type=MESH,
        )

    def others(step):
        lax.fori_loop(1, n, lambda j, carry: (step(lax.rem(me + j, n)), carry)[1], 0)

    def wait(peer):
        copy(peer, me).wait_send()
        copy(peer, peer).wait_recv()

    def total_wait(peer):
        total_copy(peer, me).wait_send()
        total_copy(peer, peer).wait_recv()

    for reduce in reduces:
        reduce.start(0)
    others(lambda peer: copy(peer, me).start())
    own = pltpu.make_async_copy(x_ref.at[my_dp, my_unit], out_ref.at[me], own_sem)
    own.start()
    own.wait()

    more_copy = pltpu.make_async_copy(more_hbm, more_ref, more_sem)
    more_copy.start()
    tiles, part, tile = base_ref.shape
    vocab = tiles * tile
    cap = ids_ref.shape[0] // n
    turned = jnp.swapaxes(asked_ref[...], 0, 1)
    for p in range(n):
        ids_ref[p * cap : (p + 1) * cap, :] = turned[:cap, p : p + 1]
    halves = 2 if tile % 256 == 0 else 1
    block = tile // halves

    def add_rows(b):
        first = b * block
        v, at = divmod(first, tile)
        lanes = lax.broadcasted_iota(jnp.int32, (ids_ref.shape[0], block), 1) + first
        hit = jnp.where(ids_ref[...] == lanes, 1.0, 0.0).astype(jnp.bfloat16)
        where = slice(first, first + block)
        both = (
            base_ref[v, :, at : at + block]
            + more_ref[:, where].astype(jnp.float32)
            + product(rows_ref[...], hit)
        )
        table_ref[:, where] = both
        return row_sum(both * both)

    steps = 4 + (count - 1) // 2
    blocks = vocab // block
    squares = jnp.zeros((1, block), jnp.float32)
    for t in range(steps):
        for i, reduce in enumerate(reduces):
            stage = t - i // 2
            if 0 <= stage < 4:
                reduce.finish(stage)
                if stage < 3:
                    reduce.start(stage + 1)
        if t == 1:
            more_copy.wait()
            others(wait)
            arrived = unpack_rows(out_ref, ids_ref.shape[0] // n, part, 0, part)
            rows_ref[...] = jnp.swapaxes(arrived, 0, 1).astype(jnp.bfloat16)
        if t >= 1:
            done, left = t - 1, steps - 1
            for b in range(blocks * done // left, blocks * (done + 1) // left):
                squares = squares + add_rows(b)
    last = shares[count - 1]
    seq = last.shape[1] - 128
    own_slope = score_slope(vec_own[...].astype(jnp.bfloat16).astype(jnp.float32))
    column = lax.broadcasted_iota(jnp.int32, own_slope.shape, 1)
    last[:, seq:] += jnp.where(column == 13, info[2:3, 0:1] * own_slope, 0.0)
    own_slope = score_slope(small_own[...].astype(jnp.bfloat16).astype(jnp.float32))
    line = lax.broadcasted_iota(jnp.int32, own_slope.shape, 0)
    column = lax.broadcasted_iota(jnp.int32, own_slope.shape, 1)
    is_unit = jnp.logical_and(line == 1, column < units)
    small_share[...] = dp_shares[extras - 1][...] + jnp.where(
        is_unit, info[3:4, 0:1] * own_slope, 0.0
    )
    square = jnp.sum(squares, 1, keepdims=True)
    for share in (*shares, *dp_shares[: extras - 1], small_share):
        square = square + jnp.sum(row_sum(share[...] * share[...]), 1, keepdims=True)
    lane = lax.broadcasted_iota(jnp.int32, (8, 128), 1)
    mine_ref[...] = jnp.where(lane == 127, square, info[0:1, :])
    others(lambda peer: total_copy(peer, me).start())
    held_ref[me] = mine_ref[...]
    others(total_wait)
    totals_ref[...] = jnp.zeros_like(totals_ref)

    def add_total(j, carry):
        totals_ref[...] += held_ref[j]
        return carry

    lax.fori_loop(0, n, add_total, 0)


def return_rows(
    x, asked, base, more, vec_own, small_own, info, grads, dp_shares, units, cap, nu, nd, collective
):
    n = nu * nd
    grid = grid_of(nu, nd)
    count, extras = len(grads), len(dp_shares)
    reach = max(grid)
    shapes = [(g.shape[0] // n, g.shape[1]) for g in grads]
    helds, sums = reduce_scratch(grid, [REDUCE_ORDERS[i % 2] for i in range(count)], shapes)
    tiles, part, tile = base.shape
    return pl.pallas_call(
        functools.partial(return_kernel, nu, nd, count, extras, units),
        out_shape=(
            jax.ShapeDtypeStruct((part, tiles * tile), jnp.float32),
            jax.ShapeDtypeStruct((8, 128), jnp.float32),
            *(jax.ShapeDtypeStruct(shape, jnp.float32) for shape in shapes),
            jax.ShapeDtypeStruct(dp_shares[-1].shape, jnp.float32),
        ),
        in_specs=[on_chip()] * 3
        + [pl.BlockSpec(memory_space=pl.ANY)]
        + [on_chip()] * (3 + count + extras),
        out_specs=(on_chip(),) * (3 + count),
        scratch_shapes=[
            pltpu.VMEM((n,) + x.shape[2:], x.dtype),
            pltpu.VMEM((part, n * cap), x.dtype),
            pltpu.VMEM((8, 128), jnp.float32),
            pltpu.VMEM((n, 8, 128), jnp.float32),
            pltpu.VMEM((n * cap, 1), jnp.int32),
            pltpu.VMEM(more.shape, more.dtype),
            pltpu.SemaphoreType.DMA,
            *helds,
            *sums,
            pltpu.SemaphoreType.DMA((n,)),
            pltpu.SemaphoreType.DMA((n,)),
            pltpu.SemaphoreType.DMA,
            pltpu.SemaphoreType.DMA((count, 4, reach)),
            pltpu.SemaphoreType.DMA((count, 4, reach)),
            pltpu.SemaphoreType.DMA((n,)),
            pltpu.SemaphoreType.DMA((n,)),
        ],
        compiler_params=call_params(collective),
    )(
        x,
        asked,
        base,
        more,
        vec_own,
        small_own,
        info,
        *(g.reshape(*grid, *shape) for g, shape in zip(grads, shapes, strict=True)),
        *dp_shares,
    )


def update_kernel(heads, npos, mats, *refs):
    totals, info, scal = refs[:3]
    shares = refs[3 : mats + 6]
    share_t = refs[mats + 6]
    mw, mf, ms, vw, vf, vs, fw, ff, fs, uw, uf, us, bw, bf, bs, kw, kf, ks, tw, tf, ts = refs[
        mats + 7 : mats + 28
    ]
    outs = refs[mats + 28 :]
    m_new, m_grad, v_new, v_grad, f_new, f_grad = outs[:6]
    u_new, u_grad, b_new, b_grad, k_new, k_grad, stat, t_new, t_grad = outs[6:]
    lane = lax.broadcasted_iota(jnp.int32, (1, 128), 1)
    share_k = jnp.where(lane < heads + 2, totals[0:1, :] + info[1:2, :], 0.0)
    norm = jnp.sqrt(totals[0:1, 127:128] + jnp.sum(share_k * share_k, 1, keepdims=True))
    coef = jnp.minimum(1.0, MAX_NORM / (norm + 1e-06))
    first_scale, second_scale = scal[3:4, 0:1], scal[3:4, 1:2]

    def step(share, weight, first, second, rate):
        grad = share * coef
        first = BETA_ONE * first + (1.0 - BETA_ONE) * grad
        second = BETA_TWO * second + (1.0 - BETA_TWO) * grad * grad
        first_hat = first / first_scale
        second_hat = second / second_scale
        new = weight - rate * (first_hat / (jnp.sqrt(second_hat) + ADAM_EPS) + DECAY * weight)
        return grad, new

    t_grad[...], t_new[...] = step(share_t[...], tw[...], tf[...], ts[...], RATE_TABLE)

    @pl.when(pl.program_id(0) == 0)
    def _():
        first = 0
        for k in range(mats):
            length = min(shares[k].shape[1], mw.shape[1] - first)
            where = slice(first, first + length)
            m_grad[:, where], m_new[:, where] = step(
                shares[k][:, :length], mw[:, where], mf[:, where], ms[:, where], RATE_MATS
            )
            first += length

    @pl.when(pl.program_id(0) == 1)
    def _():
        for k in range(2):
            f_grad[k], f_new[k] = step(shares[mats + k][...], fw[k], ff[k], fs[k], RATE_MATS)

    @pl.when(pl.program_id(0) == 2)
    def _():
        last, small = shares[mats - 1], shares[mats + 2]
        turned = jnp.swapaxes(last[:, last.shape[1] - 128 :], 0, 1)[: vw.shape[0]]
        v_grad[...], v_new[...] = step(turned, vw[...], vf[...], vs[...], RATE_VECS)
        u_grad[...], u_new[...] = step(
            small[0:2, : uw.shape[1]], uw[...], uf[...], us[...], RATE_VECS
        )
        b_grad[...], b_new[...] = step(
            small[2:3, : bw.shape[1]], bw[...], bf[...], bs[...], RATE_VECS
        )
        k_grad[...], k_new[...] = step(
            share_k[:, : kw.shape[1]], kw[...], kf[...], ks[...], RATE_VECS
        )
        kl_all = totals[0:1, heads + 2 : heads + 3]
        loss = TEMPER * TEMPER * kl_all / npos + info[5:6, 0:1]
        line = lax.broadcasted_iota(jnp.int32, (8, 128), 0)
        stat[...] = jnp.where(line == 0, loss, jnp.where(line == 1, info[4:5, 0:1], norm))


def update_step(heads, npos, totals, info, scal, shares, share_table, small, table):
    part, vocab = share_table.shape
    blocks = 4
    row = pl.BlockSpec((part // blocks, vocab), lambda i: (i, 0))

    def whole(x):
        zeros = (0,) * len(x.shape)
        return pl.BlockSpec(x.shape, lambda i: zeros)

    args = [totals, info, scal, *shares, share_table]
    specs = [whole(x) for x in args[:-1]] + [row]
    for trio in small:
        args += trio
        specs += [whole(x) for x in trio]
    args += table
    specs += [row] * 3
    outs = [x for trio in small for x in (trio[0], trio[0])] + [totals, table[0], table[0]]
    return pl.pallas_call(
        functools.partial(update_kernel, heads, npos, len(shares) - 3),
        grid=(blocks,),
        out_shape=tuple(jax.ShapeDtypeStruct(x.shape, x.dtype) for x in outs),
        in_specs=specs,
        out_specs=tuple(whole(x) for x in outs[:-2]) + (row, row),
        compiler_params=pltpu.CompilerParams(vmem_limit_bytes=VMEM_LIMIT),
    )(*args)


def row_sum(values):
    return jnp.sum(values, 0, keepdims=True)


class UnitGather:
    def __init__(self, n, me, buf, send_sem, recv_sem):
        self.n, self.me, self.buf = n, me, buf
        self.send_sem, self.recv_sem = send_sem, recv_sem
        self.inner = n // 2
        self.half, self.idx = me // self.inner, lax.rem(me, self.inner)
        self.mirror = (1 - self.half) * self.inner + self.idx

    def near(self, hop):
        return self.half * self.inner + lax.rem(self.idx + hop, self.inner)

    def copy(self, block, to, kind, hop):
        return pltpu.make_async_remote_copy(
            src_ref=self.buf.at[block],
            dst_ref=self.buf.at[block],
            send_sem=self.send_sem.at[kind, hop],
            recv_sem=self.recv_sem.at[block],
            device_id={"unit": to},
            device_id_type=MESH,
        )

    def hops(self, step):
        lax.fori_loop(1, self.inner, lambda hop, carry: (step(hop), carry)[1], 0)

    def start(self):
        self.copy(self.me, self.mirror, 0, 0).start()
        self.hops(lambda hop: self.copy(self.me, self.near(hop), 0, hop).start())

    def forward(self):
        self.copy(self.mirror, self.mirror, 0, 0).wait_recv()
        self.hops(lambda hop: self.copy(self.mirror, self.near(hop), 1, hop).start())

    def wait_half(self):
        self.hops(lambda hop: self.copy(self.near(hop), self.mirror, 0, 0).wait_recv())

    def wait_rest(self):
        far = (1 - self.half) * self.inner

        def step(hop):
            block = far + lax.rem(self.idx + hop, self.inner)
            self.copy(block, self.mirror, 0, 0).wait_recv()

        self.hops(step)

    def finish(self):
        self.copy(self.me, self.mirror, 0, 0).wait_send()

        def step(hop):
            self.copy(self.me, self.near(hop), 0, hop).wait_send()
            self.copy(self.mirror, self.near(hop), 1, hop).wait_send()

        self.hops(step)


class UnitReduce:
    def __init__(self, n, me, part, held, mine, other, send_sem, recv_sem):
        self.n, self.me, self.part = n, me, part
        self.held, self.mine, self.other = held, mine, other
        self.send_sem, self.recv_sem = send_sem, recv_sem
        self.inner = n // 2
        self.half, self.idx = me // self.inner, lax.rem(me, self.inner)
        self.mirror = (1 - self.half) * self.inner + self.idx

    def copy(self, kind, hop):
        index = lax.rem(self.idx + hop, self.inner)
        half = self.half if kind else 1 - self.half
        return pltpu.make_async_remote_copy(
            src_ref=self.part.at[half * self.inner + index],
            dst_ref=self.held.at[kind, hop - 1],
            send_sem=self.send_sem.at[kind, hop],
            recv_sem=self.recv_sem.at[kind, hop],
            device_id={"unit": self.half * self.inner + index},
            device_id_type=MESH,
        )

    def across(self):
        return pltpu.make_async_remote_copy(
            src_ref=self.mine,
            dst_ref=self.other,
            send_sem=self.send_sem.at[0, 0],
            recv_sem=self.recv_sem.at[0, 0],
            device_id={"unit": self.mirror},
            device_id_type=MESH,
        )

    def start(self, kind):
        def step(hop, carry):
            self.copy(kind, hop).start()
            return carry

        lax.fori_loop(1, self.inner, step, 0)

    def wait(self, kind):
        def step(hop, carry):
            self.copy(kind, hop).wait()
            return carry

        lax.fori_loop(1, self.inner, step, 0)

    def total(self, kind, block):
        result = self.part[block].astype(jnp.float32)
        for hop in range(1, self.inner):
            result = result + self.held[kind, hop - 1].astype(jnp.float32)
        return result

    def middle(self):
        self.wait(0)
        self.mine[...] = self.total(0, self.mirror).astype(jnp.bfloat16)
        self.across().start()

    def finish(self):
        self.wait(1)
        result = self.total(1, self.me)
        self.across().wait()
        return result + self.other[...].astype(jnp.float32)


def mid_kernel(n, nd, npos, *refs):
    middle_ref, ffn_ref, pack_ref, noise_ref, own_ref, tab_in, teach_ref, wt_ref, vecs_ref = refs[
        :9
    ]
    share, small_out, gup, gdown, gwt, gmid, gvecs, stat_out = refs[9:17]
    unit_ref = refs[17]
    rows, backs, trans, hpre, hid, ghp, student, glow, acc, tmax, statc, stats = refs[18:30]
    part, mine, helds, others = refs[30], refs[31], refs[32:35], refs[35:38]
    gather_send, gather_recv, reduce_send, reduce_recv, stat_send, stat_recv = refs[38:44]
    gtable, dp_send, dp_recv, tab, halves, packs, vbias_ref, gvbias, gunit = refs[44:53]
    part_send, part_recv, tab_sem = refs[53:56]
    dp_scratch = refs[56:]
    me = lax.axis_index("unit")
    all_grid = grid_of(n, nd)
    grid, place, device = dp_grid(all_grid, grid_place(all_grid))
    low, full = jnp.bfloat16, jnp.float32
    count, width = middle_ref.shape
    vocab = own_ref.shape[1]
    tiles, tile = tab.shape[0], tab.shape[-1]
    early = tab_in.shape[0]
    group = max(1, 256 // count)
    block = group * count
    per_half = n // 2 // group
    half = me // (n // 2)
    table_reduces = [
        Reduce(
            grid,
            place,
            DP_ORDER,
            gtable.at[v],
            dp_scratch[3 * v : 3 * v + 2],
            dp_scratch[3 * v + 2 : 3 * v + 3],
            share.at[v],
            dp_send.at[v],
            dp_recv.at[v],
            device,
        )
        for v in range(tiles)
    ]
    own_blocks = (half * per_half, (half + 1) * per_half)
    far_blocks = ((1 - half) * per_half, (2 - half) * per_half)
    greet_all(n, nd, me * nd + lax.axis_index("dp"))
    gathers = [
        UnitGather(n, me, buf, gather_send.at[i], gather_recv.at[i])
        for i, buf in enumerate((rows, trans, backs))
    ]
    reduces = [
        UnitReduce(
            n, me, part, helds[i], mine, others[i], reduce_send.at[i], reduce_recv.at[i]
        )
        for i in range(3)
    ]

    loads = [
        (low_loader(ffn_ref, 0), halves.at[0]),
        (low_loader(ffn_ref, 1), halves.at[1]),
        (low_loader(pack_ref, slice(None)), packs),
        *((column_loader(own_ref, v * tile, tile), tab.at[v]) for v in range(early, tiles)),
    ]
    parts_in = [
        Gather(
            grid, place, DP_GATHER, load, out, part_send.at[i], part_recv.at[i], device
        )
        for i, (load, out) in enumerate(loads)
    ]
    tab_copy = pltpu.make_async_copy(tab_in, tab.at[pl.ds(0, early)], tab_sem)

    def up_w():
        return halves[0].reshape(width, -1)

    def down_w():
        return halves[1].reshape(width, -1)

    def table_tile(v):
        return tab[v].reshape(width, tile)

    def vec(k):
        return vecs_ref[k : k + 1, :]

    def loop(span, step):
        lax.fori_loop(span[0], span[1], lambda b, carry: (step(b), carry)[1], 0)

    def lines(b):
        return pl.ds(pl.multiple_of(b * block, block), block)

    def columns(v):
        return pl.ds(v * tile if isinstance(v, int) else pl.multiple_of(v * tile, 128), tile)

    def gathered(buf, b):
        return buf[pl.ds(b * group, group)].reshape(block, width)

    def put_part(b, values):
        part[pl.ds(b * group, group)] = values.astype(low).reshape(group, count, width)

    middle = middle_ref[...]
    rows[me] = middle.astype(low)
    gathers[0].start()
    for one in parts_in:
        one.start(0)
    tab_copy.start()

    def teacher_top(b):
        top = jnp.max(teach_ref[lines(b), :].astype(full), 1, keepdims=True) / TEMPER
        tmax[lines(b), :] = jnp.broadcast_to(top, (block, 128))

    loop((0, n // group), teacher_top)
    gathers[0].forward()
    for one in parts_in[:3]:
        one.finish(0)
        one.start(1)
    gathers[0].wait_half()
    for one in parts_in[:3]:
        one.finish(1)
    blocks_in = [packs[0, 0, d // grid[3], d % grid[3]].astype(full) for d in range(nd)]
    units, biases = unit_ref.shape[1] // nd, vocab // nd
    logit = jnp.concatenate([item[1:2, :units] for item in blocks_in], 1)
    unit_ref[0:1, :] = jnp.concatenate([item[0:1, :units] for item in blocks_in], 1)
    unit_ref[1:2, :] = gate(logit, noise_ref[...])
    unit_ref[2:3, :] = jnp.broadcast_to(
        jnp.sum(keep_score(logit), 1, keepdims=True), logit.shape
    )
    vbias_ref[...] = jnp.concatenate([item[2:3, :biases] for item in blocks_in], 1)

    def up_down(b):
        pre = (
            jnp.dot(gathered(rows, b), up_w(), preferred_element_type=full)
            + unit_ref[0:1, :]
        )
        hpre[lines(b), :] = pre
        hidden = (jax.nn.gelu(pre) * unit_ref[1:2, :]).astype(low)
        hid[lines(b), :] = hidden
        put_part(
            b,
            lax.dot_general(
                hidden, down_w(), (((1,), (1,)), ((), ())), preferred_element_type=full
            ),
        )

    loop(own_blocks, up_down)
    reduces[0].start(1)
    gathers[0].wait_rest()
    loop(far_blocks, up_down)
    reduces[0].start(0)
    for one in parts_in[3:]:
        one.finish(0)
        one.start(1)
    reduces[0].middle()
    ffn_res = reduces[0].finish() + vec(7)
    final_in = middle + ffn_res * vec(14)
    final = layer_norm(final_in, vec(8), vec(9))
    picked = final.astype(low)
    trans_pre = jnp.dot(picked, wt_ref[...], preferred_element_type=full) + vec(10)
    trans_gelu = jax.nn.gelu(trans_pre)
    trans[me] = layer_norm(trans_gelu, vec(11), vec(12)).astype(low)
    gathers[1].start()
    gathers[0].finish()
    gathers[1].forward()
    tab_copy.wait()
    gathers[1].wait_half()

    def head(b, arriving=False):
        these = gathered(trans, b)
        t_top = tmax[lines(b), :1]

        def one(v, carry):
            s_max, s_sum, t_sum, cross = carry
            logits = (
                jnp.dot(these, table_tile(v), preferred_element_type=full)
                + vbias_ref[:, columns(v)]
            ) / TEMPER
            student[lines(b), columns(v)] = logits
            teach = teach_ref[lines(b), columns(v)].astype(full) / TEMPER
            top = jnp.maximum(s_max, jnp.max(logits, 1, keepdims=True))
            s_sum = s_sum * jnp.exp(s_max - top) + jnp.sum(
                jnp.exp(logits - top), 1, keepdims=True
            )
            t_exp = jnp.exp(teach - t_top)
            t_sum = t_sum + jnp.sum(t_exp, 1, keepdims=True)
            cross = cross + jnp.sum(t_exp * (teach - logits), 1, keepdims=True)
            return top, s_sum, t_sum, cross

        zero = jnp.zeros((block, 1), full)
        carry = (jnp.full((block, 1), -1e30, full), zero, zero, zero)
        if arriving:
            carry = lax.fori_loop(0, early, one, carry)
            for v in range(early, tiles):

                @pl.when(b == own_blocks[0])
                def _():
                    parts_in[3 + v - early].finish(1)

                carry = one(v, carry)
        else:
            carry = lax.fori_loop(0, tiles, one, carry)
        s_max, s_sum, t_sum, cross = carry
        lane = lax.broadcasted_iota(jnp.int32, (block, 128), 1)
        packed = jnp.where(lane == 0, s_max, unit_ref[2:3, 0:1])
        for k, item in ((1, s_sum), (2, t_top), (3, t_sum), (4, cross)):
            packed = jnp.where(lane == k, item, packed)
        statc[lines(b), :] = packed

    loop(own_blocks, lambda b: head(b, True))
    gathers[1].wait_rest()
    loop(far_blocks, head)
    stats[me] = jnp.swapaxes(statc[...], 0, 1)[:8]

    def stat_copy(peer, slot):
        return pltpu.make_async_remote_copy(
            src_ref=stats.at[me],
            dst_ref=stats.at[slot],
            send_sem=stat_send.at[peer],
            recv_sem=stat_recv.at[slot],
            device_id={"unit": peer},
            device_id_type=MESH,
        )

    def stat_wait(j):
        peer = lax.rem(me + j, n)
        stat_copy(peer, me).wait_send()
        stat_copy(peer, peer).wait_recv()

    loop((1, n), lambda j: stat_copy(lax.rem(me + j, n), me).start())
    gathers[1].finish()
    loop((1, n), stat_wait)
    s_top, t_top = stats[0, 0:1], stats[0, 2:3]
    for k in range(1, n):
        s_top = jnp.maximum(s_top, stats[k, 0:1])
        t_top = jnp.maximum(t_top, stats[k, 2:3])
    s_all = t_all = cross_all = jnp.zeros_like(s_top)
    unit_all = jnp.zeros((1, 1), full)
    for k in range(n):
        s_all = s_all + stats[k, 1:2] * jnp.exp(stats[k, 0:1] - s_top)
        scale = jnp.exp(stats[k, 2:3] - t_top)
        t_all = t_all + stats[k, 3:4] * scale
        cross_all = cross_all + stats[k, 4:5] * scale
        unit_all = unit_all + stats[k, 5:6, 0:1]
    lse_student = s_top + jnp.log(s_all)
    lse_teach = t_top + jnp.log(t_all)
    kl_rows = cross_all / t_all - lse_teach + lse_student
    place = lax.broadcasted_iota(jnp.int32, kl_rows.shape, 1)
    is_own = jnp.logical_and(place >= me * count, place < (me + 1) * count)
    kl_own = jnp.sum(jnp.where(is_own, kl_rows, 0.0), 1, keepdims=True)
    line = lax.broadcasted_iota(jnp.int32, (8, 128), 0)
    stat_out[...] = jnp.where(line == 0, kl_own, unit_all)
    both = jnp.where(
        lax.broadcasted_iota(jnp.int32, (8, n * count), 0) == 0, lse_student, lse_teach
    )
    statc[:, :8] = jnp.swapaxes(both, 0, 1)

    gvbias[...] = jnp.zeros_like(gvbias)

    def head_back(b):
        acc[...] = jnp.zeros_like(acc)
        from_student, from_teach = statc[lines(b), 0:1], statc[lines(b), 1:2]

        def one(v):
            teach = teach_ref[lines(b), columns(v)].astype(full) / TEMPER
            grad = (
                TEMPER
                / npos
                * (
                    jnp.exp(student[lines(b), columns(v)] - from_student)
                    - jnp.exp(teach - from_teach)
                )
            )
            gvbias[:, columns(v)] += row_sum(grad)
            grad_low = grad.astype(low)
            glow[lines(b), columns(v)] = grad_low
            acc[...] += lax.dot_general(
                grad_low,
                table_tile(v),
                (((1,), (1,)), ((), ())),
                preferred_element_type=full,
            )

        loop((0, tiles), one)
        put_part(b, acc[...])

    loop(far_blocks, head_back)
    reduces[1].start(0)
    loop(own_blocks, head_back)
    reduces[1].start(1)
    reduces[1].middle()

    for v in range(tiles):
        gtable[v] = (
            contract_rows(
                trans[...].reshape(n * count, width), glow[:, v * tile : (v + 1) * tile]
            )
            .astype(low)
            .reshape(gtable.shape[1:])
        )
        table_reduces[v].start(0)
    grad_trans = reduces[1].finish()
    grad_tgelu, grad_hgain, grad_hshift = norm_back(trans_gelu, vec(11), vec(12), grad_trans)
    grad_tpre = gelu_back(trans_pre, grad_tgelu)
    grad_tpre_low = grad_tpre.astype(low)
    grad_final = lax.dot_general(
        grad_tpre_low, wt_ref[...], (((1,), (1,)), ((), ())), preferred_element_type=full
    )
    grad_final_in, grad_gain2, grad_shift2 = norm_back(final_in, vec(8), vec(9), grad_final)
    grad_fres = grad_final_in * vec(14)
    backs[me] = grad_fres.astype(low)
    gathers[2].start()
    gvecs[0:7, :] = jnp.zeros((7, width), full)
    gvecs[7:8, :] = row_sum(grad_fres)
    gvecs[8:9, :] = grad_gain2
    gvecs[9:10, :] = grad_shift2
    gvecs[10:11, :] = row_sum(grad_tpre)
    gvecs[11:12, :] = grad_hgain
    gvecs[12:13, :] = grad_hshift
    gvecs[13:14, :] = row_sum(grad_final_in * ffn_res)
    gvecs[14:16, :] = jnp.zeros((2, width), full)
    gwt[...] = contract_rows(picked, grad_tpre_low).astype(low)
    for table_reduce in table_reduces:
        table_reduce.finish(0)
        table_reduce.start(1)
    gathers[2].forward()
    gathers[2].wait_half()
    gunit[...] = jnp.zeros_like(gunit)

    def up_down_back(b):
        grad_hidden = jnp.dot(gathered(backs, b), down_w(), preferred_element_type=full)
        pre = hpre[lines(b), :]
        gunit[1:2, :] += row_sum(grad_hidden * jax.nn.gelu(pre))
        grad_pre = gelu_back(pre, grad_hidden * unit_ref[1:2, :])
        gunit[0:1, :] += row_sum(grad_pre)
        grad_pre_low = grad_pre.astype(low)
        ghp[lines(b), :] = grad_pre_low
        put_part(
            b,
            lax.dot_general(
                grad_pre_low, up_w(), (((1,), (1,)), ((), ())), preferred_element_type=full
            ),
        )

    loop(own_blocks, up_down_back)
    reduces[2].start(1)
    gathers[2].wait_rest()
    loop(far_blocks, up_down_back)
    reduces[2].start(0)
    gup[...] = (
        contract_rows(rows[...].reshape(n * count, width), ghp[...]).astype(low).reshape(gup.shape)
    )
    reduces[2].middle()
    gdown[...] = (
        contract_rows(backs[...].reshape(n * count, width), hid[...])
        .astype(low)
        .reshape(gdown.shape)
    )
    grad_logit = gate_back(logit, noise_ref[...], gunit[1:2, :])
    small_out[...] = jnp.zeros_like(small_out)
    for d in range(nd):
        cut, wide = slice(d * units, (d + 1) * units), slice(d * biases, (d + 1) * biases)
        at = (0, 0, d // grid[3], d % grid[3])
        small_out[(*at, slice(0, 1), slice(0, units))] = gunit[0:1, :][:, cut].astype(low)
        small_out[(*at, slice(1, 2), slice(0, units))] = grad_logit[:, cut].astype(low)
        small_out[(*at, slice(2, 3), slice(0, biases))] = gvbias[...][:, wide].astype(low)
    gmid[...] = grad_final_in + reduces[2].finish()
    gathers[2].finish()
    for table_reduce in table_reduces:
        table_reduce.finish(1)


def mid_step(
    middle, ffn, pack, noise, own, tab_in, teach, w_trans, vec_rows, n, nd, npos, collective
):
    count, width = middle.shape
    vocab, units = own.shape[1], ffn.shape[2]
    low, full = jnp.bfloat16, jnp.float32
    rows = n * count
    inner = n // 2
    blocks = pltpu.VMEM((n, count, width), low)
    one = pltpu.VMEM((count, width), low)
    tile = tile_of(vocab)
    tiles = vocab // tile
    late = tiles - early_tiles(vocab)
    grid = (1, 1, *grid_of(n, nd)[2:])
    helds, sums = reduce_scratch(grid, [DP_ORDER] * tiles, [(width // nd, tile)] * tiles)
    dp_scratch = []
    for v in range(tiles):
        dp_scratch += [helds[2 * v], helds[2 * v + 1], sums[v]]
    return pl.pallas_call(
        functools.partial(mid_kernel, n, nd, npos),
        out_shape=(
            jax.ShapeDtypeStruct((tiles, width // nd, tile), full),
            jax.ShapeDtypeStruct((*grid, *pack.shape), low),
            jax.ShapeDtypeStruct((*grid, *ffn.shape[1:]), low),
            jax.ShapeDtypeStruct((*grid, *ffn.shape[1:]), low),
            jax.ShapeDtypeStruct((width, width), low),
            jax.ShapeDtypeStruct((count, width), full),
            jax.ShapeDtypeStruct((16, width), full),
            jax.ShapeDtypeStruct((8, 128), full),
        ),
        in_specs=[on_chip()] * 5 + [pl.BlockSpec(memory_space=pl.ANY)] + [on_chip()] * 3,
        out_specs=(on_chip(),) * 8,
        scratch_shapes=[
            pltpu.VMEM((8, units), full),
            blocks,
            blocks,
            blocks,
            pltpu.VMEM((rows, units), full),
            pltpu.VMEM((rows, units), low),
            pltpu.VMEM((rows, units), low),
            pltpu.VMEM((rows, vocab), full),
            pltpu.VMEM((rows, vocab), low),
            pltpu.VMEM((max(256, count), width), full),
            pltpu.VMEM((rows, 128), full),
            pltpu.VMEM((rows, 128), full),
            pltpu.VMEM((n, 8, rows), full),
            blocks,
            one,
            *[pltpu.VMEM((2, inner - 1, count, width), low)] * 3,
            *[one] * 3,
            pltpu.SemaphoreType.DMA((3, 2, inner)),
            pltpu.SemaphoreType.DMA((3, n)),
            pltpu.SemaphoreType.DMA((3, 2, inner)),
            pltpu.SemaphoreType.DMA((3, 2, inner)),
            pltpu.SemaphoreType.DMA((n,)),
            pltpu.SemaphoreType.DMA((n,)),
            pltpu.VMEM((tiles, *grid, width // nd, tile), low),
            pltpu.SemaphoreType.DMA((tiles, 2, max(grid))),
            pltpu.SemaphoreType.DMA((tiles, 2, max(grid))),
            pltpu.VMEM((tiles, *grid, width // nd, tile), low),
            pltpu.VMEM((2, *grid, *ffn.shape[1:]), low),
            pltpu.VMEM((*grid, *pack.shape), low),
            pltpu.VMEM((1, vocab), full),
            pltpu.VMEM((1, vocab), full),
            pltpu.VMEM((8, units), full),
            pltpu.SemaphoreType.DMA((3 + late, 2, max(grid))),
            pltpu.SemaphoreType.DMA((3 + late, 2, max(grid))),
            pltpu.SemaphoreType.DMA,
            *dp_scratch,
        ],
        compiler_params=call_params(collective),
    )(middle, ffn, pack, noise, own, tab_in, teach, w_trans, vec_rows)


def split_low(values):
    parts = []
    for _ in range(3):
        part = values.astype(jnp.bfloat16)
        parts.append(part)
        values = values - part.astype(jnp.float32)
    return parts


def picked_lines(pos_ref, seq):
    count = pos_ref.shape[0]
    return pos_ref[...] == lax.broadcasted_iota(jnp.int32, (count, seq), 1)


def per_head(values, heads):
    rows, width = values.shape
    size = width // heads
    shape = (heads, rows, width)
    lane = lax.broadcasted_iota(jnp.int32, shape, 2) // size
    keep = lane == lax.broadcasted_iota(jnp.int32, shape, 0)
    return jnp.where(keep, jnp.broadcast_to(values[None], shape), 0.0).reshape(
        heads * rows, width
    )


def from_heads(values, heads):
    total, width = values.shape
    size = width // heads
    shape = (heads, total // heads, width)
    lane = lax.broadcasted_iota(jnp.int32, shape, 2) // size
    keep = lane == lax.broadcasted_iota(jnp.int32, shape, 0)
    return jnp.sum(jnp.where(keep, values.reshape(shape), 0.0), 0)


def mask_row(scal):
    return scal[0:1, :].astype(jnp.bfloat16).astype(jnp.float32)


def attend_kernel(heads, cap, *refs):
    (
        words_ref,
        extra_hbm,
        code_ref,
        pos_ref,
        seg_ref,
        noise_ref,
        scal,
        pos_vecs,
        w_q,
        w_k,
        w_v,
        w_out,
    ) = refs[:12]
    middle_ref, gates_ref = refs[12:14]
    vecs, embed_ref, start_ref, keys, values, queries, probs_ref, small = refs[14:22]
    extra_ref, extra_sem = refs[22:]
    extra_copy = pltpu.make_async_copy(extra_hbm, extra_ref, extra_sem)
    extra_copy.start()
    low, full = jnp.bfloat16, jnp.float32
    seq, width = embed_ref.shape
    nd, nu = words_ref.shape[:2]
    part = width // nd
    count = pos_ref.shape[0]
    n_vecs = 14
    turned = jnp.swapaxes(pos_vecs[:, seq:].astype(full), 0, 1)
    vecs[...] = turned[:16]
    zhid = gate(vecs[13:14, :], noise_ref[...])
    open_masks = gate(mask_row(scal), scal[1:2, :])
    of_head = lax.broadcasted_iota(jnp.int32, (1, width), 1) // (width // heads)
    zcols = jnp.zeros((1, width), full)
    for h in range(heads):
        zcols = jnp.where(of_head == h, open_masks[:, h : h + 1], zcols)
    gates_ref[0:1, :] = zcols
    gates_ref[1:2, :] = jnp.broadcast_to(open_masks[:, heads : heads + 1], (1, width))
    gates_ref[2:8, :] = jnp.broadcast_to(open_masks[:, heads + 1 : heads + 2], (6, width))
    zmlp_hid = gates_ref[2:3, :] * zhid
    vecs[n_vecs : n_vecs + 1, :] = zmlp_hid
    vecs[n_vecs + 1 : n_vecs + 2, :] = zhid

    def vec(k):
        return vecs[k : k + 1, :]

    found = jnp.zeros((nu * cap, width), full)
    for d in range(nd):
        found = found + unpack_rows(words_ref.at[d], cap, width, d * part, part)
    spread = jnp.where(
        code_ref[...] == lax.broadcasted_iota(jnp.int32, (seq, nu * cap), 1), 1.0, 0.0
    ).astype(low)
    extra_copy.wait()
    embed = (
        product(spread, found.astype(low))
        + extra_ref[...].astype(full)
        + jnp.swapaxes(pos_vecs[:, :seq].astype(full), 0, 1)
    )
    embed_ref[...] = embed
    start = layer_norm(embed, vec(0), vec(1)) * zhid
    start_low = start.astype(low)
    start_ref[...] = start_low
    pick_mask = picked_lines(pos_ref, seq)
    pick = jnp.where(pick_mask, 1.0, 0.0).astype(low)
    start_p = sum(product(pick, item) for item in split_low(start))
    start_p_low = start_p.astype(low)
    query = (product(start_p_low, w_q[...]) + vec(2)).astype(low)
    keys[...] = product(start_low, w_k[...]).astype(low)
    values[...] = (product(start_low, w_v[...]) + vec(3)).astype(low)
    queries[...] = query
    seg = seg_ref[...]
    seg_p = jnp.sum(jnp.where(pick_mask, seg, 0), 1, keepdims=True)
    same = jnp.broadcast_to((seg_p == seg)[None], (heads, count, seq)).reshape(
        heads * count, seq
    )
    scale = (width // heads) ** (-0.5)
    scores = (
        product(per_head(query.astype(full), heads).astype(low), keys[...], 1, 1) * scale
    )
    scores = jnp.where(same, scores, -1000000000.0)
    lifted = jnp.exp(scores - jnp.max(scores, 1, keepdims=True))
    probs = lifted / jnp.sum(lifted, 1, keepdims=True)
    probs_ref[...] = probs
    context = from_heads(product(probs.astype(low), values[...]), heads)
    scaled = (context * gates_ref[0:1, :]).astype(low)
    attn_res = product(scaled, w_out[...]) + vec(4)
    middle_in = start_p + attn_res * gates_ref[1:2, :] * zhid
    middle_ref[...] = layer_norm(middle_in, vec(5), vec(6))
    small[0] = start_p
    small[1] = context
    small[2] = attn_res
    small[3] = middle_in


def attend_step(heads, cap, words, extra, code, pos, seg, noise, scal, pos_vecs, maps):
    low, full = jnp.bfloat16, jnp.float32
    seq, width = extra.shape
    count = pos.shape[0]
    return pl.pallas_call(
        functools.partial(attend_kernel, heads, cap),
        out_shape=(
            jax.ShapeDtypeStruct((count, width), full),
            jax.ShapeDtypeStruct((8, width), full),
            jax.ShapeDtypeStruct((16, width), full),
            jax.ShapeDtypeStruct((seq, width), full),
            jax.ShapeDtypeStruct((seq, width), low),
            jax.ShapeDtypeStruct((seq, width), low),
            jax.ShapeDtypeStruct((seq, width), low),
            jax.ShapeDtypeStruct((count, width), low),
            jax.ShapeDtypeStruct((heads * count, seq), full),
            jax.ShapeDtypeStruct((4, count, width), full),
        ),
        in_specs=[on_chip(), pl.BlockSpec(memory_space=pl.ANY)] + [on_chip()] * 10,
        out_specs=(on_chip(),) * 10,
        scratch_shapes=[pltpu.VMEM(extra.shape, extra.dtype), pltpu.SemaphoreType.DMA],
        compiler_params=pltpu.CompilerParams(vmem_limit_bytes=VMEM_LIMIT),
    )(words, extra, code, pos, seg, noise, scal, pos_vecs, *maps)


def attend_back_kernel(heads, nu, nd, cap, ffn_width, *refs):
    (
        gmid_ref,
        mid_vecs,
        vecs,
        embed_ref,
        start_ref,
        keys,
        values,
        queries,
        probs_ref,
        small,
        code_ref,
        pos_ref,
        noise_ref,
        gates_ref,
        scal,
        mid_stats,
        w_q,
        w_k,
        w_v,
        w_out,
    ) = refs[:20]
    extra_in = refs[20:23]
    g_q, g_k, g_v, g_out, g_last, sent, low_embed, info = refs[23:31]
    extra_out = refs[31:34]
    lines = refs[34]
    scratch = refs[35:44]
    send_r, recv_r = refs[44:]
    grid = grid_of(nu, nd)
    place = grid_place(grid)
    part_grid, part_place, part_device = dp_grid(grid, place)
    reduces = [
        Reduce(
            part_grid,
            part_place,
            DP_ORDER,
            extra_in[i],
            scratch[3 * i : 3 * i + 2],
            scratch[3 * i + 2 : 3 * i + 3],
            extra_out[i],
            send_r.at[i],
            recv_r.at[i],
            part_device,
        )
        for i in range(3)
    ]
    me = lax.axis_index("unit") * nd + lax.axis_index("dp")
    greet_all(nu, nd, me, False)
    low, full = jnp.bfloat16, jnp.float32
    seq, width = embed_ref.shape
    part = width // nd

    def vec(k):
        return vecs[k : k + 1, :]

    zhid = vec(15)
    zcols, zmha = gates_ref[0:1, :], gates_ref[1:2, :]
    start_p, context, attn_res, middle_in = small[0], small[1], small[2], small[3]
    grad_middle_in, grad_gain1, grad_shift1 = norm_back(middle_in, vec(5), vec(6), gmid_ref[...])
    grad_ares = grad_middle_in * zmha * zhid
    grad_ares_low = grad_ares.astype(low)
    through = row_sum(grad_middle_in * attn_res)
    scaled = (context * zcols).astype(low)
    g_out[...] = contract_rows(scaled, grad_ares_low).astype(low)
    grad_scaled = product(grad_ares_low, w_out[...], 1, 1)
    pl.semaphore_wait(pltpu.get_barrier_semaphore(), nu * nd - 1)
    for reduce in reduces:
        reduce.start(0)
    lane = lax.broadcasted_iota(jnp.int32, (1, 128), 1)
    of_head = lax.broadcasted_iota(jnp.int32, (1, width), 1) // (width // heads)
    head_terms = row_sum(grad_scaled * context)
    grad_open = jnp.zeros((1, 128), full)
    for h in range(heads):
        one = jnp.sum(jnp.where(of_head == h, head_terms, 0.0), 1, keepdims=True)
        grad_open = jnp.where(lane == h, one, grad_open)
    for k, terms in ((heads, through * zhid), (heads + 1, mid_vecs[13:14, :] * zhid)):
        grad_open = jnp.where(lane == k, jnp.sum(terms, 1, keepdims=True), grad_open)
    masks = mask_row(scal)
    grad_masks = gate_back(masks, scal[1:2, :], grad_open)
    scores = keep_score(masks)
    mha, mlp = scores[:, heads : heads + 1], scores[:, heads + 1 : heads + 2]
    plain_heads = jnp.sum(jnp.where(lane < heads, scores, 0.0), 1, keepdims=True)
    hid_sum = jnp.sum(keep_score(vec(13)), 1, keepdims=True)
    unit_score = mid_stats[1:2, 0:1]
    full_size = 4.0 * width * width + 2.0 * width * ffn_width
    per_head_size = 4.0 * (width // heads)
    head_sum, unit_sum = plain_heads * mha, unit_score * mlp
    kept_share = (per_head_size * hid_sum * head_sum + 2.0 * hid_sum * unit_sum) / full_size
    over = 1.0 - kept_share - TARGET
    first_mult, second_mult = scal[2:3, 0:1], scal[2:3, 1:2]
    slope = -(first_mult + 2.0 * second_mult * over) / full_size
    lag = slope * per_head_size * hid_sum * jnp.where(lane < heads, mha, plain_heads)
    lag = jnp.where(lane == heads + 1, slope * 2.0 * hid_sum * unit_score, lag)
    lag = jnp.where(lane < heads + 2, lag * score_slope(masks), 0.0)
    info[...] = jnp.zeros_like(info)
    info[0:1, :] = jnp.where(
        lane < heads + 2, grad_masks, jnp.where(lane == heads + 2, mid_stats[0:1, :], 0.0)
    )
    info[1:2, :] = lag
    for k, item in (
        (2, slope * (per_head_size * head_sum + 2.0 * unit_sum)),
        (3, slope * 2.0 * hid_sum * mlp),
        (4, kept_share),
        (5, first_mult * over + second_mult * over * over),
    ):
        info[k : k + 1, :] = jnp.broadcast_to(item, (1, 128))
    grad_context = per_head((grad_scaled * zcols).astype(low).astype(full), heads).astype(low)
    scale = (width // heads) ** (-0.5)
    probs = probs_ref[...]
    grad_probs = product(grad_context, values[...], 1, 1)
    grad_scores = (
        probs * (grad_probs - jnp.sum(grad_probs * probs, 1, keepdims=True))
    ).astype(low)
    grad_q = (from_heads(product(grad_scores, keys[...]), heads) * scale).astype(low)
    grad_k = (
        contract_rows(grad_scores, per_head(queries[...].astype(full), heads).astype(low)) * scale
    ).astype(low)
    grad_v = contract_rows(probs.astype(low), grad_context).astype(low)
    for reduce in reduces:
        reduce.finish(0)
        reduce.start(1)
    start_low = start_ref[...]
    g_q[...] = contract_rows(start_p.astype(low), grad_q).astype(low)
    g_k[...] = contract_rows(start_low, grad_k).astype(low)
    g_v[...] = contract_rows(start_low, grad_v).astype(low)
    grad_start_p = grad_middle_in + product(grad_q, w_q[...], 1, 1)
    pick = jnp.where(picked_lines(pos_ref, seq), 1.0, 0.0).astype(low)
    grad_start = (
        sum(contract_rows(pick, item) for item in split_low(grad_start_p))
        + product(grad_k, w_k[...], 1, 1)
        + product(grad_v, w_v[...], 1, 1)
    )
    embed = embed_ref[...]
    center = embed - jnp.mean(embed, 1, keepdims=True)
    unit_norm = center * lax.rsqrt(jnp.mean(center * center, 1, keepdims=True) + EPS_NORM)
    start_norm = unit_norm * vec(0) + vec(1)
    grad_zhid = (
        mid_vecs[13:14, :] * gates_ref[2:3, :]
        + through * zmha
        + row_sum(grad_start * start_norm)
    )
    grad_embed, grad_gain0, grad_shift0 = norm_back(embed, vec(0), vec(1), grad_start * zhid)
    embed_low = grad_embed.astype(low)
    low_embed[...] = embed_low
    match = jnp.where(
        code_ref[...] == lax.broadcasted_iota(jnp.int32, (nu * cap, seq), 0), 1.0, 0.0
    ).astype(low)
    gathered = product(match, embed_low).astype(low)
    for d in range(nd):
        head, tails = pack_rows(gathered, nu, cap, width, d * part, part)
        sent[d, :, :cap] = head
        for tail in tails:
            sent[d, :, cap:] = tail
    lines[...] = jnp.zeros_like(lines)
    items = (
        grad_gain0,
        grad_shift0,
        row_sum(grad_q.astype(full)),
        row_sum(grad_v.astype(full)),
        row_sum(grad_ares),
        grad_gain1,
        grad_shift1,
    )
    for k, item in enumerate(items):
        lines[k : k + 1, :] = item.reshape(1, width)
    lines[7:13, :] = mid_vecs[7:13, :]
    lines[13:14, :] = gate_back(vec(13), noise_ref[...], grad_zhid)
    g_last[:, :seq] = jnp.swapaxes(grad_embed, 0, 1).astype(low)
    g_last[:, seq:] = jnp.swapaxes(lines[...], 0, 1).astype(low)
    for reduce in reduces:
        reduce.finish(1)


def attend_back_step(
    heads,
    nd,
    nu,
    cap,
    ffn_width,
    gmid,
    mid_vecs,
    kept,
    code,
    pos,
    noise,
    gates,
    scal,
    stats,
    maps,
    slices,
    collective,
):
    low, full = jnp.bfloat16, jnp.float32
    seq, width = kept[1].shape
    square = jax.ShapeDtypeStruct((width, width), low)
    grid = grid_of(nu, nd)
    part_grid = (1, 1, *grid[2:])
    shapes = [x.shape[4:] for x in slices]
    part_helds, part_sums = reduce_scratch(part_grid, [DP_ORDER] * 3, shapes)
    scratch = []
    for k in range(3):
        scratch += [part_helds[2 * k], part_helds[2 * k + 1], part_sums[k]]
    return pl.pallas_call(
        functools.partial(attend_back_kernel, heads, nu, nd, cap, ffn_width),
        out_shape=(
            square,
            square,
            square,
            square,
            jax.ShapeDtypeStruct((width, seq + 128), low),
            jax.ShapeDtypeStruct((nd, nu, *packed_shape(cap, width // nd)), low),
            jax.ShapeDtypeStruct((seq, width), low),
            jax.ShapeDtypeStruct((8, 128), full),
            *(jax.ShapeDtypeStruct(shape, full) for shape in shapes),
        ),
        in_specs=[on_chip()] * 23,
        out_specs=(on_chip(),) * 11,
        scratch_shapes=[
            pltpu.VMEM((128, width), full),
            *scratch,
            pltpu.SemaphoreType.DMA((3, 2, max(part_grid))),
            pltpu.SemaphoreType.DMA((3, 2, max(part_grid))),
        ],
        compiler_params=call_params(collective),
    )(
        gmid,
        mid_vecs,
        *kept,
        code,
        pos,
        noise,
        gates,
        scal,
        stats,
        *maps,
        *slices,
    )


def adamw(weight, first, second, grad, rate, count):
    first = BETA_ONE * first + (1.0 - BETA_ONE) * grad
    second = BETA_TWO * second + (1.0 - BETA_TWO) * grad * grad
    first_hat = first / (1.0 - BETA_ONE**count)
    second_hat = second / (1.0 - BETA_TWO**count)
    return weight - rate * (first_hat / (jnp.sqrt(second_hat) + ADAM_EPS) + DECAY * weight)


def on_device(
    token_ids,
    segments,
    positions,
    teacher,
    gate_noise,
    unit_noise,
    multipliers,
    step_count,
    layer_mats,
    mats_first,
    mats_second,
    layer_vecs,
    vecs_first,
    vecs_second,
    ffn_mats,
    ffn_first,
    ffn_second,
    unit_vecs,
    unit_first,
    unit_second,
    word_table,
    table_first,
    table_second,
    word_bias,
    bias_first,
    bias_second,
    mask_logits,
    mask_first,
    mask_second,
):
    low_type = jnp.bfloat16
    full_type = jnp.float32
    exact = lax.Precision.HIGHEST
    units_n = lax.axis_size("unit")
    groups_n = lax.axis_size("dp")
    everyone = ("unit", "dp")
    heads = mask_logits.shape[0] - 2
    share_rows = layer_mats.shape[0]
    width = share_rows * units_n * groups_n
    head_size = width // heads
    seq_len = segments.shape[2]
    nmask = positions.shape[2]
    unit_idx = lax.axis_index("unit")
    n_vecs = layer_vecs.shape[0]
    vec_pad = -n_vecs % 128
    table_turned = word_table.T
    vocab_slice = word_table.shape[0]
    table_part = word_table.shape[1]
    cap = 16 * -(-seq_len // (16 * units_n))

    count = step_count[0].astype(full_type)
    n_masks = heads + 2

    def line_of(values, rest=0.0):
        return jnp.pad(values, (0, 128 - values.shape[0]), constant_values=rest)

    scal = jnp.concatenate(
        [
            line_of(mask_logits)[None],
            line_of(gate_noise[width:], 0.5)[None],
            line_of(multipliers)[None],
            line_of(jnp.stack([1.0 - BETA_ONE**count, 1.0 - BETA_TWO**count]))[None],
            jnp.zeros((4, 128), full_type),
        ],
        0,
    )
    vec_own = jnp.pad(layer_vecs.T, ((0, 0), (0, vec_pad)))

    mats_low = layer_mats.astype(low_type)
    trans_end = 5 * width
    table_low = table_turned.astype(low_type)
    map_parts = [mats_low[:, k * width : (k + 1) * width] for k in range(5)] + [
        jnp.concatenate(
            [
                mats_low[:, trans_end:],
                vec_own.astype(low_type),
            ],
            1,
        )
    ]
    pack_lanes = 128 * -(-max(unit_vecs.shape[1], word_bias.shape[0]) // 128)
    small_pack = jnp.concatenate(
        [
            jnp.pad(unit_vecs, ((0, 0), (0, pack_lanes - unit_vecs.shape[1]))),
            jnp.pad(word_bias, (0, pack_lanes - word_bias.shape[0]))[None],
            jnp.zeros((13, pack_lanes), full_type),
        ],
        0,
    )
    ids = lax.dynamic_index_in_dim(token_ids[0], unit_idx, 0, keepdims=False)
    place = jnp.arange(seq_len, dtype=jnp.int32)
    same_id = ids[:, None] == ids[None, :]
    first_place = jnp.min(jnp.where(same_id, place[None, :], seq_len), 1)
    is_first = first_place == place
    owner = ids // vocab_slice
    slot = jnp.sum(
        (
            is_first[None, :]
            & (owner[None, :] == owner[:, None])
            & (place[None, :] < first_place[:, None])
        ).astype(jnp.int32),
        1,
    )
    slots_used = jnp.max(slot) + 1
    local_id = ids - owner * vocab_slice
    entry = jnp.arange(units_n * cap, dtype=jnp.int32)

    def round_code(k):
        here = slot - k * cap
        return jnp.where((here >= 0) & (here < cap), owner * cap + here, -1)

    def round_match(k):
        return entry[:, None] == round_code(k)[None, :]

    def round_wanted(match):
        return jnp.max(
            jnp.where(match & is_first[None, :], local_id[None, :], -1), 1
        ).reshape(units_n, cap)

    match_0 = round_match(0)
    wanted_0 = jnp.concatenate(
        [
            round_wanted(match_0),
            jnp.broadcast_to(slots_used, (units_n, 128 - cap)),
        ],
        1,
    )[:, None, :]
    fetched, asked, *maps = fetch_rows(
        wanted_0, table_low, map_parts, units_n, groups_n, cap, 1
    )
    *maps, table_early = maps
    w_q, w_k, w_v, w_out, w_trans, pos_vecs = [part.reshape(width, -1) for part in maps]
    asked = asked[:, 0, :]
    rounds = (jnp.max(asked[:, cap:]) + cap - 1) // cap
    code_0 = round_code(0)

    def spread(match, parts):
        return jnp.concatenate(
            [
                contract_rows(match, parts[d].reshape(units_n * cap, table_part))
                for d in range(groups_n)
            ],
            1,
        )

    def round_asked(match):
        wanted_all = lax.all_gather(round_wanted(match), everyone, axis=0)
        return lax.dynamic_index_in_dim(wanted_all, unit_idx, 1, keepdims=False)

    def more_words(k, words):
        match = round_match(k)
        mine = round_asked(match)
        found = jnp.where(
            (mine >= 0)[:, :, None],
            jnp.moveaxis(jnp.take(table_low, jnp.maximum(mine, 0), axis=1), 0, 2),
            0,
        )
        found = lax.all_to_all(found, everyone, 0, 0, tiled=True)
        found = jnp.swapaxes(
            found.reshape(units_n, groups_n, cap, table_part), 0, 1
        )
        return words + spread(match.astype(low_type), found).astype(low_type)

    extra = lax.fori_loop(1, rounds, more_words, jnp.zeros((seq_len, width), low_type))

    noise_hid = gate_noise[:width][None]
    picks = positions.reshape(-1, 1)
    middle, gates, vec_rows, *kept_rows = attend_step(
        heads,
        cap,
        fetched,
        extra,
        code_0[:, None],
        picks,
        segments.reshape(1, -1),
        noise_hid,
        scal,
        pos_vecs,
        (w_q, w_k, w_v, w_out),
    )
    slice_units = unit_vecs.shape[1] * groups_n
    ffn_width = slice_units * units_n
    noise_units = lax.dynamic_slice_in_dim(unit_noise, unit_idx * slice_units, slice_units, 0)
    npos = groups_n * units_n * nmask
    (
        share_head,
        grad_small,
        grad_up,
        grad_down,
        grad_wtrans,
        grad_middle,
        mid_vecs,
        mid_stats,
    ) = mid_step(
        middle,
        ffn_mats,
        small_pack,
        noise_units[None],
        table_low,
        table_early,
        teacher.reshape(-1, vocab_slice),
        w_trans,
        vec_rows,
        units_n,
        groups_n,
        npos,
        2,
    )
    (
        grad_wq,
        grad_wk,
        grad_wv,
        grad_wout,
        grad_last,
        word_grads,
        embed_low,
        info,
        share_up,
        share_down,
        share_small,
    ) = attend_back_step(
        heads,
        groups_n,
        units_n,
        cap,
        ffn_width,
        grad_middle,
        mid_vecs,
        (vec_rows, *kept_rows),
        code_0[None],
        picks,
        noise_hid,
        gates,
        scal,
        mid_stats,
        (w_q, w_k, w_v, w_out),
        (grad_up, grad_down, grad_small),
        3,
    )

    def word_parts(match):
        return jnp.stack(
            [
                jnp.dot(
                    match,
                    embed_low[:, d * table_part : (d + 1) * table_part],
                    preferred_element_type=full_type,
                )
                .astype(low_type)
                .reshape(units_n, cap, table_part)
                for d in range(groups_n)
            ]
        )

    def more_grads(k, total):
        match = round_match(k)
        mine = round_asked(match).reshape(-1)
        back = jnp.swapaxes(word_parts(match.astype(low_type)), 0, 1).reshape(
            units_n * groups_n, cap, table_part
        )
        back = lax.all_to_all(back, everyone, 0, 0, tiled=True).reshape(-1, table_part)
        target = jnp.where(mine >= 0, mine, vocab_slice)
        added = total.astype(full_type).at[:, target].add(
            back.T.astype(full_type), mode="drop"
        )
        return added.astype(low_type)

    more = lax.fori_loop(
        1, rounds, more_grads, jnp.zeros((table_part, vocab_slice), low_type)
    )

    share_table, totals, *shares, share_small = return_rows(
        word_grads,
        asked,
        share_head,
        more,
        vec_own,
        small_pack,
        info,
        (grad_wq, grad_wk, grad_wv, grad_wout, grad_wtrans, grad_last),
        (share_up, share_down, share_small),
        unit_vecs.shape[1],
        cap,
        units_n,
        groups_n,
        9,
    )
    news = update_step(
        heads,
        npos,
        totals,
        info,
        scal,
        (*shares, share_up, share_down, share_small),
        share_table,
        [
            (layer_mats, mats_first, mats_second),
            (layer_vecs, vecs_first, vecs_second),
            (ffn_mats, ffn_first, ffn_second),
            (unit_vecs, unit_first, unit_second),
            (word_bias[None], bias_first[None], bias_second[None]),
            (mask_logits[None], mask_first[None], mask_second[None]),
        ],
        (table_turned, table_first.T, table_second.T),
    )
    mats_new, mats_grad, vecs_new, vecs_grad, ffn_new, ffn_grad, unit_new, unit_grad = news[:8]
    bias_new, bias_grad, mask_new, mask_grad, stat, table_new, table_grad = news[8:]
    return (
        stat[0, 0],
        stat[1, 0],
        stat[2, 0],
        mats_new,
        mats_grad,
        vecs_new,
        vecs_grad,
        ffn_new,
        ffn_grad,
        unit_new,
        unit_grad,
        table_new.T,
        table_grad.T,
        bias_new[0],
        bias_grad[0],
        mask_new[0],
        mask_grad[0],
    )


def solution(mesh):
    return jax.shard_map(
        on_device,
        mesh=mesh,
        in_specs=(
            P("dp", None, None),
            P("dp", "unit", None),
            P("dp", "unit", None),
            P("dp", None, None, "unit"),
            P(),
            P(),
            P(),
            P(),
            P(("unit", "dp"), None),
            P(("unit", "dp"), None),
            P(("unit", "dp"), None),
            P(None, ("unit", "dp")),
            P(None, ("unit", "dp")),
            P(None, ("unit", "dp")),
            P(None, "dp", "unit"),
            P(None, "dp", "unit"),
            P(None, "dp", "unit"),
            P(None, ("unit", "dp")),
            P(None, ("unit", "dp")),
            P(None, ("unit", "dp")),
            P("unit", "dp"),
            P("unit", "dp"),
            P("unit", "dp"),
            P(("unit", "dp")),
            P(("unit", "dp")),
            P(("unit", "dp")),
            P(),
            P(),
            P(),
        ),
        out_specs=(
            P(),
            P(),
            P(),
            P(("unit", "dp"), None),
            P(("unit", "dp"), None),
            P(None, ("unit", "dp")),
            P(None, ("unit", "dp")),
            P(None, "dp", "unit"),
            P(None, "dp", "unit"),
            P(None, ("unit", "dp")),
            P(None, ("unit", "dp")),
            P("unit", "dp"),
            P("unit", "dp"),
            P(("unit", "dp")),
            P(("unit", "dp")),
            P(),
            P(),
        ),
        check_vma=False,
    )
```
